32 devices in a mesh: dp: 4 (over y, x), expert: 8 (over z, core).
Axes of the slice: x: 2, y: 2, z: 4, core: 2. Of those that a mesh axis runs over, the one named last changes fastest.
Arguments:
- query_rows: bfloat16 [8, 512, 2048], P('dp', 'expert'), may hold values from -4 to 4
- key_rows: bfloat16 [8, 512, 256], P('dp', 'expert'), may hold values from -4 to 4
- value_rows: bfloat16 [8, 512, 256], P('dp', 'expert'), may hold values from -6 to 6
- gate_logits: bfloat16 [8, 512, 2048], P('dp', 'expert'), may hold values from -6 to 6
- gated_grad: bfloat16 [8, 512, 2048], P('dp', 'expert'), may hold values from -6 to 6
- moe_input: bfloat16 [4096, 2048], P(('dp', 'expert')), may hold values from -6 to 6
- out_grad: bfloat16 [4096, 2048], P(('dp', 'expert')), may hold values from -24 to 24
- routes: int32 [4096, 10], P(('dp', 'expert')), may hold values from 0 to 511, as said below
- route_weights: bfloat16 [4096, 10], P(('dp', 'expert')), may hold values from 0.019897461 to 0.29882812
- gate_proj: bfloat16 [8, 2048, 256], P('expert', 'dp'), may hold values from -0.125 to 0.125
- up_proj: bfloat16 [8, 2048, 256], P('expert', 'dp'), may hold values from -0.125 to 0.125
- down_proj: bfloat16 [8, 256, 2048], P('expert', None, 'dp'), may hold values from -0.375 to 0.375
Outputs:
- query_grad: bfloat16 [8, 512, 2048], P('dp', 'expert')
- key_grad: bfloat16 [8, 512, 256], P('dp', 'expert')
- value_grad: bfloat16 [8, 512, 256], P('dp', 'expert')
- gate_grad: bfloat16 [8, 512, 2048], P('dp', 'expert')
- input_grad: bfloat16 [4096, 2048], P(('dp', 'expert'))
- route_grad: bfloat16 [4096, 10], P(('dp', 'expert'))
- gate_proj_grad: float32 [8, 2048, 256], P('expert', 'dp')
- up_proj_grad: float32 [8, 2048, 256], P('expert', 'dp')
- down_proj_grad: float32 [8, 256, 2048], P('expert', None, 'dp')
The draws below stay inside these ranges and needn't reach their ends.
Inputs may be any that keep to these rules, and one draw needn't show every extreme that they name: `routes`: each token names 10 different experts. A token names at most one expert below 8; the 128 tokens of one block name each such expert at most 2 times, and in every data group one expert below 8 is named exactly 2 times by every block of the group.
All inputs are finite; a program needn't handle non-finite values.
Results may differ from the reference program's by a relative error of at most 0.035.
Values may be sent and summed in bfloat16 or wider, within the bound.
No kernel may reach another device: no remote copies, remote signals or barrier semaphores. Data moves between devices by JAX's collectives and lax.ppermute only.
A program may use at most 64 MiB of HBM per device.

```python
import jax
import jax.numpy as jnp
from jax import lax

D = 2048
HEADS = 8
HEAD = 256
EXP_HID = 256
EXPERTS = 512
TOP = 10
CAP = 2
TOK_DEV = 128
SHARD = 64
LEN = 512
BATCH = 8
TOKENS = 4096
FLIGHT = 8
N_DP = 4
N_EXPERT = 8


def draw_query_rows(key, part):
    own_key = jax.random.fold_in(key, 11)
    values = jnp.clip(jax.random.normal(own_key, (BATCH, LEN, HEADS, HEAD), jnp.float32), -4.0, 4.0)
    return values.reshape(BATCH, LEN, HEADS * HEAD).astype(jnp.bfloat16)


def draw_key_rows(key, part):
    own_key = jax.random.fold_in(key, 21)
    values = jnp.clip(jax.random.normal(own_key, (BATCH, LEN, HEAD), jnp.float32), -4.0, 4.0)
    return values.astype(jnp.bfloat16)


def route_block(key, block_index):
    flight = N_EXPERT
    group_index = block_index // N_EXPERT
    hot_expert = jax.random.randint(jax.random.fold_in(key, 50000 + group_index), (), 0, flight)
    block_key = jax.random.fold_in(key, block_index)
    counts = jax.random.randint(jax.random.fold_in(block_key, 1), (flight,), 0, CAP + 1)
    counts = jnp.where(jnp.arange(flight) == hot_expert, CAP, counts)
    token_order = jax.random.permutation(jax.random.fold_in(block_key, 2), TOK_DEV)
    slot_index = jnp.arange(flight * CAP)
    expert_of = slot_index // CAP
    slot_used = slot_index % CAP < counts[expert_of]
    live_expert = jnp.full((TOK_DEV,), -1, jnp.int32).at[token_order[:flight * CAP]].set(jnp.where(slot_used, expert_of, -1).astype(jnp.int32))
    column = jax.random.randint(jax.random.fold_in(block_key, 3), (TOK_DEV,), 0, TOP)
    offset_base = jax.random.randint(jax.random.fold_in(block_key, 4), (TOK_DEV,), 0, EXPERTS - flight)
    others = flight + (offset_base[:, None] + jnp.arange(TOP)[None, :]) % (EXPERTS - flight)
    placed = (jnp.arange(TOP)[None, :] == column[:, None]) & (live_expert[:, None] >= 0)
    return jnp.where(placed, live_expert[:, None], others).astype(jnp.int32)


def draw_routes(key, part):
    block_ids = jnp.arange(N_DP * N_EXPERT)
    routed = jax.vmap(partial_block(key))(block_ids)
    return routed.reshape(TOKENS, TOP)


def partial_block(key):

    def make_block(block_index):
        return route_block(key, block_index)
    return make_block


def block_levels(key, dims, split, smallest, largest):
    factor_of, own = 1.0, jax.random.fold_in(key, 6)
    for axis_at, blocks in split:
        draws = jnp.exp(jax.random.uniform(jax.random.fold_in(own, axis_at), (blocks,), jnp.float32, smallest / len(split), largest / len(split)))
        factor_of = factor_of * jnp.repeat(draws, dims[axis_at] // blocks).reshape([-1 if axis == axis_at else 1 for axis in range(len(dims))])
    return factor_of


def noise(key, extent, spread, bound, pieces=(), held_as=jnp.bfloat16):
    level = block_levels(key, extent, pieces, -0.22, 0.18) if pieces else 1.0
    array = jax.random.normal(key, extent, jnp.float32) * spread * level
    return jnp.minimum(jnp.maximum(array, -bound), bound).astype(held_as)


def setup_inputs(seed: int = 0) -> dict:
    key_of = jax.random.split(jax.random.key(seed), 13)
    return {
        "query_rows": draw_query_rows(jax.random.fold_in(key_of[12], 71), 0),
        "key_rows": draw_key_rows(jax.random.fold_in(key_of[12], 71), 0),
        "value_rows": noise(key_of[2], (BATCH, LEN, HEAD), 1.0, 6.0, ((0, 4), (1, 8))),
        "gate_logits": noise(key_of[3], (BATCH, LEN, HEADS * HEAD), 1.0, 6.0, ((0, 4), (1, 8))),
        "gated_grad": noise(key_of[4], (BATCH, LEN, HEADS * HEAD), 1.0, 6.0, ((0, 4), (1, 8))),
        "moe_input": noise(key_of[5], (TOKENS, D), 1.0, 6.0, ((0, 32),)),
        "out_grad": noise(key_of[6], (TOKENS, D), 4.0, 24.0, ((0, 32),)),
        "routes": draw_routes(jax.random.fold_in(key_of[12], 71), 0),
        "route_weights": jnp.clip(0.019897461 + 0.27893066 * jax.random.uniform(key_of[8], (TOKENS, TOP), jnp.float32) ** block_levels(key_of[8], (TOKENS, TOP), ((0, 32),), -0.2, 0.2), 0.019897461, 0.29882812).astype(jnp.bfloat16),
        "gate_proj": noise(key_of[9], (FLIGHT, D, EXP_HID), D ** -0.5, 0.125, ((0, 8), (1, 4))),
        "up_proj": noise(key_of[10], (FLIGHT, D, EXP_HID), D ** -0.5, 0.125, ((0, 8), (1, 4))),
        "down_proj": noise(key_of[11], (FLIGHT, EXP_HID, D), EXP_HID ** -0.5, 0.375, ((0, 8), (2, 4))),
    }


def attend_sequence(operands):
    query_seq, key_seq, value_seq, logit_seq, gated_seq = operands
    score_scale = HEAD ** -0.5
    queries = query_seq.reshape(LEN, HEADS, HEAD).astype(jnp.float32)
    key_wide = key_seq.astype(jnp.float32)
    value_wide = value_seq.astype(jnp.float32)
    scores = jnp.einsum("phd,rd->hpr", queries, key_wide) * score_scale
    causal = (jnp.arange(LEN)[:, None] >= jnp.arange(LEN)[None, :])[None]
    masked = jnp.where(causal, scores, -jnp.inf)
    row_max = jnp.max(masked, axis=2, keepdims=True)
    log_total = row_max + jnp.log(jnp.sum(jnp.exp(masked - row_max), axis=2, keepdims=True))
    exact_probs = jnp.where(causal, jnp.exp(scores - log_total), 0.0)
    probs_low = exact_probs.astype(jnp.bfloat16)
    context = jnp.einsum("hpr,rd->phd", probs_low.astype(jnp.float32), value_wide)
    sigmoid_gate = jax.nn.sigmoid(logit_seq.astype(jnp.float32)).reshape(LEN, HEADS, HEAD)
    upstream = gated_seq.astype(jnp.float32).reshape(LEN, HEADS, HEAD)
    context_grad = (upstream * sigmoid_gate).astype(jnp.bfloat16)
    gate_grad = (upstream * context * sigmoid_gate * (1.0 - sigmoid_gate)).astype(jnp.bfloat16)
    grad_wide = context_grad.astype(jnp.float32)
    grad_dot = jnp.transpose(jnp.sum(grad_wide * context, axis=2))
    prob_grad = jnp.einsum("phd,rd->hpr", grad_wide, value_wide)
    score_grad = (exact_probs * (prob_grad - grad_dot[:, :, None]) * score_scale).astype(jnp.bfloat16)
    score_wide = score_grad.astype(jnp.float32)
    query_grad = jnp.einsum("hpr,rd->phd", score_wide, key_wide).astype(jnp.bfloat16)
    blocked_scores = score_wide.reshape(HEADS, N_EXPERT, SHARD, LEN)
    blocked_probs = probs_low.astype(jnp.float32).reshape(HEADS, N_EXPERT, SHARD, LEN)
    key_parts = jnp.einsum("hnpr,nphd->nrd", blocked_scores, queries.reshape(N_EXPERT, SHARD, HEADS, HEAD)).astype(jnp.bfloat16)
    value_parts = jnp.einsum("hnpr,nphd->nrd", blocked_probs, grad_wide.reshape(N_EXPERT, SHARD, HEADS, HEAD)).astype(jnp.bfloat16)
    key_grad = jnp.sum(key_parts.astype(jnp.float32), axis=0).astype(jnp.bfloat16)
    value_grad = jnp.sum(value_parts.astype(jnp.float32), axis=0).astype(jnp.bfloat16)
    return (query_grad.reshape(LEN, HEADS * HEAD), key_grad, value_grad, gate_grad.reshape(LEN, HEADS * HEAD))


def group_sum(left, right, groups):
    left_wide = left.reshape(groups, -1, left.shape[-1]).astype(jnp.float32)
    right_wide = right.reshape(groups, -1, right.shape[-1]).astype(jnp.float32)
    partial_sums = jnp.einsum("grc,gre->gce", left_wide, right_wide).astype(jnp.bfloat16)
    return jnp.sum(partial_sums.astype(jnp.float32), axis=0)


def expert_pass(operands):
    rows_in, grads_in, weights_in, gate_mat, up_mat, down_mat = operands
    groups = rows_in.shape[0]
    flat_rows = rows_in.reshape(-1, D)
    flat_grads = grads_in.reshape(-1, D)
    gate_pre = jnp.dot(flat_rows, gate_mat, preferred_element_type=jnp.float32)
    up_pre = jnp.dot(flat_rows, up_mat, preferred_element_type=jnp.float32)
    sigmoid_pre = jax.nn.sigmoid(gate_pre)
    silu_value = gate_pre * sigmoid_pre
    hidden = (silu_value * up_pre).astype(jnp.bfloat16)
    expert_out = jnp.dot(hidden, down_mat, preferred_element_type=jnp.float32)
    weight_back = jnp.sum(expert_out * flat_grads.astype(jnp.float32), axis=1).astype(jnp.bfloat16)
    scaled_grad = (weights_in.reshape(-1)[:, None].astype(jnp.float32) * flat_grads.astype(jnp.float32)).astype(jnp.bfloat16)
    hidden_grad = jnp.dot(scaled_grad, down_mat.T, preferred_element_type=jnp.float32)
    slope = sigmoid_pre * (1.0 + gate_pre * (1.0 - sigmoid_pre))
    gate_rows = (hidden_grad * up_pre * slope).astype(jnp.bfloat16)
    up_rows = (hidden_grad * silu_value).astype(jnp.bfloat16)
    input_rows = (jnp.dot(gate_rows, gate_mat.T, preferred_element_type=jnp.float32)
                  + jnp.dot(up_rows, up_mat.T, preferred_element_type=jnp.float32)).astype(jnp.bfloat16)
    gate_total = group_sum(flat_rows, gate_rows, groups)
    up_total = group_sum(flat_rows, up_rows, groups)
    down_total = group_sum(hidden, scaled_grad, groups)
    return input_rows, weight_back, gate_total, up_total, down_total


def reference(query_rows, key_rows, value_rows, gate_logits, gated_grad, moe_input, out_grad, routes, route_weights, gate_proj, up_proj, down_proj):
    query_grad, key_grad, value_grad, gate_grad = lax.map(attend_sequence, (query_rows, key_rows, value_rows, gate_logits, gated_grad))
    blocks = N_DP * N_EXPERT
    slot_total = N_EXPERT * CAP
    route_ids = routes.reshape(blocks, TOK_DEV, TOP)
    live_slot = route_ids < N_EXPERT
    has_live = jnp.any(live_slot, axis=2)
    live_expert = jnp.sum(jnp.where(live_slot, route_ids, 0), axis=2).astype(jnp.int32)
    member = (live_expert[:, :, None] == jnp.arange(N_EXPERT, dtype=jnp.int32)[None, None, :]) & has_live[:, :, None]
    member_count = member.astype(jnp.int32)
    before = jnp.cumsum(member_count, axis=1) - member_count
    slot_rank = jnp.sum(jnp.where(member, before, 0), axis=2).astype(jnp.int32)
    slot_of = jnp.where(has_live, live_expert * CAP + slot_rank, slot_total).astype(jnp.int32)
    token_ids = jnp.broadcast_to(jnp.arange(TOK_DEV, dtype=jnp.int32)[None, :], (blocks, TOK_DEV))
    block_ids = jnp.broadcast_to(jnp.arange(blocks, dtype=jnp.int32)[:, None], (blocks, TOK_DEV))
    table = jnp.full((blocks, slot_total), TOK_DEV, jnp.int32).at[block_ids, slot_of].set(token_ids, mode="drop")
    token_weight = jnp.sum(jnp.where(live_slot, route_weights.reshape(blocks, TOK_DEV, TOP).astype(jnp.float32), 0.0), axis=2).astype(jnp.bfloat16)

    def pick_rows(values):
        padded = jnp.concatenate([values, jnp.zeros((blocks, 1, values.shape[2]), values.dtype)], axis=1)
        return jnp.take_along_axis(padded, table[:, :, None], axis=1)

    def by_expert(values):
        shaped = values.reshape((N_DP, N_EXPERT, N_EXPERT, CAP) + values.shape[2:])
        moved = jnp.moveaxis(shaped, 2, 0)
        return moved.reshape((N_EXPERT, N_DP, N_EXPERT * CAP) + values.shape[2:])

    def back_to_blocks(values):
        shaped = values.reshape((N_EXPERT, N_DP, N_EXPERT, CAP) + values.shape[2:])
        moved = jnp.moveaxis(shaped, 0, 2)
        return moved.reshape((blocks, slot_total) + values.shape[2:])

    rows_all = pick_rows(moe_input.reshape(blocks, TOK_DEV, D))
    grads_all = pick_rows(out_grad.reshape(blocks, TOK_DEV, D))
    weights_all = pick_rows(token_weight[:, :, None])[:, :, 0]
    input_rows, weight_back, gate_total, up_total, down_total = lax.map(
        expert_pass, (by_expert(rows_all), by_expert(grads_all), by_expert(weights_all), gate_proj, up_proj, down_proj))
    input_blocks = back_to_blocks(input_rows.reshape(N_EXPERT, N_DP * N_EXPERT * CAP, D))
    weight_blocks = back_to_blocks(weight_back.reshape(N_EXPERT, N_DP * N_EXPERT * CAP))
    input_padded = jnp.concatenate([input_blocks, jnp.zeros((blocks, 1, D), jnp.bfloat16)], axis=1)
    input_grad = jnp.take_along_axis(input_padded, slot_of[:, :, None], axis=1).reshape(TOKENS, D)
    weight_padded = jnp.concatenate([weight_blocks, jnp.zeros((blocks, 1), jnp.bfloat16)], axis=1)
    token_back = jnp.take_along_axis(weight_padded, slot_of, axis=1)
    route_grad = jnp.where(live_slot, token_back[:, :, None], jnp.zeros((), jnp.bfloat16)).astype(jnp.bfloat16).reshape(TOKENS, TOP)
    return (query_grad, key_grad, value_grad, gate_grad, input_grad, route_grad, gate_total, up_total, down_total)
```

```python
import functools

import jax
import jax.numpy as jnp
from jax import lax
from jax.experimental import pallas as pl
from jax.experimental.pallas import tpu as pltpu
from jax.sharding import PartitionSpec as P

HEADS = 8
HEAD = 256
CAP = 2
LANES = 128
BF16 = jnp.bfloat16
F32 = jnp.float32
MIB = 1 << 20


def dot(a, b, ca=1, cb=0):
    return lax.dot_general(a, b, (((ca,), (cb,)), ((), ())), preferred_element_type=F32)


def iota(shape, dim):
    return lax.broadcasted_iota(jnp.int32, shape, dim)


def params(mib):
    return pltpu.CompilerParams(vmem_limit_bytes=mib * MIB)


def cost(flops, bytes_accessed):
    return pl.CostEstimate(flops=int(flops), bytes_accessed=int(bytes_accessed), transcendentals=0)


def attention_kernel(chips, *refs):
    q_ref, logit_ref, grad_ref = refs[:3]
    kv_refs = refs[3 : 3 + 2 * chips]
    query_grad_ref, gate_grad_ref, other_ref = refs[3 + 2 * chips : 6 + 2 * chips]
    mine_refs = refs[6 + 2 * chips :]
    length = q_ref.shape[1]
    keys_total = 2 * chips * length
    scale = HEAD ** (-0.5)
    position = lax.axis_index("expert")
    chip, core = position // 2, position % 2

    def stacked(ref):
        return jnp.concatenate(
            [ref[0, :, h * HEAD : (h + 1) * HEAD] for h in range(HEADS)], axis=0
        )

    queries = stacked(q_ref)
    keys = jnp.concatenate([r[0, :, :HEAD] for r in kv_refs], axis=0)
    values = jnp.concatenate([r[0, :, HEAD:] for r in kv_refs], axis=0)
    rows = HEADS * length
    shape = (rows, keys_total)
    row_pos = iota(shape, 0) % length
    col = iota(shape, 1)
    col_pos = col % length
    half = (col // length) % 2
    back = col // (2 * length)
    core_full = jnp.full(shape, core, jnp.int32)
    allowed = ((back > 0) & (back <= chip)) | (
        (back == 0) & (((half == 0) & (col_pos <= row_pos)) | ((half == 1) & (core_full == 1)))
    )
    scores = jnp.where(allowed, dot(queries, keys, 1, 1) * scale, -jnp.inf)
    row_max = jnp.max(scores, axis=1, keepdims=True)
    unnormed = jnp.exp(scores - row_max)
    probs = unnormed / jnp.sum(unnormed, axis=1, keepdims=True)
    probs_low = probs.astype(BF16)
    context = dot(probs_low, values)
    gate = jax.nn.sigmoid(stacked(logit_ref).astype(F32))
    upstream = stacked(grad_ref).astype(F32)
    context_grad = (upstream * gate).astype(BF16)
    gate_grad = (upstream * context * gate * (1.0 - gate)).astype(BF16)
    grad_dot = jnp.sum(context_grad.astype(F32) * context, axis=1, keepdims=True)
    prob_grad = dot(context_grad, values, 1, 1)
    score_grad = (probs * (prob_grad - grad_dot) * scale).astype(BF16)
    key_part = dot(score_grad, queries, 0, 0).astype(BF16)
    value_part = dot(probs_low, context_grad, 0, 0).astype(BF16)
    query_grad = dot(score_grad, keys).astype(BF16)
    for h in range(HEADS):
        rows_h = slice(h * length, (h + 1) * length)
        query_grad_ref[0, :, h * HEAD : (h + 1) * HEAD] = query_grad[rows_h]
        gate_grad_ref[0, :, h * HEAD : (h + 1) * HEAD] = gate_grad[rows_h]
    for d in range(chips):
        start = 2 * d * length
        mine_refs[d][0, :, :HEAD] = key_part[start : start + length]
        mine_refs[d][0, :, HEAD:] = value_part[start : start + length]
        other_ref[d, 0, :, :HEAD] = key_part[start + length : start + 2 * length]
        other_ref[d, 0, :, HEAD:] = value_part[start + length : start + 2 * length]


def attention(query_rows, gate_logits, gated_grad, pieces):
    seqs, length, width = query_rows.shape
    chips = len(pieces) // 2
    wide = pl.BlockSpec((1, length, width), lambda s: (s, 0, 0))
    narrow = pl.BlockSpec((1, length, 2 * HEAD), lambda s: (s, 0, 0))
    piece = jax.ShapeDtypeStruct((seqs, length, 2 * HEAD), BF16)
    full = jax.ShapeDtypeStruct((seqs, length, width), BF16)
    flops = 12 * seqs * HEADS * length * 2 * chips * length * HEAD
    out = pl.pallas_call(
        functools.partial(attention_kernel, chips),
        grid=(seqs,),
        in_specs=[wide] * 3 + [narrow] * (2 * chips),
        out_specs=[
            wide,
            wide,
            pl.BlockSpec((chips, 1, length, 2 * HEAD), lambda s: (0, s, 0, 0)),
        ]
        + [narrow] * chips,
        out_shape=[full, full, jax.ShapeDtypeStruct((chips,) + piece.shape, BF16)] + [piece] * chips,
        compiler_params=params(56),
        cost_estimate=cost(flops * 4, 8 * MIB),
        name="attention",
    )(query_rows, gate_logits, gated_grad, *pieces)
    return out[0], out[1], out[2], out[3:]


def merge_kernel(chips, *refs):
    mine, arrived, outs = refs[:chips], refs[chips], refs[chips + 1 :]
    for d in range(chips):
        outs[d][...] = (mine[d][...].astype(F32) + arrived[d].astype(F32)).astype(BF16)


def merge(mine, arrived):
    chips = len(mine)
    return pl.pallas_call(
        functools.partial(merge_kernel, chips),
        out_shape=[jax.ShapeDtypeStruct(mine[0].shape, BF16)] * chips,
        compiler_params=params(32),
        cost_estimate=cost(MIB, 2 * MIB),
        name="merge",
    )(*mine, arrived)


def close_kernel(*refs):
    parts, (key_ref, value_ref) = refs[:-2], refs[-2:]
    total = parts[0][...].astype(F32)
    for part in parts[1:]:
        total = total + part[...].astype(F32)
    key_ref[...] = total[:, :, :HEAD].astype(BF16)
    value_ref[...] = total[:, :, HEAD:].astype(BF16)


def close(parts):
    seqs, length, _ = parts[0].shape
    half = jax.ShapeDtypeStruct((seqs, length, HEAD), BF16)
    return pl.pallas_call(
        close_kernel,
        out_shape=[half, half],
        compiler_params=params(32),
        cost_estimate=cost(MIB, MIB),
        name="close",
    )(*parts)


def slots(routes_ref, weights_ref, experts):
    routes = routes_ref[...]
    tokens = routes.shape[0]
    live = routes < experts
    expert = jnp.sum(jnp.where(live, routes, 0), axis=1, keepdims=True)
    has_live = jnp.sum(live.astype(jnp.int32), axis=1, keepdims=True) > 0
    weight = jnp.sum(
        jnp.where(live, weights_ref[...].astype(F32), 0.0), axis=1, keepdims=True
    )
    wide = max(experts, LANES)
    member = (iota((tokens, wide), 1) == expert) & has_live
    earlier = (iota((tokens, tokens), 1) < iota((tokens, tokens), 0)).astype(BF16)
    before = dot(earlier, member.astype(BF16))
    rank = jnp.sum(jnp.where(member, before, 0.0), axis=1, keepdims=True).astype(jnp.int32)
    return jnp.where(has_live, expert * CAP + rank, -1), weight, live


def dispatch_kernel(experts, groups, rows, input_ref, grad_ref, routes_ref, weights_ref, out_ref):
    slot, weight, _ = slots(routes_ref, weights_ref, experts)
    tokens, width = input_ref.shape
    share = width // groups
    pieces = share // LANES
    total = experts * rows
    slot_row = jnp.transpose(jnp.broadcast_to(slot.astype(F32), (tokens, LANES)))[:1].astype(
        jnp.int32
    )
    sent = (input_ref[...], (weight * grad_ref[...].astype(F32)).astype(BF16))
    shape = (total, tokens)
    row = iota(shape, 0)
    inner = row % rows
    hit = slot_row == (row // rows) * CAP + (inner // pieces) % CAP
    acc = None
    for a in range(2):
        for l in range(pieces):
            pick = hit & (inner // (CAP * pieces) == a) & (inner % pieces == l)
            source = jnp.concatenate(
                [
                    sent[a][:, g * share + l * LANES : g * share + (l + 1) * LANES]
                    for g in range(groups)
                ],
                axis=1,
            )
            term = dot(pick.astype(BF16), source)
            acc = term if acc is None else acc + term
    acc = acc.astype(BF16)
    for g in range(groups):
        out_ref[g * total : (g + 1) * total, :] = acc[:, g * LANES : (g + 1) * LANES]


def enter_kernel(
    sources, rows, recv_ref, gate_ref, up_ref, down_ref, input_ref, grad_ref, own_ref, send_ref
):
    pieces = input_ref.shape[1] // LANES
    block = min(sources, 32)
    shape = (block * CAP, block * rows)
    out_row, in_row = iota(shape, 0), iota(shape, 1)
    base = (out_row // CAP) * rows + (out_row % CAP) * pieces
    picks = [
        [(in_row == base + a * CAP * pieces + l).astype(BF16) for l in range(pieces)]
        for a in range(2)
    ]
    for b in range(sources // block):
        arrived = recv_ref[b * block * rows : (b + 1) * block * rows, :]
        here = slice(b * block * CAP, (b + 1) * block * CAP)
        inputs, grads = (
            jnp.concatenate([dot(pick, arrived) for pick in picks[a]], axis=1).astype(BF16)
            for a in range(2)
        )
        input_ref[here, :] = inputs
        grad_ref[here, :] = grads
        partial = jnp.concatenate(
            [dot(inputs, gate_ref[0]), dot(inputs, up_ref[0]), dot(grads, down_ref[0], 1, 1)],
            axis=1,
        )
        own_ref[here, :] = partial
        send_ref[here, :] = partial.astype(BF16)


def middle_kernel(sources, rows, peers, *refs):
    own_ref = refs[0]
    parts = refs[1 : 1 + peers]
    gate_ref, up_ref, back_ref, hidden_ref, gate_rows_ref, up_rows_ref = refs[1 + peers :]
    share = gate_ref.shape[1]
    pieces = share // LANES
    hid = gate_ref.shape[2]
    block = min(sources, 32)
    shape = (block * rows, block * CAP)
    out_row, in_row = iota(shape, 0), iota(shape, 1)
    same = out_row // rows == in_row // CAP
    inner, which = out_row % rows, in_row % CAP
    picks = [(same & (inner == which * pieces + l)).astype(BF16) for l in range(pieces)]
    pick_dot = (same & (inner == CAP * pieces + which)).astype(BF16)
    for b in range(sources // block):
        here = slice(b * block * CAP, (b + 1) * block * CAP)
        total = own_ref[here, :]
        for part in parts:
            total = total + part[here, :].astype(F32)
        gate_pre, up_pre, hidden_grad = total[:, :hid], total[:, hid : 2 * hid], total[:, 2 * hid :]
        sig = jax.nn.sigmoid(gate_pre)
        silu = gate_pre * sig
        hidden = (silu * up_pre).astype(BF16)
        slope = sig * (1.0 + gate_pre * (1.0 - sig))
        gate_rows = (hidden_grad * up_pre * slope).astype(BF16)
        up_rows = (hidden_grad * silu).astype(BF16)
        hidden_ref[here, :] = hidden
        gate_rows_ref[here, :] = gate_rows
        up_rows_ref[here, :] = up_rows
        routed = jnp.sum(hidden.astype(F32) * hidden_grad, axis=1, keepdims=True)
        high = routed.astype(BF16)
        low = (routed - high.astype(F32)).astype(BF16)
        lane = iota((block * CAP, LANES), 1)
        routed_wide = jnp.where(lane < LANES // 2, high.astype(F32), low.astype(F32)).astype(BF16)
        input_rows = (
            dot(gate_rows, gate_ref[0], 1, 1) + dot(up_rows, up_ref[0], 1, 1)
        ).astype(BF16)
        back = dot(pick_dot, routed_wide)
        for l in range(pieces):
            back = back + dot(picks[l], input_rows[:, l * LANES : (l + 1) * LANES])
        back_ref[b * block * rows : (b + 1) * block * rows, :] = back.astype(BF16)


def weight_kernel(
    input_ref, grad_ref, hidden_ref, gate_rows_ref, up_rows_ref, gate_out, up_out, down_out
):
    gate_out[0] = dot(input_ref[...], gate_rows_ref[...], 0, 0)
    up_out[0] = dot(input_ref[...], up_rows_ref[...], 0, 0)
    down_out[0] = dot(hidden_ref[...], grad_ref[...], 0, 0)


def combine_kernel(
    experts, groups, rows, back_ref, routes_ref, weights_ref, input_grad_ref, route_grad_ref
):
    slot, weight, live = slots(routes_ref, weights_ref, experts)
    tokens, width = input_grad_ref.shape
    share = width // groups
    pieces = share // LANES
    total = experts * rows
    shape = (tokens, total)
    col = iota(shape, 1)
    inner = col % rows
    expert = col // rows
    hit = (slot == expert * CAP + inner // pieces) & (inner < CAP * pieces)
    wide = jnp.concatenate([back_ref[g * total : (g + 1) * total, :] for g in range(groups)], axis=1)
    for l in range(pieces):
        grad = dot((hit & (inner % pieces == l)).astype(BF16), wide).astype(BF16)
        for g in range(groups):
            input_grad_ref[:, g * share + l * LANES : g * share + (l + 1) * LANES] = grad[
                :, g * LANES : (g + 1) * LANES
            ]
    hit_dot = slot == expert * CAP + inner - CAP * pieces
    hit_dot = hit_dot & (inner >= CAP * pieces) & (inner < CAP * (pieces + 1))
    routed = dot(hit_dot.astype(BF16), back_ref[:total, :])
    routed = routed[:, :1] + routed[:, LANES // 2 : LANES // 2 + 1]
    routed = routed / jnp.where(weight > 0.0, weight, 1.0)
    route_grad_ref[...] = jnp.where(live, routed, 0.0).astype(BF16)


def shards(
    query_rows,
    key_rows,
    value_rows,
    gate_logits,
    gated_grad,
    moe_input,
    out_grad,
    routes,
    route_weights,
    gate_proj,
    up_proj,
    down_proj,
):
    devices = lax.axis_size("expert")
    groups = lax.axis_size("dp")
    sources = devices * groups
    chips = devices // 2
    tokens, width = moe_input.shape
    share = width // groups
    pieces = share // LANES
    hid = gate_proj.shape[2]
    rows = -(-2 * CAP * pieces // 16) * 16
    axes = ("dp", "expert")
    swap = [(i, i ^ 1) for i in range(devices)]

    packed = jnp.concatenate([key_rows, value_rows], axis=2)
    mine = [packed]
    for d in range(1, chips):
        up = [(i, i + 2 * d) for i in range(devices - 2 * d)]
        mine.append(lax.ppermute(packed, "expert", up))
    pieces_kv = []
    for block in mine:
        pieces_kv += [block, lax.ppermute(block, "expert", swap)]

    send = pl.pallas_call(
        functools.partial(dispatch_kernel, devices, groups, rows),
        out_shape=jax.ShapeDtypeStruct((sources * rows, LANES), BF16),
        compiler_params=params(48),
        cost_estimate=cost(2e9, 2 * MIB),
        name="dispatch",
    )(moe_input, out_grad, routes, route_weights)
    recv = lax.all_to_all(
        send.reshape(sources, rows, LANES), axes, split_axis=0, concat_axis=0, tiled=True
    ).reshape(sources * rows, LANES)

    slot_rows = jax.ShapeDtypeStruct((sources * CAP, share), BF16)
    hid_rows = jax.ShapeDtypeStruct((sources * CAP, hid), BF16)
    inputs, grads, own, sent = pl.pallas_call(
        functools.partial(enter_kernel, sources, rows),
        out_shape=[
            slot_rows,
            slot_rows,
            jax.ShapeDtypeStruct((sources * CAP, 3 * hid), F32),
            jax.ShapeDtypeStruct((sources * CAP, 3 * hid), BF16),
        ],
        compiler_params=params(48),
        cost_estimate=cost(2e9, 2 * MIB),
        name="enter",
    )(recv, gate_proj, up_proj, down_proj)
    parts = []
    for k in range(1, groups):
        parts.append(lax.ppermute(sent, "dp", [(g, g ^ k) for g in range(groups)]))
    back, hidden, gate_rows, up_rows = pl.pallas_call(
        functools.partial(middle_kernel, sources, rows, groups - 1),
        out_shape=[jax.ShapeDtypeStruct((sources * rows, LANES), BF16)] + [hid_rows] * 3,
        compiler_params=params(48),
        cost_estimate=cost(2e9, 2 * MIB),
        name="middle",
    )(own, *parts, gate_proj, up_proj)
    returned = lax.all_to_all(
        back.reshape(sources, rows, LANES), axes, split_axis=0, concat_axis=0, tiled=True
    ).reshape(sources * rows, LANES)
    gate_proj_grad, up_proj_grad, down_proj_grad = pl.pallas_call(
        weight_kernel,
        out_shape=[
            jax.ShapeDtypeStruct(gate_proj.shape, F32),
            jax.ShapeDtypeStruct(up_proj.shape, F32),
            jax.ShapeDtypeStruct(down_proj.shape, F32),
        ],
        compiler_params=params(48),
        cost_estimate=cost(2e9, 2 * MIB),
        name="weight_grads",
    )(inputs, grads, hidden, gate_rows, up_rows)
    input_grad, route_grad = pl.pallas_call(
        functools.partial(combine_kernel, devices, groups, rows),
        out_shape=[
            jax.ShapeDtypeStruct(moe_input.shape, BF16),
            jax.ShapeDtypeStruct(routes.shape, BF16),
        ],
        compiler_params=params(48),
        cost_estimate=cost(2e9, 2 * MIB),
        name="combine",
    )(returned, routes, route_weights)

    query_grad, gate_grad, other_parts, mine_parts = attention(
        query_rows, gate_logits, gated_grad, pieces_kv
    )
    arrived = lax.ppermute(other_parts, "expert", swap)
    merged = merge(mine_parts, arrived)
    terms = [merged[0]]
    for d in range(1, chips):
        down = [(i, i - 2 * d) for i in range(2 * d, devices)]
        terms.append(lax.ppermute(merged[d], "expert", down))
    key_grad, value_grad = close(terms)
    return (
        query_grad,
        key_grad,
        value_grad,
        gate_grad,
        input_grad,
        route_grad,
        gate_proj_grad,
        up_proj_grad,
        down_proj_grad,
    )


def solution(mesh):
    rows3 = P("dp", "expert", None)
    tokens2 = P(("dp", "expert"), None)
    weights = P("expert", "dp", None)
    weights_down = P("expert", None, "dp")
    return jax.shard_map(
        shards,
        mesh=mesh,
        in_specs=(rows3,) * 5 + (tokens2,) * 4 + (weights, weights, weights_down),
        out_specs=(rows3,) * 4 + (tokens2,) * 2 + (weights, weights, weights_down),
        check_vma=False,
    )
```

```python
import functools

import jax
import jax.numpy as jnp
from jax import lax
from jax.experimental import pallas as pl
from jax.experimental.pallas import tpu as pltpu
from jax.sharding import PartitionSpec as P

HEADS = 8
HEAD = 256
CAP = 2
LANES = 128
BF16 = jnp.bfloat16
F32 = jnp.float32
MIB = 1 << 20
ATTENTION_MIB = 32


def dot(a, b, ca=1, cb=0):
    return lax.dot_general(a, b, (((ca,), (cb,)), ((), ())), preferred_element_type=F32)


def iota(shape, dim):
    return lax.broadcasted_iota(jnp.int32, shape, dim)


def params(mib):
    return pltpu.CompilerParams(vmem_limit_bytes=mib * MIB)


def cost(flops, bytes_accessed):
    return pl.CostEstimate(flops=int(flops), bytes_accessed=int(bytes_accessed), transcendentals=0)


def pack_kernel(key_ref, value_ref, out_ref):
    for d in range(out_ref.shape[0]):
        out_ref[d, :, :, :HEAD] = key_ref[...]
        out_ref[d, :, :, HEAD:] = value_ref[...]


def attention_kernel(
    q_ref,
    logit_ref,
    grad_ref,
    mine_ref,
    other_ref,
    query_grad_ref,
    gate_grad_ref,
    mine_part_ref,
    other_part_ref,
):
    length = q_ref.shape[1]
    chips = mine_ref.shape[0]
    side = chips * length
    scale = HEAD ** (-0.5)
    position = lax.axis_index("expert")
    chip, core = position // 2, position % 2

    def stacked(ref):
        return jnp.concatenate(
            [ref[0, :, h * HEAD : (h + 1) * HEAD] for h in range(HEADS)], axis=0
        )

    both = [ref[j, 0] for ref in (mine_ref, other_ref) for j in range(chips)]
    both = jnp.concatenate(both, axis=0)
    keys, values = both[:, :HEAD], both[:, HEAD:]
    queries = stacked(q_ref)
    shape = (HEADS * length, 2 * side)
    row_pos = iota(shape, 0) % length
    col = iota(shape, 1)
    col_pos = col % length
    col_chip = (col // length) % chips
    limit = jnp.where(col < side, row_pos, core * length - 1)
    allowed = (col_chip < chip) | ((col_chip == chip) & (col_pos <= limit))
    scores = jnp.where(allowed, dot(queries, keys, 1, 1) * scale, -jnp.inf)
    row_max = jnp.max(scores, axis=1, keepdims=True)
    unnormed = jnp.exp(scores - row_max)
    probs = unnormed * (1.0 / jnp.sum(unnormed, axis=1, keepdims=True))
    probs_low = probs.astype(BF16)
    context = dot(probs_low, values)
    gate = jax.nn.sigmoid(stacked(logit_ref).astype(F32))
    upstream = stacked(grad_ref).astype(F32)
    context_grad = (upstream * gate).astype(BF16)
    gate_grad = (upstream * context * gate * (1.0 - gate)).astype(BF16)
    grad_dot = jnp.sum(context_grad.astype(F32) * context, axis=1, keepdims=True)
    prob_grad = dot(context_grad, values, 1, 1)
    score_grad = (probs * (prob_grad - grad_dot) * scale).astype(BF16)
    key_part = dot(score_grad, queries, 0, 0).astype(BF16)
    value_part = dot(probs_low, context_grad, 0, 0).astype(BF16)
    for half, ref in enumerate((mine_part_ref, other_part_ref)):
        for j in range(chips):
            start = half * side + j * length
            ref[j, 0, :, :HEAD] = key_part[start : start + length]
            ref[j, 0, :, HEAD:] = value_part[start : start + length]
    query_grad = dot(score_grad, keys).astype(BF16)
    for h in range(HEADS):
        rows_h = slice(h * length, (h + 1) * length)
        query_grad_ref[0, :, h * HEAD : (h + 1) * HEAD] = query_grad[rows_h]
        gate_grad_ref[0, :, h * HEAD : (h + 1) * HEAD] = gate_grad[rows_h]


def attention(query_rows, gate_logits, gated_grad, mine, other):
    seqs, length, width = query_rows.shape
    chips = mine.shape[0]
    wide = pl.BlockSpec((1, length, width), lambda s: (s, 0, 0))
    stack = pl.BlockSpec((chips, 1, length, 2 * HEAD), lambda s: (0, s, 0, 0))
    full = jax.ShapeDtypeStruct((seqs, length, width), BF16)
    part = jax.ShapeDtypeStruct(mine.shape, BF16)
    flops = 12 * seqs * HEADS * length * 2 * chips * length * HEAD
    return pl.pallas_call(
        attention_kernel,
        grid=(seqs,),
        in_specs=[wide] * 3 + [stack] * 2,
        out_specs=[wide] * 2 + [stack] * 2,
        out_shape=[full] * 2 + [part] * 2,
        compiler_params=params(ATTENTION_MIB if chips <= 4 else 60),
        cost_estimate=cost(flops * 4, 8 * MIB),
        name="attention",
    )(query_rows, gate_logits, gated_grad, mine, other)


def merge_kernel(mine_ref, arrived_ref, out_ref):
    out_ref[...] = (mine_ref[...].astype(F32) + arrived_ref[...].astype(F32)).astype(BF16)


def close_kernel(parts_ref, key_ref, value_ref):
    total = parts_ref[0].astype(F32)
    for j in range(1, parts_ref.shape[0]):
        total = total + parts_ref[j].astype(F32)
    key_ref[...] = total[:, :, :HEAD].astype(BF16)
    value_ref[...] = total[:, :, HEAD:].astype(BF16)


def slots(routes_ref, weights_ref, experts):
    routes = routes_ref[...]
    tokens = routes.shape[1]
    live = routes < experts
    expert = jnp.sum(jnp.where(live, routes, 0), axis=0, keepdims=True)
    has_live = jnp.sum(live.astype(jnp.int32), axis=0, keepdims=True) > 0
    weight = jnp.sum(
        jnp.where(live, weights_ref[...].astype(F32), 0.0), axis=0, keepdims=True
    )
    tall = max(experts, 16)
    member = (iota((tall, tokens), 0) == expert) & has_live
    earlier = (iota((tokens, tokens), 0) < iota((tokens, tokens), 1)).astype(BF16)
    before = dot(member.astype(BF16), earlier)
    rank = jnp.sum(jnp.where(member, before, 0.0), axis=0, keepdims=True).astype(jnp.int32)
    return jnp.where(has_live, expert * CAP + rank, -1), weight, live


def dispatch_kernel(
    experts,
    groups,
    rows,
    input_hbm,
    grad_hbm,
    routes_ref,
    weights_ref,
    out_ref,
    input_ref,
    grad_ref,
    sems,
):
    tokens, width = input_ref.shape
    step = tokens // sems.shape[1]
    copies = [
        pltpu.make_async_copy(
            src.at[pl.ds(i * step, step)], dst.at[pl.ds(i * step, step)], sems.at[a, i]
        )
        for a, (src, dst) in enumerate(((input_hbm, input_ref), (grad_hbm, grad_ref)))
        for i in range(sems.shape[1])
    ]
    for copy in copies:
        copy.start()
    slot, weight, _ = slots(routes_ref, weights_ref, experts)
    share = width // groups
    pieces = share // LANES
    total = experts * rows
    shape = (total, tokens)
    row = iota(shape, 0)
    inner = row % rows
    hit = slot == (row // rows) * CAP + (inner // pieces) % CAP
    for copy in copies:
        copy.wait()
    acc = None
    for a, (ref, value) in enumerate(((input_ref, 1.0), (grad_ref, weight))):
        for l in range(pieces):
            pick = hit & (inner // (CAP * pieces) == a) & (inner % pieces == l)
            source = jnp.concatenate(
                [
                    ref[:, g * share + l * LANES : g * share + (l + 1) * LANES]
                    for g in range(groups)
                ],
                axis=1,
            )
            term = dot(jnp.where(pick, value, 0.0).astype(BF16), source)
            acc = term if acc is None else acc + term
    acc = acc.astype(BF16)
    for g in range(groups):
        out_ref[g * total : (g + 1) * total, :] = acc[:, g * LANES : (g + 1) * LANES]


def enter_kernel(
    sources, rows, recv_ref, gate_ref, up_ref, down_ref, input_ref, grad_ref, send_ref
):
    pieces = input_ref.shape[1] // LANES
    block = min(sources, 32)
    shape = (block * CAP, block * rows)
    out_row, in_row = iota(shape, 0), iota(shape, 1)
    base = (out_row // CAP) * rows + (out_row % CAP) * pieces
    picks = [
        [(in_row == base + a * CAP * pieces + l).astype(BF16) for l in range(pieces)]
        for a in range(2)
    ]
    for b in range(sources // block):
        arrived = recv_ref[b * block * rows : (b + 1) * block * rows, :]
        here = slice(b * block * CAP, (b + 1) * block * CAP)
        inputs, grads = (
            jnp.concatenate([dot(pick, arrived) for pick in picks[a]], axis=1).astype(BF16)
            for a in range(2)
        )
        input_ref[here, :] = inputs
        grad_ref[here, :] = grads
        partial = jnp.concatenate(
            [dot(inputs, gate_ref[0]), dot(inputs, up_ref[0]), dot(grads, down_ref[0], 1, 1)],
            axis=1,
        ).astype(BF16)
        for c in range(send_ref.shape[0]):
            send_ref[c, here, :] = partial


def middle_kernel(sources, rows, *refs):
    parts = refs[:-6]
    gate_ref, up_ref, back_ref, hidden_ref, gate_rows_ref, up_rows_ref = refs[-6:]
    share = gate_ref.shape[1]
    pieces = share // LANES
    hid = gate_ref.shape[2]
    block = min(sources, 32)
    shape = (block * rows, block * CAP)
    out_row, in_row = iota(shape, 0), iota(shape, 1)
    same = out_row // rows == in_row // CAP
    inner, which = out_row % rows, in_row % CAP
    picks = [(same & (inner == which * pieces + l)).astype(BF16) for l in range(pieces)]
    pick_dot = (same & (inner == CAP * pieces + which)).astype(BF16)
    for b in range(sources // block):
        here = slice(b * block * CAP, (b + 1) * block * CAP)
        terms = [part[c, here, :].astype(F32) for part in parts for c in range(part.shape[0])]
        total = functools.reduce(jnp.add, terms)
        gate_pre, up_pre, hidden_grad = total[:, :hid], total[:, hid : 2 * hid], total[:, 2 * hid :]
        sig = jax.nn.sigmoid(gate_pre)
        silu = gate_pre * sig
        hidden = (silu * up_pre).astype(BF16)
        slope = sig * (1.0 + gate_pre * (1.0 - sig))
        gate_rows = (hidden_grad * up_pre * slope).astype(BF16)
        up_rows = (hidden_grad * silu).astype(BF16)
        hidden_ref[here, :] = hidden
        gate_rows_ref[here, :] = gate_rows
        up_rows_ref[here, :] = up_rows
        routed = jnp.sum(hidden.astype(F32) * hidden_grad, axis=1, keepdims=True)
        high = routed.astype(BF16)
        low = (routed - high.astype(F32)).astype(BF16)
        lane = iota((block * CAP, LANES), 1)
        routed_wide = jnp.where(lane < LANES // 2, high.astype(F32), low.astype(F32)).astype(BF16)
        input_rows = (
            dot(gate_rows, gate_ref[0], 1, 1) + dot(up_rows, up_ref[0], 1, 1)
        ).astype(BF16)
        back = dot(pick_dot, routed_wide)
        for l in range(pieces):
            back = back + dot(picks[l], input_rows[:, l * LANES : (l + 1) * LANES])
        back_ref[b * block * rows : (b + 1) * block * rows, :] = back.astype(BF16)


def weight_kernel(
    input_ref, grad_ref, hidden_ref, gate_rows_ref, up_rows_ref, gate_out, up_out, down_out
):
    gate_out[0] = dot(input_ref[...], gate_rows_ref[...], 0, 0)
    up_out[0] = dot(input_ref[...], up_rows_ref[...], 0, 0)
    down_out[0] = dot(hidden_ref[...], grad_ref[...], 0, 0)


def combine_kernel(
    experts, groups, rows, back_ref, routes_ref, weights_ref, input_grad_ref, route_grad_ref
):
    slot, weight, live = slots(routes_ref, weights_ref, experts)
    tokens, width = input_grad_ref.shape
    share = width // groups
    pieces = share // LANES
    total = experts * rows
    shape = (total, tokens)
    row = iota(shape, 0)
    inner = row % rows
    expert = row // rows
    hit = (slot == expert * CAP + inner // pieces) & (inner < CAP * pieces)
    wide = jnp.concatenate([back_ref[g * total : (g + 1) * total, :] for g in range(groups)], axis=1)
    for l in range(pieces):
        pick = (hit & (inner % pieces == l)).astype(BF16)
        grad = dot(pick, wide, 0, 0).astype(BF16)
        for g in range(groups):
            input_grad_ref[:, g * share + l * LANES : g * share + (l + 1) * LANES] = grad[
                :, g * LANES : (g + 1) * LANES
            ]
    hit_dot = slot == expert * CAP + inner - CAP * pieces
    hit_dot = hit_dot & (inner >= CAP * pieces) & (inner < CAP * (pieces + 1))
    routed = dot(back_ref[:total, :], hit_dot.astype(BF16), 0, 0)
    routed = routed[:1] + routed[LANES // 2 : LANES // 2 + 1]
    routed = routed / jnp.where(weight > 0.0, weight, 1.0)
    route_grad_ref[...] = jnp.where(live, routed, 0.0).astype(BF16)


def shards(
    query_rows,
    key_rows,
    value_rows,
    gate_logits,
    gated_grad,
    moe_input,
    out_grad,
    routes,
    route_weights,
    gate_proj,
    up_proj,
    down_proj,
):
    devices = lax.axis_size("expert")
    groups = lax.axis_size("dp")
    sources = devices * groups
    chips = devices // 2
    seqs, length, _ = key_rows.shape
    tokens, width = moe_input.shape
    share = width // groups
    pieces = share // LANES
    hid = gate_proj.shape[2]
    rows = -(-2 * CAP * pieces // 16) * 16
    axes = ("dp", "expert")
    swap = [(i, i ^ 1) for i in range(devices)]
    same_core = [list(range(c, devices, 2)) for c in range(2)]

    def between_chips(array):
        return lax.all_to_all(
            array, "expert", split_axis=0, concat_axis=0, axis_index_groups=same_core, tiled=True
        )

    packed = pl.pallas_call(
        pack_kernel,
        out_shape=jax.ShapeDtypeStruct((chips, seqs, length, 2 * HEAD), BF16),
        compiler_params=params(32),
        cost_estimate=cost(MIB, MIB),
        name="pack",
    )(key_rows, value_rows)
    mine = between_chips(packed)
    other = lax.ppermute(mine, "expert", swap)

    routes_t, weights_t = routes.T, route_weights.T
    send = pl.pallas_call(
        functools.partial(dispatch_kernel, devices, groups, rows),
        in_specs=[pl.BlockSpec(memory_space=pltpu.HBM)] * 2
        + [pl.BlockSpec(memory_space=pltpu.VMEM)] * 2,
        out_shape=jax.ShapeDtypeStruct((sources * rows, LANES), BF16),
        scratch_shapes=[
            pltpu.VMEM(moe_input.shape, BF16),
            pltpu.VMEM(out_grad.shape, BF16),
            pltpu.SemaphoreType.DMA((2, 4)),
        ],
        compiler_params=params(32),
        cost_estimate=cost(2e9, 2 * MIB),
        name="dispatch",
    )(moe_input, out_grad, routes_t, weights_t)
    recv = lax.all_to_all(
        send.reshape(sources, rows, LANES), axes, split_axis=0, concat_axis=0, tiled=True
    ).reshape(sources * rows, LANES)

    slot_rows = jax.ShapeDtypeStruct((sources * CAP, share), BF16)
    hid_rows = jax.ShapeDtypeStruct((sources * CAP, hid), BF16)
    few = groups <= 4
    inputs, grads, sent = pl.pallas_call(
        functools.partial(enter_kernel, sources, rows),
        out_shape=[
            slot_rows,
            slot_rows,
            jax.ShapeDtypeStruct((groups if few else 1, sources * CAP, 3 * hid), BF16),
        ],
        compiler_params=params(32),
        cost_estimate=cost(2e9, 2 * MIB),
        name="enter",
    )(recv, gate_proj, up_proj, down_proj)
    if few:
        parts = [lax.all_to_all(sent, "dp", split_axis=0, concat_axis=0, tiled=True)]
    else:
        parts = [sent] + [
            lax.ppermute(sent, "dp", [(g, (g + k) % groups) for g in range(groups)])
            for k in range(1, groups)
        ]
    back, hidden, gate_rows, up_rows = pl.pallas_call(
        functools.partial(middle_kernel, sources, rows),
        out_shape=[jax.ShapeDtypeStruct((sources * rows, LANES), BF16)] + [hid_rows] * 3,
        compiler_params=params(32 if few else 60),
        cost_estimate=cost(2e9, 2 * MIB),
        name="middle",
    )(*parts, gate_proj, up_proj)
    returned = lax.all_to_all(
        back.reshape(sources, rows, LANES), axes, split_axis=0, concat_axis=0, tiled=True
    ).reshape(sources * rows, LANES)
    gate_proj_grad, up_proj_grad, down_proj_grad = pl.pallas_call(
        weight_kernel,
        out_shape=[
            jax.ShapeDtypeStruct(gate_proj.shape, F32),
            jax.ShapeDtypeStruct(up_proj.shape, F32),
            jax.ShapeDtypeStruct(down_proj.shape, F32),
        ],
        compiler_params=params(32),
        cost_estimate=cost(2e9, 2 * MIB),
        name="weight_grads",
    )(inputs, grads, hidden, gate_rows, up_rows)
    input_grad, route_grad = pl.pallas_call(
        functools.partial(combine_kernel, devices, groups, rows),
        out_shape=[
            jax.ShapeDtypeStruct(moe_input.shape, BF16),
            jax.ShapeDtypeStruct(routes_t.shape, BF16),
        ],
        compiler_params=params(32),
        cost_estimate=cost(2e9, 2 * MIB),
        name="combine",
    )(returned, routes_t, weights_t)

    query_grad, gate_grad, mine_part, other_part = attention(
        query_rows, gate_logits, gated_grad, mine, other
    )
    arrived = lax.ppermute(other_part, "expert", swap)
    merged = pl.pallas_call(
        merge_kernel,
        out_shape=jax.ShapeDtypeStruct(mine_part.shape, BF16),
        compiler_params=params(32),
        cost_estimate=cost(MIB, 2 * MIB),
        name="merge",
    )(mine_part, arrived)
    terms = between_chips(merged)
    key_grad, value_grad = pl.pallas_call(
        close_kernel,
        out_shape=[jax.ShapeDtypeStruct((seqs, length, HEAD), BF16)] * 2,
        compiler_params=params(32),
        cost_estimate=cost(MIB, MIB),
        name="close",
    )(terms)
    return (
        query_grad,
        key_grad,
        value_grad,
        gate_grad,
        input_grad,
        route_grad.T,
        gate_proj_grad,
        up_proj_grad,
        down_proj_grad,
    )


def solution(mesh):
    rows3 = P("dp", "expert", None)
    tokens2 = P(("dp", "expert"), None)
    weights = P("expert", "dp", None)
    weights_down = P("expert", None, "dp")
    return jax.shard_map(
        shards,
        mesh=mesh,
        in_specs=(rows3,) * 5 + (tokens2,) * 4 + (weights, weights, weights_down),
        out_specs=(rows3,) * 4 + (tokens2,) * 2 + (weights, weights, weights_down),
        check_vma=False,
    )
```

```python
import functools

import jax
import jax.numpy as jnp
from jax import lax
from jax.experimental import pallas as pl
from jax.experimental.pallas import tpu as pltpu
from jax.sharding import PartitionSpec as P

HEADS = 8
HEAD = 256
CAP = 2
LANES = 128
BF16 = jnp.bfloat16
F32 = jnp.float32
MIB = 1 << 20
ATTENTION_MIB = 32
IN_HBM = pl.BlockSpec(memory_space=pltpu.HBM)
IN_VMEM = pl.BlockSpec(memory_space=pltpu.VMEM)
ANYWHERE = pl.BlockSpec(memory_space=pl.ANY)


def dot(a, b, ca=1, cb=0):
    return lax.dot_general(a, b, (((ca,), (cb,)), ((), ())), preferred_element_type=F32)


def iota(shape, dim):
    return lax.broadcasted_iota(jnp.int32, shape, dim)


def params(mib):
    return pltpu.CompilerParams(vmem_limit_bytes=mib * MIB)


def cost(flops, bytes_accessed):
    return pl.CostEstimate(flops=int(flops), bytes_accessed=int(bytes_accessed), transcendentals=0)


def pack_kernel(key_hbm, value_hbm, out_ref, key_ref, value_ref, sems):
    copies = [
        pltpu.make_async_copy(src, dst, sems.at[i])
        for i, (src, dst) in enumerate(((key_hbm, key_ref), (value_hbm, value_ref)))
    ]
    for copy in copies:
        copy.start()
    copies[0].wait()
    out_ref[:, :, :HEAD] = key_ref[...]
    copies[1].wait()
    out_ref[:, :, HEAD:] = value_ref[...]


def attention_kernel(chips, *refs):
    wide_hbm = refs[:3]
    kv_refs = refs[3 : 3 + 2 * chips]
    query_grad_hbm, gate_grad_hbm, other_ref = refs[4 + 2 * chips : 7 + 2 * chips]
    mine_refs = refs[7 + 2 * chips : 7 + 3 * chips]
    q_ref, logit_ref, grad_ref, query_grad_ref, gate_grad_ref, in_sems, out_sems = refs[
        7 + 3 * chips :
    ]
    seqs, length, _ = q_ref.shape
    side = chips * length
    scale = HEAD ** (-0.5)
    position = lax.axis_index("expert")
    chip, core = position >> 1, position & 1

    loads = [
        [
            pltpu.make_async_copy(src.at[s], dst.at[s], in_sems.at[s, i])
            for i, (src, dst) in enumerate(zip(wide_hbm, (q_ref, logit_ref, grad_ref)))
        ]
        for s in range(seqs)
    ]
    for row in loads:
        for load in row:
            load.start()

    shape = (1, 2 * side)
    col = iota(shape, 1)
    half, back, inner = col // side, (col % side) // length, col % length
    block = 2 * (chip - back) + jnp.where(half == 0, core, 1 - core)
    key_pos = jnp.where(back <= chip, block * length + inner, 2 * side)
    query_pos = position * length + (iota((HEADS * length, 1), 0) % length)

    def stacked(ref, s):
        return jnp.concatenate(
            [ref[s, :, h * HEAD : (h + 1) * HEAD] for h in range(HEADS)], axis=0
        )

    stores = []
    for s in range(seqs):
        both = jnp.concatenate([ref[s] for ref in kv_refs], axis=0)
        keys, values = both[:, :HEAD], both[:, HEAD:]
        loads[s][0].wait()
        queries = stacked(q_ref, s)
        scores = jnp.where(key_pos <= query_pos, dot(queries, keys, 1, 1), -jnp.inf)
        row_max = jnp.max(scores, axis=1, keepdims=True)
        unnormed = jnp.exp((scores - row_max) * scale)
        probs = unnormed * (1.0 / jnp.sum(unnormed, axis=1, keepdims=True))
        probs_low = probs.astype(BF16)
        context = dot(probs_low, values)
        loads[s][1].wait()
        loads[s][2].wait()
        gate = jax.nn.sigmoid(stacked(logit_ref, s).astype(F32))
        upstream = stacked(grad_ref, s).astype(F32)
        context_grad = (upstream * gate).astype(BF16)
        gate_grad = (upstream * context * gate * (1.0 - gate)).astype(BF16)
        for h in range(HEADS):
            gate_grad_ref[s, :, h * HEAD : (h + 1) * HEAD] = gate_grad[h * length : (h + 1) * length]
        stores.append(pltpu.make_async_copy(gate_grad_ref.at[s], gate_grad_hbm.at[s], out_sems.at[s, 0]))
        stores[-1].start()
        grad_dot = jnp.sum(context_grad.astype(F32) * context, axis=1, keepdims=True)
        prob_grad = dot(context_grad, values, 1, 1)
        score_grad = (probs * (prob_grad - grad_dot)).astype(BF16)
        query_grad = (dot(score_grad, keys) * scale).astype(BF16)
        for h in range(HEADS):
            query_grad_ref[s, :, h * HEAD : (h + 1) * HEAD] = query_grad[h * length : (h + 1) * length]
        stores.append(pltpu.make_async_copy(query_grad_ref.at[s], query_grad_hbm.at[s], out_sems.at[s, 1]))
        stores[-1].start()
        key_part = (dot(score_grad, queries, 0, 0) * scale).astype(BF16)
        value_part = dot(probs_low, context_grad, 0, 0).astype(BF16)
        for d in range(chips):
            start = d * length
            mine_refs[d][s, :, :HEAD] = key_part[start : start + length]
            mine_refs[d][s, :, HEAD:] = value_part[start : start + length]
            start = side + d * length
            other_ref[d, s, :, :HEAD] = key_part[start : start + length]
            other_ref[d, s, :, HEAD:] = value_part[start : start + length]
    for store in stores:
        store.wait()


def attention(query_rows, gate_logits, gated_grad, pieces, after):
    seqs, length, width = query_rows.shape
    chips = len(pieces) // 2
    full = jax.ShapeDtypeStruct((seqs, length, width), BF16)
    part = jax.ShapeDtypeStruct(pieces[0].shape, BF16)
    flops = 12 * seqs * HEADS * length * 2 * chips * length * HEAD
    out = pl.pallas_call(
        functools.partial(attention_kernel, chips),
        in_specs=[IN_HBM] * 3 + [IN_VMEM] * (2 * chips) + [ANYWHERE],
        out_specs=[IN_HBM] * 2 + [IN_VMEM] * (1 + chips),
        out_shape=[full] * 2 + [jax.ShapeDtypeStruct((chips,) + part.shape, BF16)] + [part] * chips,
        scratch_shapes=[pltpu.VMEM(query_rows.shape, BF16)] * 5
        + [pltpu.SemaphoreType.DMA((seqs, 3)), pltpu.SemaphoreType.DMA((seqs, 2))],
        compiler_params=params(ATTENTION_MIB if chips <= 4 else 56),
        cost_estimate=cost(flops * 4, 8 * MIB),
        name="attention",
    )(query_rows, gate_logits, gated_grad, *pieces, after)
    return out[0], out[1], out[2], out[3:]


def merge_kernel(chips, *refs):
    mine, arrived, outs = refs[:chips], refs[chips], refs[chips + 1 :]
    for d in range(chips):
        outs[d][...] = (mine[d][...].astype(F32) + arrived[d].astype(F32)).astype(BF16)


def close_kernel(*refs):
    parts, (key_ref, value_ref) = refs[:-2], refs[-2:]
    total = parts[0][...].astype(F32)
    for part in parts[1:]:
        total = total + part[...].astype(F32)
    key_ref[...] = total[:, :, :HEAD].astype(BF16)
    value_ref[...] = total[:, :, HEAD:].astype(BF16)


def slots(routes_ref, weights_ref, experts):
    routes = routes_ref[...]
    tokens = routes.shape[1]
    live = routes < experts
    expert = jnp.sum(jnp.where(live, routes, 0), axis=0, keepdims=True)
    has_live = jnp.sum(live.astype(jnp.int32), axis=0, keepdims=True) > 0
    weight = jnp.sum(
        jnp.where(live, weights_ref[...].astype(F32), 0.0), axis=0, keepdims=True
    )
    tall = max(experts, 16)
    member = (iota((tall, tokens), 0) == expert) & has_live
    earlier = (iota((tokens, tokens), 0) < iota((tokens, tokens), 1)).astype(BF16)
    before = dot(member.astype(BF16), earlier)
    rank = jnp.sum(jnp.where(member, before, 0.0), axis=0, keepdims=True).astype(jnp.int32)
    return jnp.where(has_live, expert * CAP + rank, -1), weight, live


def dispatch_kernel(
    experts, groups, rows, input_ref, grad_ref, routes_ref, weights_ref, after_ref, out_ref
):
    tokens, width = input_ref.shape
    slot, weight, _ = slots(routes_ref, weights_ref, experts)
    share = width // groups
    pieces = share // LANES
    total = experts * rows
    shape = (total, tokens)
    row = iota(shape, 0)
    inner = row % rows
    hit = slot == (row // rows) * CAP + (inner // pieces) % CAP
    acc = None
    for a, (ref, value) in enumerate(((input_ref, 1.0), (grad_ref, weight))):
        for l in range(pieces):
            pick = hit & (inner // (CAP * pieces) == a) & (inner % pieces == l)
            source = jnp.concatenate(
                [
                    ref[:, g * share + l * LANES : g * share + (l + 1) * LANES]
                    for g in range(groups)
                ],
                axis=1,
            )
            term = dot(jnp.where(pick, value, 0.0).astype(BF16), source)
            acc = term if acc is None else acc + term
    acc = acc.astype(BF16)
    for g in range(groups):
        out_ref[g * total : (g + 1) * total, :] = acc[:, g * LANES : (g + 1) * LANES]


def enter_kernel(
    sources, rows, recv_ref, gate_ref, up_ref, down_ref, input_ref, grad_ref, send_ref
):
    pieces = input_ref.shape[1] // LANES
    block = min(sources, 32)
    shape = (block * CAP, block * rows)
    out_row, in_row = iota(shape, 0), iota(shape, 1)
    base = (out_row // CAP) * rows + (out_row % CAP) * pieces
    picks = [
        [(in_row == base + a * CAP * pieces + l).astype(BF16) for l in range(pieces)]
        for a in range(2)
    ]
    for b in range(sources // block):
        arrived = recv_ref[b * block * rows : (b + 1) * block * rows, :]
        here = slice(b * block * CAP, (b + 1) * block * CAP)
        inputs, grads = (
            jnp.concatenate([dot(pick, arrived) for pick in picks[a]], axis=1).astype(BF16)
            for a in range(2)
        )
        input_ref[here, :] = inputs
        grad_ref[here, :] = grads
        partial = jnp.concatenate(
            [dot(inputs, gate_ref[0]), dot(inputs, up_ref[0]), dot(grads, down_ref[0], 1, 1)],
            axis=1,
        )
        send_ref[here, :] = partial.astype(BF16)


def middle_kernel(sources, rows, *refs):
    parts = refs[:-7]
    gate_ref, up_ref, _, back_ref, hidden_ref, gate_rows_ref, up_rows_ref = refs[-7:]
    share = gate_ref.shape[1]
    pieces = share // LANES
    hid = gate_ref.shape[2]
    block = min(sources, 32)
    shape = (block * rows, block * CAP)
    out_row, in_row = iota(shape, 0), iota(shape, 1)
    same = out_row // rows == in_row // CAP
    inner, which = out_row % rows, in_row % CAP
    picks = [(same & (inner == which * pieces + l)).astype(BF16) for l in range(pieces)]
    pick_dot = (same & (inner == CAP * pieces + which)).astype(BF16)
    for b in range(sources // block):
        here = slice(b * block * CAP, (b + 1) * block * CAP)
        terms = [part[here, :].astype(F32) for part in parts]
        total = functools.reduce(jnp.add, terms)
        gate_pre, up_pre, hidden_grad = total[:, :hid], total[:, hid : 2 * hid], total[:, 2 * hid :]
        sig = jax.nn.sigmoid(gate_pre)
        silu = gate_pre * sig
        hidden = (silu * up_pre).astype(BF16)
        slope = sig * (1.0 + gate_pre * (1.0 - sig))
        gate_rows = (hidden_grad * up_pre * slope).astype(BF16)
        up_rows = (hidden_grad * silu).astype(BF16)
        hidden_ref[here, :] = hidden
        gate_rows_ref[here, :] = gate_rows
        up_rows_ref[here, :] = up_rows
        routed = jnp.sum(hidden.astype(F32) * hidden_grad, axis=1, keepdims=True)
        high = routed.astype(BF16)
        low = (routed - high.astype(F32)).astype(BF16)
        lane = iota((block * CAP, LANES), 1)
        routed_wide = jnp.where(lane < LANES // 2, high.astype(F32), low.astype(F32)).astype(BF16)
        input_rows = (
            dot(gate_rows, gate_ref[0], 1, 1) + dot(up_rows, up_ref[0], 1, 1)
        ).astype(BF16)
        back = dot(pick_dot, routed_wide)
        for l in range(pieces):
            back = back + dot(picks[l], input_rows[:, l * LANES : (l + 1) * LANES])
        back_ref[b * block * rows : (b + 1) * block * rows, :] = back.astype(BF16)


def weight_kernel(
    input_ref, grad_ref, hidden_ref, gate_rows_ref, up_rows_ref, gate_out, up_out, down_out
):
    gate_out[0] = dot(input_ref[...], gate_rows_ref[...], 0, 0)
    up_out[0] = dot(input_ref[...], up_rows_ref[...], 0, 0)
    down_out[0] = dot(hidden_ref[...], grad_ref[...], 0, 0)


def combine_kernel(
    experts, groups, rows, back_ref, routes_ref, weights_ref, input_grad_ref, route_grad_ref
):
    slot, weight, live = slots(routes_ref, weights_ref, experts)
    tokens, width = input_grad_ref.shape
    share = width // groups
    pieces = share // LANES
    total = experts * rows
    shape = (total, tokens)
    row = iota(shape, 0)
    inner = row % rows
    expert = row // rows
    hit = (slot == expert * CAP + inner // pieces) & (inner < CAP * pieces)
    wide = jnp.concatenate([back_ref[g * total : (g + 1) * total, :] for g in range(groups)], axis=1)
    for l in range(pieces):
        pick = (hit & (inner % pieces == l)).astype(BF16)
        grad = dot(pick, wide, 0, 0).astype(BF16)
        for g in range(groups):
            input_grad_ref[:, g * share + l * LANES : g * share + (l + 1) * LANES] = grad[
                :, g * LANES : (g + 1) * LANES
            ]
    hit_dot = slot == expert * CAP + inner - CAP * pieces
    hit_dot = hit_dot & (inner >= CAP * pieces) & (inner < CAP * (pieces + 1))
    routed = dot(back_ref[:total, :], hit_dot.astype(BF16), 0, 0)
    routed = routed[:1] + routed[LANES // 2 : LANES // 2 + 1]
    routed = routed / jnp.where(weight > 0.0, weight, 1.0)
    route_grad_ref[...] = jnp.where(live, routed, 0.0).astype(BF16)


def shards(
    query_rows,
    key_rows,
    value_rows,
    gate_logits,
    gated_grad,
    moe_input,
    out_grad,
    routes,
    route_weights,
    gate_proj,
    up_proj,
    down_proj,
):
    devices = lax.axis_size("expert")
    groups = lax.axis_size("dp")
    sources = devices * groups
    chips = devices // 2
    seqs, length, _ = key_rows.shape
    tokens, width = moe_input.shape
    share = width // groups
    pieces = share // LANES
    hid = gate_proj.shape[2]
    rows = -(-2 * CAP * pieces // 16) * 16
    axes = ("dp", "expert")
    swap = [(i, i ^ 1) for i in range(devices)]
    same_core = [list(range(c, devices, 2)) for c in range(2)]

    packed = pl.pallas_call(
        pack_kernel,
        in_specs=[IN_HBM] * 2,
        out_shape=jax.ShapeDtypeStruct((seqs, length, 2 * HEAD), BF16),
        scratch_shapes=[pltpu.VMEM(key_rows.shape, BF16)] * 2 + [pltpu.SemaphoreType.DMA((2,))],
        compiler_params=params(16),
        cost_estimate=cost(MIB, MIB),
        name="pack",
    )(key_rows, value_rows)
    mine = [packed]
    for d in range(1, chips):
        up = [(i, i + 2 * d) for i in range(devices - 2 * d)]
        mine.append(lax.ppermute(packed, "expert", up))
    other = [lax.ppermute(block, "expert", swap) for block in mine]

    routes_t, weights_t = routes.T, route_weights.T
    send = pl.pallas_call(
        functools.partial(dispatch_kernel, devices, groups, rows),
        in_specs=[IN_VMEM] * 4 + [ANYWHERE],
        out_shape=jax.ShapeDtypeStruct((sources * rows, LANES), BF16),
        compiler_params=params(16),
        cost_estimate=cost(2e9, 2 * MIB),
        name="dispatch",
    )(moe_input, out_grad, routes_t, weights_t, packed)
    recv = lax.all_to_all(
        send.reshape(sources, rows, LANES), axes, split_axis=0, concat_axis=0, tiled=True
    ).reshape(sources * rows, LANES)

    slot_rows = jax.ShapeDtypeStruct((sources * CAP, share), BF16)
    hid_rows = jax.ShapeDtypeStruct((sources * CAP, hid), BF16)
    inputs, grads, sent = pl.pallas_call(
        functools.partial(enter_kernel, sources, rows),
        out_shape=[slot_rows, slot_rows, jax.ShapeDtypeStruct((sources * CAP, 3 * hid), BF16)],
        compiler_params=params(16),
        cost_estimate=cost(2e9, 2 * MIB),
        name="enter",
    )(recv, gate_proj, up_proj, down_proj)
    parts = [sent] + [
        lax.ppermute(sent, "dp", [(g, g ^ k) for g in range(groups)]) for k in range(1, groups)
    ]

    query_grad, gate_grad, other_part, mine_part = attention(
        query_rows, gate_logits, gated_grad, mine + other, sent
    )
    arrived = lax.ppermute(other_part, "expert", swap)
    merged = pl.pallas_call(
        functools.partial(merge_kernel, chips),
        out_shape=[jax.ShapeDtypeStruct(packed.shape, BF16)] * chips,
        compiler_params=params(16),
        cost_estimate=cost(MIB, 2 * MIB),
        name="merge",
    )(*mine_part, arrived)
    terms = [merged[0]]
    for d in range(1, chips):
        down = [(i, i - 2 * d) for i in range(2 * d, devices)]
        terms.append(lax.ppermute(merged[d], "expert", down))
    key_grad, value_grad = pl.pallas_call(
        close_kernel,
        out_shape=[jax.ShapeDtypeStruct((seqs, length, HEAD), BF16)] * 2,
        compiler_params=params(16),
        cost_estimate=cost(MIB, MIB),
        name="close",
    )(*terms)

    back, hidden, gate_rows, up_rows = pl.pallas_call(
        functools.partial(middle_kernel, sources, rows),
        in_specs=[IN_VMEM] * (len(parts) + 2) + [ANYWHERE],
        out_shape=[jax.ShapeDtypeStruct((sources * rows, LANES), BF16)] + [hid_rows] * 3,
        compiler_params=params(16 if groups <= 4 else 60),
        cost_estimate=cost(2e9, 2 * MIB),
        name="middle",
    )(*parts, gate_proj, up_proj, merged[0])
    returned = lax.all_to_all(
        back.reshape(sources, rows, LANES), axes, split_axis=0, concat_axis=0, tiled=True
    ).reshape(sources * rows, LANES)
    gate_proj_grad, up_proj_grad, down_proj_grad = pl.pallas_call(
        weight_kernel,
        out_shape=[
            jax.ShapeDtypeStruct(gate_proj.shape, F32),
            jax.ShapeDtypeStruct(up_proj.shape, F32),
            jax.ShapeDtypeStruct(down_proj.shape, F32),
        ],
        compiler_params=params(16),
        cost_estimate=cost(2e9, 2 * MIB),
        name="weight_grads",
    )(inputs, grads, hidden, gate_rows, up_rows)
    input_grad, route_grad = pl.pallas_call(
        functools.partial(combine_kernel, devices, groups, rows),
        out_shape=[
            jax.ShapeDtypeStruct(moe_input.shape, BF16),
            jax.ShapeDtypeStruct(routes_t.shape, BF16),
        ],
        compiler_params=params(16),
        cost_estimate=cost(2e9, 2 * MIB),
        name="combine",
    )(returned, routes_t, weights_t)

    return (
        query_grad,
        key_grad,
        value_grad,
        gate_grad,
        input_grad,
        route_grad.T,
        gate_proj_grad,
        up_proj_grad,
        down_proj_grad,
    )


def solution(mesh):
    rows3 = P("dp", "expert", None)
    tokens2 = P(("dp", "expert"), None)
    weights = P("expert", "dp", None)
    weights_down = P("expert", None, "dp")
    return jax.shard_map(
        shards,
        mesh=mesh,
        in_specs=(rows3,) * 5 + (tokens2,) * 4 + (weights, weights, weights_down),
        out_specs=(rows3,) * 4 + (tokens2,) * 2 + (weights, weights, weights_down),
        check_vma=False,
    )
```

```python
import functools

import jax
import jax.numpy as jnp
from jax import lax
from jax.experimental import pallas as pl
from jax.experimental.pallas import tpu as pltpu
from jax.sharding import PartitionSpec as P

HEADS = 8
HEAD = 256
CAP = 2
LANES = 128
BF16 = jnp.bfloat16
F32 = jnp.float32
MIB = 1 << 20
ATTENTION_MIB = 32
IN_HBM = pl.BlockSpec(memory_space=pltpu.HBM)
IN_VMEM = pl.BlockSpec(memory_space=pltpu.VMEM)
ANYWHERE = pl.BlockSpec(memory_space=pl.ANY)


def dot(a, b, ca=1, cb=0):
    return lax.dot_general(a, b, (((ca,), (cb,)), ((), ())), preferred_element_type=F32)


def div(x, size):
    assert size & (size - 1) == 0
    return x >> (size.bit_length() - 1)


def mod(x, size):
    assert size & (size - 1) == 0
    return x & (size - 1)


def iota(shape, dim):
    return lax.broadcasted_iota(jnp.int32, shape, dim)


def params(mib):
    return pltpu.CompilerParams(vmem_limit_bytes=mib * MIB)


def cost(flops, bytes_accessed):
    return pl.CostEstimate(flops=int(flops), bytes_accessed=int(bytes_accessed), transcendentals=0)


def pack_kernel(key_hbm, value_hbm, out_ref, key_ref, value_ref, sems):
    copies = [
        pltpu.make_async_copy(src, dst, sems.at[i])
        for i, (src, dst) in enumerate(((key_hbm, key_ref), (value_hbm, value_ref)))
    ]
    for copy in copies:
        copy.start()
    copies[0].wait()
    out_ref[:, :, :HEAD] = key_ref[...]
    copies[1].wait()
    out_ref[:, :, HEAD:] = value_ref[...]


def attention_kernel(chips, *refs):
    wide_hbm = refs[:3]
    kv_refs = refs[3 : 3 + 2 * chips]
    query_grad_hbm, gate_grad_hbm, other_ref = refs[4 + 2 * chips : 7 + 2 * chips]
    mine_refs = refs[7 + 2 * chips : 7 + 3 * chips]
    q_ref, logit_ref, grad_ref, query_grad_ref, gate_grad_ref, in_sems, out_sems = refs[
        7 + 3 * chips :
    ]
    seqs, length, _ = q_ref.shape
    side = chips * length
    scale = HEAD ** (-0.5)
    position = lax.axis_index("expert")
    chip, core = position >> 1, position & 1

    loads = [
        [
            pltpu.make_async_copy(src.at[s], dst.at[s], in_sems.at[s, i])
            for i, (src, dst) in enumerate(zip(wide_hbm, (q_ref, logit_ref, grad_ref)))
        ]
        for s in range(seqs)
    ]
    for row in loads:
        for load in row:
            load.start()

    shape = (1, 2 * side)
    col = iota(shape, 1)
    half, back, inner = div(col, side), div(mod(col, side), length), mod(col, length)
    block = 2 * (chip - back) + jnp.where(half == 0, core, 1 - core)
    key_pos = jnp.where(back <= chip, block * length + inner, 2 * side)
    query_pos = position * length + mod(iota((HEADS * length, 1), 0), length)

    def stacked(ref, s):
        return jnp.concatenate(
            [ref[s, :, h * HEAD : (h + 1) * HEAD] for h in range(HEADS)], axis=0
        )

    stores = []
    for s in range(seqs):
        both = jnp.concatenate([ref[s] for ref in kv_refs], axis=0)
        keys, values = both[:, :HEAD], both[:, HEAD:]
        loads[s][0].wait()
        queries = stacked(q_ref, s)
        scores = jnp.where(key_pos <= query_pos, dot(queries, keys, 1, 1), -jnp.inf)
        row_max = jnp.max(scores, axis=1, keepdims=True)
        unnormed = jnp.exp((scores - row_max) * scale)
        probs = unnormed * (1.0 / jnp.sum(unnormed, axis=1, keepdims=True))
        probs_low = probs.astype(BF16)
        context = dot(probs_low, values)
        loads[s][1].wait()
        loads[s][2].wait()
        gate = jax.nn.sigmoid(stacked(logit_ref, s).astype(F32))
        upstream = stacked(grad_ref, s).astype(F32)
        context_grad = (upstream * gate).astype(BF16)
        gate_grad = (upstream * context * gate * (1.0 - gate)).astype(BF16)
        for h in range(HEADS):
            gate_grad_ref[s, :, h * HEAD : (h + 1) * HEAD] = gate_grad[h * length : (h + 1) * length]
        stores.append(pltpu.make_async_copy(gate_grad_ref.at[s], gate_grad_hbm.at[s], out_sems.at[s, 0]))
        stores[-1].start()
        grad_dot = jnp.sum(context_grad.astype(F32) * context, axis=1, keepdims=True)
        prob_grad = dot(context_grad, values, 1, 1)
        score_grad = (probs * (prob_grad - grad_dot)).astype(BF16)
        query_grad = (dot(score_grad, keys) * scale).astype(BF16)
        for h in range(HEADS):
            query_grad_ref[s, :, h * HEAD : (h + 1) * HEAD] = query_grad[h * length : (h + 1) * length]
        stores.append(pltpu.make_async_copy(query_grad_ref.at[s], query_grad_hbm.at[s], out_sems.at[s, 1]))
        stores[-1].start()
        key_part = (dot(score_grad, queries, 0, 0) * scale).astype(BF16)
        value_part = dot(probs_low, context_grad, 0, 0).astype(BF16)
        for d in range(chips):
            start = d * length
            mine_refs[d][s, :, :HEAD] = key_part[start : start + length]
            mine_refs[d][s, :, HEAD:] = value_part[start : start + length]
            start = side + d * length
            other_ref[d, s, :, :HEAD] = key_part[start : start + length]
            other_ref[d, s, :, HEAD:] = value_part[start : start + length]
    for store in stores:
        store.wait()


def attention(query_rows, gate_logits, gated_grad, pieces, after):
    seqs, length, width = query_rows.shape
    chips = len(pieces) // 2
    full = jax.ShapeDtypeStruct((seqs, length, width), BF16)
    part = jax.ShapeDtypeStruct(pieces[0].shape, BF16)
    flops = 12 * seqs * HEADS * length * 2 * chips * length * HEAD
    out = pl.pallas_call(
        functools.partial(attention_kernel, chips),
        in_specs=[IN_HBM] * 3 + [IN_VMEM] * (2 * chips) + [ANYWHERE],
        out_specs=[IN_HBM] * 2 + [IN_VMEM] * (1 + chips),
        out_shape=[full] * 2 + [jax.ShapeDtypeStruct((chips,) + part.shape, BF16)] + [part] * chips,
        scratch_shapes=[pltpu.VMEM(query_rows.shape, BF16)] * 5
        + [pltpu.SemaphoreType.DMA((seqs, 3)), pltpu.SemaphoreType.DMA((seqs, 2))],
        compiler_params=params(ATTENTION_MIB if chips <= 4 else 56),
        cost_estimate=cost(flops * 4, 8 * MIB),
        name="attention",
    )(query_rows, gate_logits, gated_grad, *pieces, after)
    return out[0], out[1], out[2], out[3:]


def merge_kernel(chips, *refs):
    mine, arrived, outs = refs[:chips], refs[chips], refs[chips + 1 :]
    for d in range(chips):
        outs[d][...] = (mine[d][...].astype(F32) + arrived[d].astype(F32)).astype(BF16)


def close_kernel(*refs):
    parts, (key_ref, value_ref) = refs[:-3], refs[-2:]
    total = parts[0][...].astype(F32)
    for part in parts[1:]:
        total = total + part[...].astype(F32)
    key_ref[...] = total[:, :, :HEAD].astype(BF16)
    value_ref[...] = total[:, :, HEAD:].astype(BF16)


def slots(routes_ref, weights_ref, experts):
    routes = routes_ref[...]
    tokens = routes.shape[1]
    live = routes < experts
    expert = jnp.sum(jnp.where(live, routes, 0), axis=0, keepdims=True)
    has_live = jnp.sum(live.astype(jnp.int32), axis=0, keepdims=True) > 0
    weight = jnp.sum(
        jnp.where(live, weights_ref[...].astype(F32), 0.0), axis=0, keepdims=True
    )
    tall = max(experts, 16)
    member = (iota((tall, tokens), 0) == expert) & has_live
    earlier = (iota((tokens, tokens), 0) < iota((tokens, tokens), 1)).astype(BF16)
    before = dot(member.astype(BF16), earlier)
    rank = jnp.sum(jnp.where(member, before, 0.0), axis=0, keepdims=True).astype(jnp.int32)
    return jnp.where(has_live, expert * CAP + rank, -1), weight, live


def dispatch_kernel(
    experts, groups, rows, input_ref, grad_ref, routes_ref, weights_ref, after_ref, out_ref
):
    tokens, width = input_ref.shape
    slot, weight, _ = slots(routes_ref, weights_ref, experts)
    share = width // groups
    pieces = share // LANES
    total = experts * rows
    shape = (total, tokens)
    row = iota(shape, 0)
    inner = mod(row, rows)
    hit = slot == div(row, rows) * CAP + mod(div(inner, pieces), CAP)
    hit = jnp.where(hit, mod(inner, pieces) + pieces * div(inner, CAP * pieces), -1)
    acc = None
    for a, (ref, value) in enumerate(((input_ref, 1.0), (grad_ref, weight))):
        for l in range(pieces):
            pick = hit == a * pieces + l
            source = jnp.concatenate(
                [
                    ref[:, g * share + l * LANES : g * share + (l + 1) * LANES]
                    for g in range(groups)
                ],
                axis=1,
            )
            term = dot(jnp.where(pick, value, 0.0).astype(BF16), source)
            acc = term if acc is None else acc + term
    acc = acc.astype(BF16)
    for g in range(groups):
        out_ref[g * total : (g + 1) * total, :] = acc[:, g * LANES : (g + 1) * LANES]


def enter_kernel(
    sources, rows, recv_ref, gate_ref, up_ref, down_ref, input_ref, grad_ref, send_ref
):
    pieces = input_ref.shape[1] // LANES
    block = min(sources, 32)
    shape = (block * CAP, block * rows)
    out_row, in_row = iota(shape, 0), iota(shape, 1)
    offset = in_row - div(out_row, CAP) * rows - mod(out_row, CAP) * pieces
    picks = [
        [(offset == a * CAP * pieces + l).astype(BF16) for l in range(pieces)]
        for a in range(2)
    ]
    for b in range(sources // block):
        arrived = recv_ref[b * block * rows : (b + 1) * block * rows, :]
        here = slice(b * block * CAP, (b + 1) * block * CAP)
        inputs, grads = (
            jnp.concatenate([dot(pick, arrived) for pick in picks[a]], axis=1).astype(BF16)
            for a in range(2)
        )
        input_ref[here, :] = inputs
        grad_ref[here, :] = grads
        partial = jnp.concatenate(
            [dot(inputs, gate_ref[0]), dot(inputs, up_ref[0]), dot(grads, down_ref[0], 1, 1)],
            axis=1,
        )
        send_ref[here, :] = partial.astype(BF16)


def middle_kernel(sources, rows, *refs):
    parts = refs[:-7]
    gate_ref, up_ref, _, back_ref, hidden_ref, gate_rows_ref, up_rows_ref = refs[-7:]
    share = gate_ref.shape[1]
    pieces = share // LANES
    hid = gate_ref.shape[2]
    block = min(sources, 32)
    shape = (block * rows, block * CAP)
    out_row, in_row = iota(shape, 0), iota(shape, 1)
    same = div(out_row, rows) == div(in_row, CAP)
    inner, which = mod(out_row, rows), mod(in_row, CAP)
    offset = jnp.where(same, inner - which * pieces, -1)
    picks = [(offset == l).astype(BF16) for l in range(pieces)]
    pick_dot = (same & (inner == CAP * pieces + which)).astype(BF16)
    for b in range(sources // block):
        here = slice(b * block * CAP, (b + 1) * block * CAP)
        terms = [part[here, :].astype(F32) for part in parts]
        total = functools.reduce(jnp.add, terms)
        gate_pre, up_pre, hidden_grad = total[:, :hid], total[:, hid : 2 * hid], total[:, 2 * hid :]
        sig = jax.nn.sigmoid(gate_pre)
        silu = gate_pre * sig
        hidden = (silu * up_pre).astype(BF16)
        slope = sig * (1.0 + gate_pre * (1.0 - sig))
        gate_rows = (hidden_grad * up_pre * slope).astype(BF16)
        up_rows = (hidden_grad * silu).astype(BF16)
        hidden_ref[here, :] = hidden
        gate_rows_ref[here, :] = gate_rows
        up_rows_ref[here, :] = up_rows
        routed = jnp.sum(hidden.astype(F32) * hidden_grad, axis=1, keepdims=True)
        high = routed.astype(BF16)
        low = (routed - high.astype(F32)).astype(BF16)
        lane = iota((block * CAP, LANES), 1)
        routed_wide = jnp.where(lane < LANES // 2, high.astype(F32), low.astype(F32)).astype(BF16)
        input_rows = (
            dot(gate_rows, gate_ref[0], 1, 1) + dot(up_rows, up_ref[0], 1, 1)
        ).astype(BF16)
        back = dot(pick_dot, routed_wide)
        for l in range(pieces):
            back = back + dot(picks[l], input_rows[:, l * LANES : (l + 1) * LANES])
        back_ref[b * block * rows : (b + 1) * block * rows, :] = back.astype(BF16)


def weight_kernel(
    input_ref, grad_ref, hidden_ref, gate_rows_ref, up_rows_ref, gate_out, up_out, down_out
):
    gate_out[0] = dot(input_ref[...], gate_rows_ref[...], 0, 0)
    up_out[0] = dot(input_ref[...], up_rows_ref[...], 0, 0)
    down_out[0] = dot(hidden_ref[...], grad_ref[...], 0, 0)


def combine_kernel(
    experts, groups, rows, back_ref, routes_ref, weights_ref, input_grad_ref, route_grad_ref
):
    slot, weight, live = slots(routes_ref, weights_ref, experts)
    tokens, width = input_grad_ref.shape
    share = width // groups
    pieces = share // LANES
    total = experts * rows
    shape = (total, tokens)
    row = iota(shape, 0)
    inner = mod(row, rows)
    expert = div(row, rows)
    hit = (slot == expert * CAP + div(inner, pieces)) & (inner < CAP * pieces)
    hit = jnp.where(hit, mod(inner, pieces), -1)
    wide = jnp.concatenate([back_ref[g * total : (g + 1) * total, :] for g in range(groups)], axis=1)
    for l in range(pieces):
        pick = (hit == l).astype(BF16)
        grad = dot(pick, wide, 0, 0).astype(BF16)
        for g in range(groups):
            input_grad_ref[:, g * share + l * LANES : g * share + (l + 1) * LANES] = grad[
                :, g * LANES : (g + 1) * LANES
            ]
    hit_dot = slot == expert * CAP + inner - CAP * pieces
    hit_dot = hit_dot & (inner >= CAP * pieces) & (inner < CAP * (pieces + 1))
    routed = dot(back_ref[:total, :], hit_dot.astype(BF16), 0, 0)
    routed = routed[:1] + routed[LANES // 2 : LANES // 2 + 1]
    routed = routed / jnp.where(weight > 0.0, weight, 1.0)
    route_grad_ref[...] = jnp.where(live, routed, 0.0).astype(BF16)


def shards(
    query_rows,
    key_rows,
    value_rows,
    gate_logits,
    gated_grad,
    moe_input,
    out_grad,
    routes,
    route_weights,
    gate_proj,
    up_proj,
    down_proj,
):
    devices = lax.axis_size("expert")
    groups = lax.axis_size("dp")
    sources = devices * groups
    chips = devices // 2
    seqs, length, _ = key_rows.shape
    tokens, width = moe_input.shape
    share = width // groups
    pieces = share // LANES
    hid = gate_proj.shape[2]
    rows = -(-2 * CAP * pieces // 16) * 16
    axes = ("dp", "expert")
    swap = [(i, i ^ 1) for i in range(devices)]
    same_core = [list(range(c, devices, 2)) for c in range(2)]

    packed = pl.pallas_call(
        pack_kernel,
        in_specs=[IN_HBM] * 2,
        out_shape=jax.ShapeDtypeStruct((seqs, length, 2 * HEAD), BF16),
        scratch_shapes=[pltpu.VMEM(key_rows.shape, BF16)] * 2 + [pltpu.SemaphoreType.DMA((2,))],
        compiler_params=params(60),
        cost_estimate=cost(MIB, MIB),
        name="pack",
    )(key_rows, value_rows)
    mine = [packed]
    for d in range(1, chips):
        up = [(i, i + 2 * d) for i in range(devices - 2 * d)]
        mine.append(lax.ppermute(packed, "expert", up))
    other = [lax.ppermute(block, "expert", swap) for block in mine]

    routes_t, weights_t = routes.T, route_weights.T
    send = pl.pallas_call(
        functools.partial(dispatch_kernel, devices, groups, rows),
        in_specs=[IN_VMEM] * 4 + [ANYWHERE],
        out_shape=jax.ShapeDtypeStruct((sources * rows, LANES), BF16),
        compiler_params=params(16),
        cost_estimate=cost(2e9, 2 * MIB),
        name="dispatch",
    )(moe_input, out_grad, routes_t, weights_t, mine[min(1, chips - 1)])
    recv = lax.all_to_all(
        send.reshape(sources, rows, LANES), axes, split_axis=0, concat_axis=0, tiled=True
    ).reshape(sources * rows, LANES)

    slot_rows = jax.ShapeDtypeStruct((sources * CAP, share), BF16)
    hid_rows = jax.ShapeDtypeStruct((sources * CAP, hid), BF16)
    inputs, grads, sent = pl.pallas_call(
        functools.partial(enter_kernel, sources, rows),
        out_shape=[slot_rows, slot_rows, jax.ShapeDtypeStruct((sources * CAP, 3 * hid), BF16)],
        compiler_params=params(16),
        cost_estimate=cost(2e9, 2 * MIB),
        name="enter",
    )(recv, gate_proj, up_proj, down_proj)
    parts = [sent] + [
        lax.ppermute(sent, "dp", [(g, g ^ k) for g in range(groups)]) for k in range(1, groups)
    ]

    query_grad, gate_grad, other_part, mine_part = attention(
        query_rows, gate_logits, gated_grad, mine + other, sent
    )
    arrived = lax.ppermute(other_part, "expert", swap)
    merged = pl.pallas_call(
        functools.partial(merge_kernel, chips),
        out_shape=[jax.ShapeDtypeStruct(packed.shape, BF16)] * chips,
        compiler_params=params(16),
        cost_estimate=cost(MIB, 2 * MIB),
        name="merge",
    )(*mine_part, arrived)
    terms = [merged[0]]
    for d in range(1, chips):
        down = [(i, i - 2 * d) for i in range(2 * d, devices)]
        terms.append(lax.ppermute(merged[d], "expert", down))
    back, hidden, gate_rows, up_rows = pl.pallas_call(
        functools.partial(middle_kernel, sources, rows),
        in_specs=[IN_VMEM] * (len(parts) + 2) + [ANYWHERE],
        out_shape=[jax.ShapeDtypeStruct((sources * rows, LANES), BF16)] + [hid_rows] * 3,
        compiler_params=params(16 if groups <= 4 else 60),
        cost_estimate=cost(2e9, 2 * MIB),
        name="middle",
    )(*parts, gate_proj, up_proj, terms[min(1, chips - 1)])
    returned = lax.all_to_all(
        back.reshape(sources, rows, LANES), axes, split_axis=0, concat_axis=0, tiled=True
    ).reshape(sources * rows, LANES)
    gate_proj_grad, up_proj_grad, down_proj_grad = pl.pallas_call(
        weight_kernel,
        out_shape=[
            jax.ShapeDtypeStruct(gate_proj.shape, F32),
            jax.ShapeDtypeStruct(up_proj.shape, F32),
            jax.ShapeDtypeStruct(down_proj.shape, F32),
        ],
        compiler_params=params(16),
        cost_estimate=cost(2e9, 2 * MIB),
        name="weight_grads",
    )(inputs, grads, hidden, gate_rows, up_rows)
    input_grad, route_grad = pl.pallas_call(
        functools.partial(combine_kernel, devices, groups, rows),
        out_shape=[
            jax.ShapeDtypeStruct(moe_input.shape, BF16),
            jax.ShapeDtypeStruct(routes_t.shape, BF16),
        ],
        compiler_params=params(16),
        cost_estimate=cost(2e9, 2 * MIB),
        name="combine",
    )(returned, routes_t, weights_t)

    key_grad, value_grad = pl.pallas_call(
        close_kernel,
        in_specs=[IN_VMEM] * chips + [ANYWHERE],
        out_shape=[jax.ShapeDtypeStruct((seqs, length, HEAD), BF16)] * 2,
        compiler_params=params(16),
        cost_estimate=cost(MIB, MIB),
        name="close",
    )(*terms, route_grad)
    return (
        query_grad,
        key_grad,
        value_grad,
        gate_grad,
        input_grad,
        route_grad.T,
        gate_proj_grad,
        up_proj_grad,
        down_proj_grad,
    )


def solution(mesh):
    rows3 = P("dp", "expert", None)
    tokens2 = P(("dp", "expert"), None)
    weights = P("expert", "dp", None)
    weights_down = P("expert", None, "dp")
    return jax.shard_map(
        shards,
        mesh=mesh,
        in_specs=(rows3,) * 5 + (tokens2,) * 4 + (weights, weights, weights_down),
        out_specs=(rows3,) * 4 + (tokens2,) * 2 + (weights, weights, weights_down),
        check_vma=False,
    )
```

```python
import functools

import jax
import jax.numpy as jnp
from jax import lax
from jax.experimental import pallas as pl
from jax.experimental.pallas import tpu as pltpu
from jax.sharding import PartitionSpec as P

HEADS = 8
HEAD = 256
CAP = 2
LANES = 128
BF16 = jnp.bfloat16
F32 = jnp.float32
MIB = 1 << 20
ATTENTION_MIB = 32
IN_HBM = pl.BlockSpec(memory_space=pltpu.HBM)
IN_VMEM = pl.BlockSpec(memory_space=pltpu.VMEM)
ANYWHERE = pl.BlockSpec(memory_space=pl.ANY)


def dot(a, b, ca=1, cb=0):
    return lax.dot_general(a, b, (((ca,), (cb,)), ((), ())), preferred_element_type=F32)


def div(x, size):
    assert size & (size - 1) == 0
    return x >> (size.bit_length() - 1)


def mod(x, size):
    assert size & (size - 1) == 0
    return x & (size - 1)


def iota(shape, dim):
    return lax.broadcasted_iota(jnp.int32, shape, dim)


def params(mib):
    return pltpu.CompilerParams(vmem_limit_bytes=mib * MIB)


def cost(flops, bytes_accessed):
    return pl.CostEstimate(flops=int(flops), bytes_accessed=int(bytes_accessed), transcendentals=0)


def pack_kernel(key_hbm, value_hbm, out_ref, key_ref, value_ref, sems):
    copies = [
        pltpu.make_async_copy(src, dst, sems.at[i])
        for i, (src, dst) in enumerate(((key_hbm, key_ref), (value_hbm, value_ref)))
    ]
    for copy in copies:
        copy.start()
    copies[0].wait()
    out_ref[:, :, :HEAD] = key_ref[...]
    copies[1].wait()
    out_ref[:, :, HEAD:] = value_ref[...]


def attention_kernel(chips, *refs):
    wide_hbm = refs[:3]
    kv_refs = refs[3 : 3 + 2 * chips]
    query_grad_hbm, gate_grad_hbm, other_ref = refs[4 + 2 * chips : 7 + 2 * chips]
    mine_refs = refs[7 + 2 * chips : 7 + 3 * chips]
    q_ref, logit_ref, grad_ref, query_grad_ref, gate_grad_ref, in_sems, out_sems = refs[
        7 + 3 * chips :
    ]
    seqs, length, _ = q_ref.shape
    side = chips * length
    scale = HEAD ** (-0.5)
    position = lax.axis_index("expert")
    chip, core = position >> 1, position & 1

    loads = [
        [
            pltpu.make_async_copy(src.at[s], dst.at[s], in_sems.at[s, i])
            for i, (src, dst) in enumerate(zip(wide_hbm, (q_ref, logit_ref, grad_ref)))
        ]
        for s in range(seqs)
    ]
    for row in loads:
        for load in row:
            load.start()

    shape = (1, 2 * side)
    col = iota(shape, 1)
    half, back, inner = div(col, side), div(mod(col, side), length), mod(col, length)
    block = 2 * (chip - back) + jnp.where(half == 0, core, 1 - core)
    key_pos = jnp.where(back <= chip, block * length + inner, 2 * side)
    query_pos = position * length + mod(iota((HEADS * length, 1), 0), length)

    def stacked(ref, s):
        return jnp.concatenate(
            [ref[s, :, h * HEAD : (h + 1) * HEAD] for h in range(HEADS)], axis=0
        )

    stores = []
    for s in range(seqs):
        both = jnp.concatenate([ref[s] for ref in kv_refs], axis=0)
        keys, values = both[:, :HEAD], both[:, HEAD:]
        loads[s][0].wait()
        queries = stacked(q_ref, s)
        scores = jnp.where(key_pos <= query_pos, dot(queries, keys, 1, 1), -jnp.inf)
        row_max = jnp.max(scores, axis=1, keepdims=True)
        unnormed = jnp.exp((scores - row_max) * scale)
        probs = unnormed * (1.0 / jnp.sum(unnormed, axis=1, keepdims=True))
        probs_low = probs.astype(BF16)
        context = dot(probs_low, values)
        loads[s][1].wait()
        loads[s][2].wait()
        gate = jax.nn.sigmoid(stacked(logit_ref, s).astype(F32))
        upstream = stacked(grad_ref, s).astype(F32)
        context_grad = (upstream * gate).astype(BF16)
        gate_grad = (upstream * context * gate * (1.0 - gate)).astype(BF16)
        for h in range(HEADS):
            gate_grad_ref[s, :, h * HEAD : (h + 1) * HEAD] = gate_grad[h * length : (h + 1) * length]
        stores.append(pltpu.make_async_copy(gate_grad_ref.at[s], gate_grad_hbm.at[s], out_sems.at[s, 0]))
        stores[-1].start()
        grad_dot = jnp.sum(context_grad.astype(F32) * context, axis=1, keepdims=True)
        prob_grad = dot(context_grad, values, 1, 1)
        score_grad = (probs * (prob_grad - grad_dot)).astype(BF16)
        query_grad = (dot(score_grad, keys) * scale).astype(BF16)
        for h in range(HEADS):
            query_grad_ref[s, :, h * HEAD : (h + 1) * HEAD] = query_grad[h * length : (h + 1) * length]
        stores.append(pltpu.make_async_copy(query_grad_ref.at[s], query_grad_hbm.at[s], out_sems.at[s, 1]))
        stores[-1].start()
        key_part = (dot(score_grad, queries, 0, 0) * scale).astype(BF16)
        value_part = dot(probs_low, context_grad, 0, 0).astype(BF16)
        for d in range(chips):
            start = d * length
            mine_refs[d][s, :, :HEAD] = key_part[start : start + length]
            mine_refs[d][s, :, HEAD:] = value_part[start : start + length]
            start = side + d * length
            other_ref[d, s, :, :HEAD] = key_part[start : start + length]
            other_ref[d, s, :, HEAD:] = value_part[start : start + length]
    for store in stores:
        store.wait()


def attention(query_rows, gate_logits, gated_grad, pieces, after):
    seqs, length, width = query_rows.shape
    chips = len(pieces) // 2
    full = jax.ShapeDtypeStruct((seqs, length, width), BF16)
    part = jax.ShapeDtypeStruct(pieces[0].shape, BF16)
    flops = 12 * seqs * HEADS * length * 2 * chips * length * HEAD
    out = pl.pallas_call(
        functools.partial(attention_kernel, chips),
        in_specs=[IN_HBM] * 3 + [IN_VMEM] * (2 * chips) + [ANYWHERE],
        out_specs=[IN_HBM] * 2 + [IN_VMEM] * (1 + chips),
        out_shape=[full] * 2 + [jax.ShapeDtypeStruct((chips,) + part.shape, BF16)] + [part] * chips,
        scratch_shapes=[pltpu.VMEM(query_rows.shape, BF16)] * 5
        + [pltpu.SemaphoreType.DMA((seqs, 3)), pltpu.SemaphoreType.DMA((seqs, 2))],
        compiler_params=params(ATTENTION_MIB if chips <= 4 else 56),
        cost_estimate=cost(flops * 40, 8 * MIB),
        name="attention",
    )(query_rows, gate_logits, gated_grad, *pieces, after)
    return out[0], out[1], out[2], out[3:]


def merge_kernel(chips, *refs):
    mine, arrived, outs = refs[:chips], refs[chips], refs[chips + 1 :]
    for d in range(chips):
        outs[d][...] = (mine[d][...].astype(F32) + arrived[d].astype(F32)).astype(BF16)


def close_kernel(*refs):
    parts, (key_ref, value_ref) = refs[:-2], refs[-2:]
    total = parts[0][...].astype(F32)
    for part in parts[1:]:
        total = total + part[...].astype(F32)
    key_ref[...] = total[:, :, :HEAD].astype(BF16)
    value_ref[...] = total[:, :, HEAD:].astype(BF16)


def slots(routes_ref, weights_ref, experts):
    routes = routes_ref[...]
    tokens = routes.shape[1]
    live = routes < experts
    expert = jnp.sum(jnp.where(live, routes, 0), axis=0, keepdims=True)
    has_live = jnp.sum(live.astype(jnp.int32), axis=0, keepdims=True) > 0
    weight = jnp.sum(
        jnp.where(live, weights_ref[...].astype(F32), 0.0), axis=0, keepdims=True
    )
    tall = max(experts, 16)
    member = (iota((tall, tokens), 0) == expert) & has_live
    earlier = (iota((tokens, tokens), 0) < iota((tokens, tokens), 1)).astype(BF16)
    before = dot(member.astype(BF16), earlier)
    rank = jnp.sum(jnp.where(member, before, 0.0), axis=0, keepdims=True).astype(jnp.int32)
    return jnp.where(has_live, expert * CAP + rank, -1), weight, live


def dispatch_kernel(
    experts, groups, rows, input_ref, grad_ref, routes_ref, weights_ref, after_ref, out_ref
):
    tokens, width = input_ref.shape
    slot, weight, _ = slots(routes_ref, weights_ref, experts)
    share = width // groups
    pieces = share // LANES
    total = experts * rows
    shape = (total, tokens)
    row = iota(shape, 0)
    inner = mod(row, rows)
    hit = slot == div(row, rows) * CAP + mod(div(inner, pieces), CAP)
    hit = jnp.where(hit, mod(inner, pieces) + pieces * div(inner, CAP * pieces), -1)
    acc = None
    for a, (ref, value) in enumerate(((input_ref, 1.0), (grad_ref, weight))):
        for l in range(pieces):
            pick = hit == a * pieces + l
            source = jnp.concatenate(
                [
                    ref[:, g * share + l * LANES : g * share + (l + 1) * LANES]
                    for g in range(groups)
                ],
                axis=1,
            )
            term = dot(jnp.where(pick, value, 0.0).astype(BF16), source)
            acc = term if acc is None else acc + term
    acc = acc.astype(BF16)
    for g in range(groups):
        out_ref[g * total : (g + 1) * total, :] = acc[:, g * LANES : (g + 1) * LANES]


def enter_kernel(
    sources, rows, recv_ref, gate_ref, up_ref, down_ref, after_ref, input_ref, grad_ref, send_ref
):
    pieces = input_ref.shape[1] // LANES
    block = min(sources, 32)
    shape = (block * CAP, block * rows)
    out_row, in_row = iota(shape, 0), iota(shape, 1)
    offset = in_row - div(out_row, CAP) * rows - mod(out_row, CAP) * pieces
    picks = [
        [(offset == a * CAP * pieces + l).astype(BF16) for l in range(pieces)]
        for a in range(2)
    ]
    for b in range(sources // block):
        arrived = recv_ref[b * block * rows : (b + 1) * block * rows, :]
        here = slice(b * block * CAP, (b + 1) * block * CAP)
        inputs, grads = (
            jnp.concatenate([dot(pick, arrived) for pick in picks[a]], axis=1).astype(BF16)
            for a in range(2)
        )
        input_ref[here, :] = inputs
        grad_ref[here, :] = grads
        partial = jnp.concatenate(
            [dot(inputs, gate_ref[0]), dot(inputs, up_ref[0]), dot(grads, down_ref[0], 1, 1)],
            axis=1,
        )
        send_ref[here, :] = partial.astype(BF16)


def middle_kernel(sources, rows, *refs):
    parts = refs[:-7]
    gate_ref, up_ref, _, back_ref, hidden_ref, gate_rows_ref, up_rows_ref = refs[-7:]
    share = gate_ref.shape[1]
    pieces = share // LANES
    hid = gate_ref.shape[2]
    block = min(sources, 32)
    shape = (block * rows, block * CAP)
    out_row, in_row = iota(shape, 0), iota(shape, 1)
    same = div(out_row, rows) == div(in_row, CAP)
    inner, which = mod(out_row, rows), mod(in_row, CAP)
    offset = jnp.where(same, inner - which * pieces, -1)
    picks = [(offset == l).astype(BF16) for l in range(pieces)]
    pick_dot = (same & (inner == CAP * pieces + which)).astype(BF16)
    for b in range(sources // block):
        here = slice(b * block * CAP, (b + 1) * block * CAP)
        terms = [part[here, :].astype(F32) for part in parts]
        total = functools.reduce(jnp.add, terms)
        gate_pre, up_pre, hidden_grad = total[:, :hid], total[:, hid : 2 * hid], total[:, 2 * hid :]
        sig = jax.nn.sigmoid(gate_pre)
        silu = gate_pre * sig
        hidden = (silu * up_pre).astype(BF16)
        slope = sig * (1.0 + gate_pre * (1.0 - sig))
        gate_rows = (hidden_grad * up_pre * slope).astype(BF16)
        up_rows = (hidden_grad * silu).astype(BF16)
        hidden_ref[here, :] = hidden
        gate_rows_ref[here, :] = gate_rows
        up_rows_ref[here, :] = up_rows
        routed = jnp.sum(hidden.astype(F32) * hidden_grad, axis=1, keepdims=True)
        high = routed.astype(BF16)
        low = (routed - high.astype(F32)).astype(BF16)
        lane = iota((block * CAP, LANES), 1)
        routed_wide = jnp.where(lane < LANES // 2, high.astype(F32), low.astype(F32)).astype(BF16)
        input_rows = (
            dot(gate_rows, gate_ref[0], 1, 1) + dot(up_rows, up_ref[0], 1, 1)
        ).astype(BF16)
        back = dot(pick_dot, routed_wide)
        for l in range(pieces):
            back = back + dot(picks[l], input_rows[:, l * LANES : (l + 1) * LANES])
        back_ref[b * block * rows : (b + 1) * block * rows, :] = back.astype(BF16)


def weight_kernel(
    input_ref, grad_ref, hidden_ref, gate_rows_ref, up_rows_ref, gate_out, up_out, down_out
):
    gate_out[0] = dot(input_ref[...], gate_rows_ref[...], 0, 0)
    up_out[0] = dot(input_ref[...], up_rows_ref[...], 0, 0)
    down_out[0] = dot(hidden_ref[...], grad_ref[...], 0, 0)


def combine_kernel(
    experts,
    groups,
    rows,
    back_ref,
    routes_ref,
    weights_ref,
    after_ref,
    input_grad_ref,
    route_grad_ref,
):
    slot, weight, live = slots(routes_ref, weights_ref, experts)
    tokens, width = input_grad_ref.shape
    share = width // groups
    pieces = share // LANES
    total = experts * rows
    shape = (total, tokens)
    row = iota(shape, 0)
    inner = mod(row, rows)
    expert = div(row, rows)
    hit = (slot == expert * CAP + div(inner, pieces)) & (inner < CAP * pieces)
    hit = jnp.where(hit, mod(inner, pieces), -1)
    wide = jnp.concatenate([back_ref[g * total : (g + 1) * total, :] for g in range(groups)], axis=1)
    for l in range(pieces):
        pick = (hit == l).astype(BF16)
        grad = dot(pick, wide, 0, 0).astype(BF16)
        for g in range(groups):
            input_grad_ref[:, g * share + l * LANES : g * share + (l + 1) * LANES] = grad[
                :, g * LANES : (g + 1) * LANES
            ]
    hit_dot = slot == expert * CAP + inner - CAP * pieces
    hit_dot = hit_dot & (inner >= CAP * pieces) & (inner < CAP * (pieces + 1))
    routed = dot(back_ref[:total, :], hit_dot.astype(BF16), 0, 0)
    routed = routed[:1] + routed[LANES // 2 : LANES // 2 + 1]
    routed = routed / jnp.where(weight > 0.0, weight, 1.0)
    route_grad_ref[...] = jnp.where(live, routed, 0.0).astype(BF16)


def shards(
    query_rows,
    key_rows,
    value_rows,
    gate_logits,
    gated_grad,
    moe_input,
    out_grad,
    routes,
    route_weights,
    gate_proj,
    up_proj,
    down_proj,
):
    devices = lax.axis_size("expert")
    groups = lax.axis_size("dp")
    sources = devices * groups
    chips = devices // 2
    seqs, length, _ = key_rows.shape
    tokens, width = moe_input.shape
    share = width // groups
    pieces = share // LANES
    hid = gate_proj.shape[2]
    rows = -(-2 * CAP * pieces // 16) * 16
    axes = ("dp", "expert")
    swap = [(i, i ^ 1) for i in range(devices)]
    same_core = [list(range(c, devices, 2)) for c in range(2)]

    packed = pl.pallas_call(
        pack_kernel,
        in_specs=[IN_HBM] * 2,
        out_shape=jax.ShapeDtypeStruct((seqs, length, 2 * HEAD), BF16),
        scratch_shapes=[pltpu.VMEM(key_rows.shape, BF16)] * 2 + [pltpu.SemaphoreType.DMA((2,))],
        compiler_params=params(60),
        cost_estimate=cost(MIB, MIB),
        name="pack",
    )(key_rows, value_rows)
    mine = [packed]
    for d in range(1, chips):
        up = [(i, i + 2 * d) for i in range(devices - 2 * d)]
        mine.append(lax.ppermute(packed, "expert", up))
    other = [lax.ppermute(block, "expert", swap) for block in mine]

    routes_t, weights_t = routes.T, route_weights.T
    send = pl.pallas_call(
        functools.partial(dispatch_kernel, devices, groups, rows),
        in_specs=[IN_VMEM] * 4 + [ANYWHERE],
        out_shape=jax.ShapeDtypeStruct((sources * rows, LANES), BF16),
        compiler_params=params(16),
        cost_estimate=cost(2e9, 2 * MIB),
        name="dispatch",
    )(moe_input, out_grad, routes_t, weights_t, packed)
    recv = lax.all_to_all(
        send.reshape(sources, rows, LANES), axes, split_axis=0, concat_axis=0, tiled=True
    ).reshape(sources * rows, LANES)

    query_grad, gate_grad, other_part, mine_part = attention(
        query_rows, gate_logits, gated_grad, mine + other, recv
    )
    slot_rows = jax.ShapeDtypeStruct((sources * CAP, share), BF16)
    hid_rows = jax.ShapeDtypeStruct((sources * CAP, hid), BF16)
    inputs, grads, sent = pl.pallas_call(
        functools.partial(enter_kernel, sources, rows),
        in_specs=[IN_VMEM] * 4 + [ANYWHERE],
        out_shape=[slot_rows, slot_rows, jax.ShapeDtypeStruct((sources * CAP, 3 * hid), BF16)],
        compiler_params=params(16),
        cost_estimate=cost(2e9, 2 * MIB),
        name="enter",
    )(recv, gate_proj, up_proj, down_proj, other_part)
    parts = [sent] + [
        lax.ppermute(sent, "dp", [(g, g ^ k) for g in range(groups)]) for k in range(1, groups)
    ]

    arrived = lax.ppermute(other_part, "expert", swap)
    merged = pl.pallas_call(
        functools.partial(merge_kernel, chips),
        out_shape=[jax.ShapeDtypeStruct(packed.shape, BF16)] * chips,
        compiler_params=params(16),
        cost_estimate=cost(MIB, 2 * MIB),
        name="merge",
    )(*mine_part, arrived)
    terms = [merged[0]]
    for d in range(1, chips):
        down = [(i, i - 2 * d) for i in range(2 * d, devices)]
        terms.append(lax.ppermute(merged[d], "expert", down))
    back, hidden, gate_rows, up_rows = pl.pallas_call(
        functools.partial(middle_kernel, sources, rows),
        in_specs=[IN_VMEM] * (len(parts) + 2) + [ANYWHERE],
        out_shape=[jax.ShapeDtypeStruct((sources * rows, LANES), BF16)] + [hid_rows] * 3,
        compiler_params=params(16 if groups <= 4 else 60),
        cost_estimate=cost(2e9, 2 * MIB),
        name="middle",
    )(*parts, gate_proj, up_proj, terms[min(1, chips - 1)])
    returned = lax.all_to_all(
        back.reshape(sources, rows, LANES), axes, split_axis=0, concat_axis=0, tiled=True
    ).reshape(sources * rows, LANES)
    gate_proj_grad, up_proj_grad, down_proj_grad = pl.pallas_call(
        weight_kernel,
        out_shape=[
            jax.ShapeDtypeStruct(gate_proj.shape, F32),
            jax.ShapeDtypeStruct(up_proj.shape, F32),
            jax.ShapeDtypeStruct(down_proj.shape, F32),
        ],
        compiler_params=params(16),
        cost_estimate=cost(2e9, 2 * MIB),
        name="weight_grads",
    )(inputs, grads, hidden, gate_rows, up_rows)
    key_grad, value_grad = pl.pallas_call(
        close_kernel,
        in_specs=[IN_VMEM] * chips,
        out_shape=[jax.ShapeDtypeStruct((seqs, length, HEAD), BF16)] * 2,
        compiler_params=params(16),
        cost_estimate=cost(6e10, MIB),
        name="close",
    )(*terms)
    input_grad, route_grad = pl.pallas_call(
        functools.partial(combine_kernel, devices, groups, rows),
        in_specs=[IN_VMEM] * 3 + [ANYWHERE],
        out_shape=[
            jax.ShapeDtypeStruct(moe_input.shape, BF16),
            jax.ShapeDtypeStruct(routes_t.shape, BF16),
        ],
        compiler_params=params(16),
        cost_estimate=cost(2e9, 2 * MIB),
        name="combine",
    )(returned, routes_t, weights_t, key_grad)

    return (
        query_grad,
        key_grad,
        value_grad,
        gate_grad,
        input_grad,
        route_grad.T,
        gate_proj_grad,
        up_proj_grad,
        down_proj_grad,
    )


def solution(mesh):
    rows3 = P("dp", "expert", None)
    tokens2 = P(("dp", "expert"), None)
    weights = P("expert", "dp", None)
    weights_down = P("expert", None, "dp")
    return jax.shard_map(
        shards,
        mesh=mesh,
        in_specs=(rows3,) * 5 + (tokens2,) * 4 + (weights, weights, weights_down),
        out_specs=(rows3,) * 4 + (tokens2,) * 2 + (weights, weights, weights_down),
        check_vma=False,
    )
```

```python
import functools

import jax
import jax.numpy as jnp
from jax import lax
from jax.experimental import pallas as pl
from jax.experimental.pallas import tpu as pltpu
from jax.sharding import PartitionSpec as P

HEADS = 8
HEAD = 256
CAP = 2
LANES = 128
BF16 = jnp.bfloat16
F32 = jnp.float32
MIB = 1 << 20
ATTENTION_MIB = 32
IN_HBM = pl.BlockSpec(memory_space=pltpu.HBM)
IN_VMEM = pl.BlockSpec(memory_space=pltpu.VMEM)
ANYWHERE = pl.BlockSpec(memory_space=pl.ANY)


def dot(a, b, ca=1, cb=0):
    return lax.dot_general(a, b, (((ca,), (cb,)), ((), ())), preferred_element_type=F32)


def div(x, size):
    assert size & (size - 1) == 0
    return x >> (size.bit_length() - 1)


def mod(x, size):
    assert size & (size - 1) == 0
    return x & (size - 1)


def iota(shape, dim):
    return lax.broadcasted_iota(jnp.int32, shape, dim)


def params(mib):
    return pltpu.CompilerParams(vmem_limit_bytes=mib * MIB)


def cost(flops, bytes_accessed):
    return pl.CostEstimate(flops=int(flops), bytes_accessed=int(bytes_accessed), transcendentals=0)


def pack_kernel(key_hbm, value_hbm, out_ref, key_ref, value_ref, sems):
    copies = [
        pltpu.make_async_copy(src, dst, sems.at[i])
        for i, (src, dst) in enumerate(((key_hbm, key_ref), (value_hbm, value_ref)))
    ]
    for copy in copies:
        copy.start()
    copies[0].wait()
    out_ref[:, :, :HEAD] = key_ref[...]
    copies[1].wait()
    out_ref[:, :, HEAD:] = value_ref[...]


def attention_kernel(chips, *refs):
    q_ref, logit_ref, grad_ref = refs[:3]
    kv_refs = refs[3 : 3 + 2 * chips]
    query_grad_hbm, gate_grad_hbm, other_ref = refs[3 + 2 * chips : 6 + 2 * chips]
    mine_refs = refs[6 + 2 * chips : 6 + 3 * chips]
    query_grad_ref, gate_grad_ref, out_sems = refs[6 + 3 * chips :]
    seqs, length, _ = q_ref.shape
    side = chips * length
    scale = HEAD ** (-0.5)
    position = lax.axis_index("expert")
    chip, core = position >> 1, position & 1

    shape = (1, 2 * side)
    col = iota(shape, 1)
    half, back, inner = div(col, side), div(mod(col, side), length), mod(col, length)
    block = 2 * (chip - back) + jnp.where(half == 0, core, 1 - core)
    key_pos = jnp.where(back <= chip, block * length + inner, 2 * side)
    query_pos = position * length + mod(iota((HEADS * length, 1), 0), length)

    def stacked(ref, s):
        return jnp.concatenate(
            [ref[s, :, h * HEAD : (h + 1) * HEAD] for h in range(HEADS)], axis=0
        )

    stores = []
    for s in range(seqs):
        both = jnp.concatenate([ref[s] for ref in kv_refs], axis=0)
        keys, values = both[:, :HEAD], both[:, HEAD:]
        queries = stacked(q_ref, s)
        scores = jnp.where(key_pos <= query_pos, dot(queries, keys, 1, 1), -jnp.inf)
        row_max = jnp.max(scores, axis=1, keepdims=True)
        unnormed = jnp.exp((scores - row_max) * scale)
        probs = unnormed * (1.0 / jnp.sum(unnormed, axis=1, keepdims=True))
        probs_low = probs.astype(BF16)
        context = dot(probs_low, values)
        gate = jax.nn.sigmoid(stacked(logit_ref, s).astype(F32))
        upstream = stacked(grad_ref, s).astype(F32)
        context_grad = (upstream * gate).astype(BF16)
        gate_grad = (upstream * context * gate * (1.0 - gate)).astype(BF16)
        for h in range(HEADS):
            gate_grad_ref[s, :, h * HEAD : (h + 1) * HEAD] = gate_grad[h * length : (h + 1) * length]
        stores.append(pltpu.make_async_copy(gate_grad_ref.at[s], gate_grad_hbm.at[s], out_sems.at[s, 0]))
        stores[-1].start()
        grad_dot = jnp.sum(context_grad.astype(F32) * context, axis=1, keepdims=True)
        prob_grad = dot(context_grad, values, 1, 1)
        score_grad = (probs * (prob_grad - grad_dot)).astype(BF16)
        query_grad = (dot(score_grad, keys) * scale).astype(BF16)
        for h in range(HEADS):
            query_grad_ref[s, :, h * HEAD : (h + 1) * HEAD] = query_grad[h * length : (h + 1) * length]
        stores.append(pltpu.make_async_copy(query_grad_ref.at[s], query_grad_hbm.at[s], out_sems.at[s, 1]))
        stores[-1].start()
        key_part = (dot(score_grad, queries, 0, 0) * scale).astype(BF16)
        value_part = dot(probs_low, context_grad, 0, 0).astype(BF16)
        for d in range(chips):
            start = d * length
            mine_refs[d][s, :, :HEAD] = key_part[start : start + length]
            mine_refs[d][s, :, HEAD:] = value_part[start : start + length]
            start = side + d * length
            other_ref[d, s, :, :HEAD] = key_part[start : start + length]
            other_ref[d, s, :, HEAD:] = value_part[start : start + length]
    for store in stores:
        store.wait()


def attention(query_rows, gate_logits, gated_grad, pieces):
    seqs, length, width = query_rows.shape
    chips = len(pieces) // 2
    full = jax.ShapeDtypeStruct((seqs, length, width), BF16)
    part = jax.ShapeDtypeStruct(pieces[0].shape, BF16)
    out = pl.pallas_call(
        functools.partial(attention_kernel, chips),
        in_specs=[IN_VMEM] * (3 + 2 * chips),
        out_specs=[IN_HBM] * 2 + [IN_VMEM] * (1 + chips),
        out_shape=[full] * 2 + [jax.ShapeDtypeStruct((chips,) + part.shape, BF16)] + [part] * chips,
        scratch_shapes=[pltpu.VMEM(query_rows.shape, BF16)] * 2
        + [pltpu.SemaphoreType.DMA((seqs, 2))],
        compiler_params=params(ATTENTION_MIB if chips <= 4 else 56),
        cost_estimate=cost(MIB, 8),
        name="attention",
    )(query_rows, gate_logits, gated_grad, *pieces)
    return out[0], out[1], out[2], out[3:]


def gate_kernel(held_ref, after_ref, out_ref):
    pass


def gate(array, after):
    return pl.pallas_call(
        gate_kernel,
        in_specs=[ANYWHERE] * 2,
        out_specs=ANYWHERE,
        out_shape=jax.ShapeDtypeStruct(array.shape, array.dtype),
        input_output_aliases={0: 0},
        compiler_params=params(16),
        cost_estimate=cost(4e9, 8),
        name="gate",
    )(array, after)


def merge_kernel(chips, *refs):
    mine, arrived, outs = refs[:chips], refs[chips], refs[chips + 1 :]
    for d in range(chips):
        outs[d][...] = (mine[d][...].astype(F32) + arrived[d].astype(F32)).astype(BF16)


def close_kernel(*refs):
    parts, (key_ref, value_ref) = refs[:-2], refs[-2:]
    total = parts[0][...].astype(F32)
    for part in parts[1:]:
        total = total + part[...].astype(F32)
    key_ref[...] = total[:, :, :HEAD].astype(BF16)
    value_ref[...] = total[:, :, HEAD:].astype(BF16)


def slots(routes_ref, weights_ref, experts):
    routes = routes_ref[...]
    tokens = routes.shape[1]
    live = routes < experts
    expert = jnp.sum(jnp.where(live, routes, 0), axis=0, keepdims=True)
    has_live = jnp.sum(live.astype(jnp.int32), axis=0, keepdims=True) > 0
    weight = jnp.sum(
        jnp.where(live, weights_ref[...].astype(F32), 0.0), axis=0, keepdims=True
    )
    tall = max(experts, 16)
    member = (iota((tall, tokens), 0) == expert) & has_live
    earlier = (iota((tokens, tokens), 0) < iota((tokens, tokens), 1)).astype(BF16)
    before = dot(member.astype(BF16), earlier)
    rank = jnp.sum(jnp.where(member, before, 0.0), axis=0, keepdims=True).astype(jnp.int32)
    return jnp.where(has_live, expert * CAP + rank, -1), weight, live


def dispatch_kernel(
    experts, groups, rows, input_ref, grad_ref, routes_ref, weights_ref, after_ref, out_ref
):
    tokens, width = input_ref.shape
    slot, weight, _ = slots(routes_ref, weights_ref, experts)
    share = width // groups
    pieces = share // LANES
    total = experts * rows
    shape = (total, tokens)
    row = iota(shape, 0)
    inner = mod(row, rows)
    hit = slot == div(row, rows) * CAP + mod(div(inner, pieces), CAP)
    hit = jnp.where(hit, mod(inner, pieces) + pieces * div(inner, CAP * pieces), -1)
    acc = None
    for a, (ref, value) in enumerate(((input_ref, 1.0), (grad_ref, weight))):
        for l in range(pieces):
            pick = hit == a * pieces + l
            source = jnp.concatenate(
                [
                    ref[:, g * share + l * LANES : g * share + (l + 1) * LANES]
                    for g in range(groups)
                ],
                axis=1,
            )
            term = dot(jnp.where(pick, value, 0.0).astype(BF16), source)
            acc = term if acc is None else acc + term
    acc = acc.astype(BF16)
    for g in range(groups):
        out_ref[g * total : (g + 1) * total, :] = acc[:, g * LANES : (g + 1) * LANES]


def enter_kernel(
    sources, rows, recv_ref, gate_ref, up_ref, down_ref, after_ref, input_ref, grad_ref, send_ref
):
    pieces = input_ref.shape[1] // LANES
    block = min(sources, 32)
    shape = (block * CAP, block * rows)
    out_row, in_row = iota(shape, 0), iota(shape, 1)
    offset = in_row - div(out_row, CAP) * rows - mod(out_row, CAP) * pieces
    picks = [
        [(offset == a * CAP * pieces + l).astype(BF16) for l in range(pieces)]
        for a in range(2)
    ]
    for b in range(sources // block):
        arrived = recv_ref[b * block * rows : (b + 1) * block * rows, :]
        here = slice(b * block * CAP, (b + 1) * block * CAP)
        inputs, grads = (
            jnp.concatenate([dot(pick, arrived) for pick in picks[a]], axis=1).astype(BF16)
            for a in range(2)
        )
        input_ref[here, :] = inputs
        grad_ref[here, :] = grads
        partial = jnp.concatenate(
            [dot(inputs, gate_ref[0]), dot(inputs, up_ref[0]), dot(grads, down_ref[0], 1, 1)],
            axis=1,
        )
        send_ref[here, :] = partial.astype(BF16)


def middle_kernel(sources, rows, *refs):
    parts = refs[:-7]
    gate_ref, up_ref, _, back_ref, hidden_ref, gate_rows_ref, up_rows_ref = refs[-7:]
    share = gate_ref.shape[1]
    pieces = share // LANES
    hid = gate_ref.shape[2]
    block = min(sources, 32)
    shape = (block * rows, block * CAP)
    out_row, in_row = iota(shape, 0), iota(shape, 1)
    same = div(out_row, rows) == div(in_row, CAP)
    inner, which = mod(out_row, rows), mod(in_row, CAP)
    offset = jnp.where(same, inner - which * pieces, -1)
    picks = [(offset == l).astype(BF16) for l in range(pieces)]
    pick_dot = (same & (inner == CAP * pieces + which)).astype(BF16)
    for b in range(sources // block):
        here = slice(b * block * CAP, (b + 1) * block * CAP)
        terms = [part[here, :].astype(F32) for part in parts]
        total = functools.reduce(jnp.add, terms)
        gate_pre, up_pre, hidden_grad = total[:, :hid], total[:, hid : 2 * hid], total[:, 2 * hid :]
        sig = jax.nn.sigmoid(gate_pre)
        silu = gate_pre * sig
        hidden = (silu * up_pre).astype(BF16)
        slope = sig * (1.0 + gate_pre * (1.0 - sig))
        gate_rows = (hidden_grad * up_pre * slope).astype(BF16)
        up_rows = (hidden_grad * silu).astype(BF16)
        hidden_ref[here, :] = hidden
        gate_rows_ref[here, :] = gate_rows
        up_rows_ref[here, :] = up_rows
        routed = jnp.sum(hidden.astype(F32) * hidden_grad, axis=1, keepdims=True)
        high = routed.astype(BF16)
        low = (routed - high.astype(F32)).astype(BF16)
        lane = iota((block * CAP, LANES), 1)
        routed_wide = jnp.where(lane < LANES // 2, high.astype(F32), low.astype(F32)).astype(BF16)
        input_rows = (
            dot(gate_rows, gate_ref[0], 1, 1) + dot(up_rows, up_ref[0], 1, 1)
        ).astype(BF16)
        back = dot(pick_dot, routed_wide)
        for l in range(pieces):
            back = back + dot(picks[l], input_rows[:, l * LANES : (l + 1) * LANES])
        back_ref[b * block * rows : (b + 1) * block * rows, :] = back.astype(BF16)


def weight_kernel(
    input_ref, grad_ref, hidden_ref, gate_rows_ref, up_rows_ref, gate_out, up_out, down_out
):
    gate_out[0] = dot(input_ref[...], gate_rows_ref[...], 0, 0)
    up_out[0] = dot(input_ref[...], up_rows_ref[...], 0, 0)
    down_out[0] = dot(hidden_ref[...], grad_ref[...], 0, 0)


def combine_kernel(
    experts,
    groups,
    rows,
    back_ref,
    routes_ref,
    weights_ref,
    after_ref,
    input_grad_ref,
    route_grad_ref,
):
    slot, weight, live = slots(routes_ref, weights_ref, experts)
    tokens, width = input_grad_ref.shape
    share = width // groups
    pieces = share // LANES
    total = experts * rows
    shape = (total, tokens)
    row = iota(shape, 0)
    inner = mod(row, rows)
    expert = div(row, rows)
    hit = (slot == expert * CAP + div(inner, pieces)) & (inner < CAP * pieces)
    hit = jnp.where(hit, mod(inner, pieces), -1)
    wide = jnp.concatenate([back_ref[g * total : (g + 1) * total, :] for g in range(groups)], axis=1)
    for l in range(pieces):
        pick = (hit == l).astype(BF16)
        grad = dot(pick, wide, 0, 0).astype(BF16)
        for g in range(groups):
            input_grad_ref[:, g * share + l * LANES : g * share + (l + 1) * LANES] = grad[
                :, g * LANES : (g + 1) * LANES
            ]
    hit_dot = slot == expert * CAP + inner - CAP * pieces
    hit_dot = hit_dot & (inner >= CAP * pieces) & (inner < CAP * (pieces + 1))
    routed = dot(back_ref[:total, :], hit_dot.astype(BF16), 0, 0)
    routed = routed[:1] + routed[LANES // 2 : LANES // 2 + 1]
    routed = routed / jnp.where(weight > 0.0, weight, 1.0)
    route_grad_ref[...] = jnp.where(live, routed, 0.0).astype(BF16)


def shards(
    query_rows,
    key_rows,
    value_rows,
    gate_logits,
    gated_grad,
    moe_input,
    out_grad,
    routes,
    route_weights,
    gate_proj,
    up_proj,
    down_proj,
):
    devices = lax.axis_size("expert")
    groups = lax.axis_size("dp")
    sources = devices * groups
    chips = devices // 2
    seqs, length, _ = key_rows.shape
    tokens, width = moe_input.shape
    share = width // groups
    pieces = share // LANES
    hid = gate_proj.shape[2]
    rows = -(-2 * CAP * pieces // 16) * 16
    axes = ("dp", "expert")
    swap = [(i, i ^ 1) for i in range(devices)]
    same_core = [list(range(c, devices, 2)) for c in range(2)]

    packed = pl.pallas_call(
        pack_kernel,
        in_specs=[IN_HBM] * 2,
        out_shape=jax.ShapeDtypeStruct((seqs, length, 2 * HEAD), BF16),
        scratch_shapes=[pltpu.VMEM(key_rows.shape, BF16)] * 2 + [pltpu.SemaphoreType.DMA((2,))],
        compiler_params=params(16),
        cost_estimate=cost(6e10, MIB),
        name="pack",
    )(key_rows, value_rows)
    mine = [packed]
    for d in range(1, chips):
        up = [(i, i + 2 * d) for i in range(devices - 2 * d)]
        mine.append(lax.ppermute(packed, "expert", up))
    other = [lax.ppermute(block, "expert", swap) for block in mine]

    routes_t, weights_t = routes.T, route_weights.T
    send = pl.pallas_call(
        functools.partial(dispatch_kernel, devices, groups, rows),
        in_specs=[IN_VMEM] * 4 + [ANYWHERE],
        out_shape=jax.ShapeDtypeStruct((sources * rows, LANES), BF16),
        compiler_params=params(16),
        cost_estimate=cost(2e9, 2 * MIB),
        name="dispatch",
    )(moe_input, out_grad, routes_t, weights_t, packed)
    recv = lax.all_to_all(
        send.reshape(sources, rows, LANES), axes, split_axis=0, concat_axis=0, tiled=True
    ).reshape(sources * rows, LANES)

    query_grad, gate_grad, other_part, mine_part = attention(
        query_rows, gate_logits, gated_grad, mine + other
    )
    other_part = gate(other_part, recv)
    slot_rows = jax.ShapeDtypeStruct((sources * CAP, share), BF16)
    hid_rows = jax.ShapeDtypeStruct((sources * CAP, hid), BF16)
    inputs, grads, sent = pl.pallas_call(
        functools.partial(enter_kernel, sources, rows),
        in_specs=[IN_VMEM] * 4 + [ANYWHERE],
        out_shape=[slot_rows, slot_rows, jax.ShapeDtypeStruct((sources * CAP, 3 * hid), BF16)],
        compiler_params=params(16),
        cost_estimate=cost(2e9, 2 * MIB),
        name="enter",
    )(recv, gate_proj, up_proj, down_proj, other_part)
    parts = [sent] + [
        lax.ppermute(sent, "dp", [(g, g ^ k) for g in range(groups)]) for k in range(1, groups)
    ]

    arrived = lax.ppermute(other_part, "expert", swap)
    merged = pl.pallas_call(
        functools.partial(merge_kernel, chips),
        out_shape=[jax.ShapeDtypeStruct(packed.shape, BF16)] * chips,
        compiler_params=params(16),
        cost_estimate=cost(MIB, 2 * MIB),
        name="merge",
    )(*mine_part, arrived)
    terms = [merged[0]]
    for d in range(1, chips):
        down = [(i, i - 2 * d) for i in range(2 * d, devices)]
        terms.append(lax.ppermute(merged[d], "expert", down))
    back, hidden, gate_rows, up_rows = pl.pallas_call(
        functools.partial(middle_kernel, sources, rows),
        in_specs=[IN_VMEM] * (len(parts) + 2) + [ANYWHERE],
        out_shape=[jax.ShapeDtypeStruct((sources * rows, LANES), BF16)] + [hid_rows] * 3,
        compiler_params=params(16 if groups <= 4 else 60),
        cost_estimate=cost(2e9, 2 * MIB),
        name="middle",
    )(*parts, gate_proj, up_proj, terms[min(1, chips - 1)])
    returned = lax.all_to_all(
        back.reshape(sources, rows, LANES), axes, split_axis=0, concat_axis=0, tiled=True
    ).reshape(sources * rows, LANES)
    gate_proj_grad, up_proj_grad, down_proj_grad = pl.pallas_call(
        weight_kernel,
        out_shape=[
            jax.ShapeDtypeStruct(gate_proj.shape, F32),
            jax.ShapeDtypeStruct(up_proj.shape, F32),
            jax.ShapeDtypeStruct(down_proj.shape, F32),
        ],
        compiler_params=params(16),
        cost_estimate=cost(2e9, 2 * MIB),
        name="weight_grads",
    )(inputs, grads, hidden, gate_rows, up_rows)
    key_grad, value_grad = pl.pallas_call(
        close_kernel,
        in_specs=[IN_VMEM] * chips,
        out_shape=[jax.ShapeDtypeStruct((seqs, length, HEAD), BF16)] * 2,
        compiler_params=params(16),
        cost_estimate=cost(6e10, MIB),
        name="close",
    )(*terms)
    input_grad, route_grad = pl.pallas_call(
        functools.partial(combine_kernel, devices, groups, rows),
        in_specs=[IN_VMEM] * 3 + [ANYWHERE],
        out_shape=[
            jax.ShapeDtypeStruct(moe_input.shape, BF16),
            jax.ShapeDtypeStruct(routes_t.shape, BF16),
        ],
        compiler_params=params(16),
        cost_estimate=cost(2e9, 2 * MIB),
        name="combine",
    )(returned, routes_t, weights_t, key_grad)

    return (
        query_grad,
        key_grad,
        value_grad,
        gate_grad,
        input_grad,
        route_grad.T,
        gate_proj_grad,
        up_proj_grad,
        down_proj_grad,
    )


def solution(mesh):
    rows3 = P("dp", "expert", None)
    tokens2 = P(("dp", "expert"), None)
    weights = P("expert", "dp", None)
    weights_down = P("expert", None, "dp")
    return jax.shard_map(
        shards,
        mesh=mesh,
        in_specs=(rows3,) * 5 + (tokens2,) * 4 + (weights, weights, weights_down),
        out_specs=(rows3,) * 4 + (tokens2,) * 2 + (weights, weights, weights_down),
        check_vma=False,
    )
```

```python
import functools

import jax
import jax.numpy as jnp
from jax import lax
from jax.experimental import pallas as pl
from jax.experimental.pallas import tpu as pltpu
from jax.sharding import PartitionSpec as P

HEADS = 8
HEAD = 256
CAP = 2
LANES = 128
BF16 = jnp.bfloat16
F32 = jnp.float32
MIB = 1 << 20
ATTENTION_MIB = 32
IN_HBM = pl.BlockSpec(memory_space=pltpu.HBM)
IN_VMEM = pl.BlockSpec(memory_space=pltpu.VMEM)
ANYWHERE = pl.BlockSpec(memory_space=pl.ANY)


def dot(a, b, ca=1, cb=0):
    return lax.dot_general(a, b, (((ca,), (cb,)), ((), ())), preferred_element_type=F32)


def div(x, size):
    assert size & (size - 1) == 0
    return x >> (size.bit_length() - 1)


def mod(x, size):
    assert size & (size - 1) == 0
    return x & (size - 1)


def iota(shape, dim):
    return lax.broadcasted_iota(jnp.int32, shape, dim)


def params(mib):
    return pltpu.CompilerParams(vmem_limit_bytes=mib * MIB)


def cost(flops, bytes_accessed):
    return pl.CostEstimate(flops=int(flops), bytes_accessed=int(bytes_accessed), transcendentals=0)


def pack_kernel(key_hbm, value_hbm, out_ref, key_ref, value_ref, sems):
    copies = [
        pltpu.make_async_copy(src, dst, sems.at[i])
        for i, (src, dst) in enumerate(((key_hbm, key_ref), (value_hbm, value_ref)))
    ]
    for copy in copies:
        copy.start()
    copies[0].wait()
    out_ref[:, :, :HEAD] = key_ref[...]
    copies[1].wait()
    out_ref[:, :, HEAD:] = value_ref[...]


def attention_kernel(chips, *refs):
    q_ref, logit_ref, grad_ref = refs[:3]
    kv_refs = refs[3 : 3 + 2 * chips]
    query_grad_hbm, gate_grad_hbm, other_ref = refs[4 + 2 * chips : 7 + 2 * chips]
    mine_refs = refs[7 + 2 * chips : 7 + 3 * chips]
    query_grad_ref, gate_grad_ref, out_sems = refs[7 + 3 * chips :]
    seqs, length, _ = q_ref.shape
    side = chips * length
    scale = HEAD ** (-0.5)
    position = lax.axis_index("expert")
    chip, core = position >> 1, position & 1

    shape = (1, 2 * side)
    col = iota(shape, 1)
    half, back, inner = div(col, side), div(mod(col, side), length), mod(col, length)
    block = 2 * (chip - back) + jnp.where(half == 0, core, 1 - core)
    key_pos = jnp.where(back <= chip, block * length + inner, 2 * side)
    query_pos = position * length + mod(iota((HEADS * length, 1), 0), length)

    def stacked(ref, s):
        return jnp.concatenate(
            [ref[s, :, h * HEAD : (h + 1) * HEAD] for h in range(HEADS)], axis=0
        )

    stores = []
    for s in range(seqs):
        both = jnp.concatenate([ref[s] for ref in kv_refs], axis=0)
        keys, values = both[:, :HEAD], both[:, HEAD:]
        queries = stacked(q_ref, s)
        scores = jnp.where(key_pos <= query_pos, dot(queries, keys, 1, 1), -jnp.inf)
        row_max = jnp.max(scores, axis=1, keepdims=True)
        unnormed = jnp.exp((scores - row_max) * scale)
        probs = unnormed * (1.0 / jnp.sum(unnormed, axis=1, keepdims=True))
        probs_low = probs.astype(BF16)
        context = dot(probs_low, values)
        gate = jax.nn.sigmoid(stacked(logit_ref, s).astype(F32))
        upstream = stacked(grad_ref, s).astype(F32)
        context_grad = (upstream * gate).astype(BF16)
        gate_grad = (upstream * context * gate * (1.0 - gate)).astype(BF16)
        for h in range(HEADS):
            gate_grad_ref[s, :, h * HEAD : (h + 1) * HEAD] = gate_grad[h * length : (h + 1) * length]
        stores.append(pltpu.make_async_copy(gate_grad_ref.at[s], gate_grad_hbm.at[s], out_sems.at[s, 0]))
        stores[-1].start()
        grad_dot = jnp.sum(context_grad.astype(F32) * context, axis=1, keepdims=True)
        prob_grad = dot(context_grad, values, 1, 1)
        score_grad = (probs * (prob_grad - grad_dot)).astype(BF16)
        query_grad = (dot(score_grad, keys) * scale).astype(BF16)
        for h in range(HEADS):
            query_grad_ref[s, :, h * HEAD : (h + 1) * HEAD] = query_grad[h * length : (h + 1) * length]
        stores.append(pltpu.make_async_copy(query_grad_ref.at[s], query_grad_hbm.at[s], out_sems.at[s, 1]))
        stores[-1].start()
        key_part = (dot(score_grad, queries, 0, 0) * scale).astype(BF16)
        value_part = dot(probs_low, context_grad, 0, 0).astype(BF16)
        for d in range(chips):
            start = d * length
            mine_refs[d][s, :, :HEAD] = key_part[start : start + length]
            mine_refs[d][s, :, HEAD:] = value_part[start : start + length]
            start = side + d * length
            other_ref[d, s, :, :HEAD] = key_part[start : start + length]
            other_ref[d, s, :, HEAD:] = value_part[start : start + length]
    for store in stores:
        store.wait()


def attention(query_rows, gate_logits, gated_grad, pieces, after):
    seqs, length, width = query_rows.shape
    chips = len(pieces) // 2
    full = jax.ShapeDtypeStruct((seqs, length, width), BF16)
    part = jax.ShapeDtypeStruct(pieces[0].shape, BF16)
    out = pl.pallas_call(
        functools.partial(attention_kernel, chips),
        in_specs=[IN_VMEM] * (3 + 2 * chips) + [ANYWHERE],
        out_specs=[IN_HBM] * 2 + [IN_VMEM] * (1 + chips),
        out_shape=[full] * 2 + [jax.ShapeDtypeStruct((chips,) + part.shape, BF16)] + [part] * chips,
        scratch_shapes=[pltpu.VMEM(query_rows.shape, BF16)] * 2
        + [pltpu.SemaphoreType.DMA((seqs, 2))],
        compiler_params=params(ATTENTION_MIB if chips <= 4 else 56),
        cost_estimate=cost(MIB, 8),
        name="attention",
    )(query_rows, gate_logits, gated_grad, *pieces, after)
    return out[0], out[1], out[2], out[3:]


def gate_kernel(held_ref, after_ref, out_ref):
    pass


def gate(array, after):
    return pl.pallas_call(
        gate_kernel,
        in_specs=[ANYWHERE] * 2,
        out_specs=ANYWHERE,
        out_shape=jax.ShapeDtypeStruct(array.shape, array.dtype),
        input_output_aliases={0: 0},
        compiler_params=params(16),
        cost_estimate=cost(4e9, 8),
        name="gate",
    )(array, after)


def merge_kernel(chips, *refs):
    mine, arrived, outs = refs[:chips], refs[chips], refs[chips + 1 :]
    for d in range(chips):
        outs[d][...] = (mine[d][...].astype(F32) + arrived[d].astype(F32)).astype(BF16)


def close_kernel(*refs):
    parts, (key_ref, value_ref) = refs[:-2], refs[-2:]
    total = parts[0][...].astype(F32)
    for part in parts[1:]:
        total = total + part[...].astype(F32)
    key_ref[...] = total[:, :, :HEAD].astype(BF16)
    value_ref[...] = total[:, :, HEAD:].astype(BF16)


def slots(routes_ref, weights_ref, experts):
    routes = routes_ref[...]
    tokens = routes.shape[1]
    live = routes < experts
    expert = jnp.sum(jnp.where(live, routes, 0), axis=0, keepdims=True)
    has_live = jnp.sum(live.astype(jnp.int32), axis=0, keepdims=True) > 0
    weight = jnp.sum(
        jnp.where(live, weights_ref[...].astype(F32), 0.0), axis=0, keepdims=True
    )
    tall = max(experts, 16)
    member = (iota((tall, tokens), 0) == expert) & has_live
    earlier = (iota((tokens, tokens), 0) < iota((tokens, tokens), 1)).astype(BF16)
    before = dot(member.astype(BF16), earlier)
    rank = jnp.sum(jnp.where(member, before, 0.0), axis=0, keepdims=True).astype(jnp.int32)
    return jnp.where(has_live, expert * CAP + rank, -1), weight, live


def dispatch_kernel(
    experts,
    groups,
    rows,
    input_hbm,
    grad_hbm,
    routes_hbm,
    weights_hbm,
    out_ref,
    input_ref,
    grad_ref,
    routes_ref,
    weights_ref,
    sems,
):
    tokens, width = input_ref.shape
    pairs = ((routes_hbm, routes_ref), (weights_hbm, weights_ref))
    pairs = pairs + ((input_hbm, input_ref), (grad_hbm, grad_ref))
    copies = [pltpu.make_async_copy(src, dst, sems.at[i]) for i, (src, dst) in enumerate(pairs)]
    for copy in copies:
        copy.start()
    copies[0].wait()
    copies[1].wait()
    slot, weight, _ = slots(routes_ref, weights_ref, experts)
    share = width // groups
    pieces = share // LANES
    total = experts * rows
    shape = (total, tokens)
    row = iota(shape, 0)
    inner = mod(row, rows)
    hit = slot == div(row, rows) * CAP + mod(div(inner, pieces), CAP)
    hit = jnp.where(hit, mod(inner, pieces) + pieces * div(inner, CAP * pieces), -1)
    copies[2].wait()
    copies[3].wait()
    acc = None
    for a, (ref, value) in enumerate(((input_ref, 1.0), (grad_ref, weight))):
        for l in range(pieces):
            pick = hit == a * pieces + l
            source = jnp.concatenate(
                [
                    ref[:, g * share + l * LANES : g * share + (l + 1) * LANES]
                    for g in range(groups)
                ],
                axis=1,
            )
            term = dot(jnp.where(pick, value, 0.0).astype(BF16), source)
            acc = term if acc is None else acc + term
    acc = acc.astype(BF16)
    for g in range(groups):
        out_ref[g * total : (g + 1) * total, :] = acc[:, g * LANES : (g + 1) * LANES]


def enter_kernel(
    sources, rows, recv_ref, gate_ref, up_ref, down_ref, after_ref, input_ref, grad_ref, send_ref
):
    pieces = input_ref.shape[1] // LANES
    block = min(sources, 32)
    shape = (block * CAP, block * rows)
    out_row, in_row = iota(shape, 0), iota(shape, 1)
    offset = in_row - div(out_row, CAP) * rows - mod(out_row, CAP) * pieces
    picks = [
        [(offset == a * CAP * pieces + l).astype(BF16) for l in range(pieces)]
        for a in range(2)
    ]
    for b in range(sources // block):
        arrived = recv_ref[b * block * rows : (b + 1) * block * rows, :]
        here = slice(b * block * CAP, (b + 1) * block * CAP)
        inputs, grads = (
            jnp.concatenate([dot(pick, arrived) for pick in picks[a]], axis=1).astype(BF16)
            for a in range(2)
        )
        input_ref[here, :] = inputs
        grad_ref[here, :] = grads
        partial = jnp.concatenate(
            [dot(inputs, gate_ref[0]), dot(inputs, up_ref[0]), dot(grads, down_ref[0], 1, 1)],
            axis=1,
        )
        send_ref[here, :] = partial.astype(BF16)


def middle_kernel(sources, rows, *refs):
    parts = refs[:-6]
    gate_ref, up_ref, back_ref, hidden_ref, gate_rows_ref, up_rows_ref = refs[-6:]
    share = gate_ref.shape[1]
    pieces = share // LANES
    hid = gate_ref.shape[2]
    block = min(sources, 32)
    shape = (block * rows, block * CAP)
    out_row, in_row = iota(shape, 0), iota(shape, 1)
    same = div(out_row, rows) == div(in_row, CAP)
    inner, which = mod(out_row, rows), mod(in_row, CAP)
    offset = jnp.where(same, inner - which * pieces, -1)
    picks = [(offset == l).astype(BF16) for l in range(pieces)]
    pick_dot = (same & (inner == CAP * pieces + which)).astype(BF16)
    for b in range(sources // block):
        here = slice(b * block * CAP, (b + 1) * block * CAP)
        terms = [part[here, :].astype(F32) for part in parts]
        total = functools.reduce(jnp.add, terms)
        gate_pre, up_pre, hidden_grad = total[:, :hid], total[:, hid : 2 * hid], total[:, 2 * hid :]
        sig = jax.nn.sigmoid(gate_pre)
        silu = gate_pre * sig
        hidden = (silu * up_pre).astype(BF16)
        slope = sig * (1.0 + gate_pre * (1.0 - sig))
        gate_rows = (hidden_grad * up_pre * slope).astype(BF16)
        up_rows = (hidden_grad * silu).astype(BF16)
        hidden_ref[here, :] = hidden
        gate_rows_ref[here, :] = gate_rows
        up_rows_ref[here, :] = up_rows
        routed = jnp.sum(hidden.astype(F32) * hidden_grad, axis=1, keepdims=True)
        high = routed.astype(BF16)
        low = (routed - high.astype(F32)).astype(BF16)
        lane = iota((block * CAP, LANES), 1)
        routed_wide = jnp.where(lane < LANES // 2, high.astype(F32), low.astype(F32)).astype(BF16)
        input_rows = (
            dot(gate_rows, gate_ref[0], 1, 1) + dot(up_rows, up_ref[0], 1, 1)
        ).astype(BF16)
        back = dot(pick_dot, routed_wide)
        for l in range(pieces):
            back = back + dot(picks[l], input_rows[:, l * LANES : (l + 1) * LANES])
        back_ref[b * block * rows : (b + 1) * block * rows, :] = back.astype(BF16)


def weight_kernel(
    input_ref, grad_ref, hidden_ref, gate_rows_ref, up_rows_ref, gate_out, up_out, down_out
):
    gate_out[0] = dot(input_ref[...], gate_rows_ref[...], 0, 0)
    up_out[0] = dot(input_ref[...], up_rows_ref[...], 0, 0)
    down_out[0] = dot(hidden_ref[...], grad_ref[...], 0, 0)


def combine_kernel(
    experts,
    groups,
    rows,
    back_ref,
    routes_ref,
    weights_ref,
    after_ref,
    input_grad_ref,
    route_grad_ref,
):
    slot, weight, live = slots(routes_ref, weights_ref, experts)
    tokens, width = input_grad_ref.shape
    share = width // groups
    pieces = share // LANES
    total = experts * rows
    shape = (total, tokens)
    row = iota(shape, 0)
    inner = mod(row, rows)
    expert = div(row, rows)
    hit = (slot == expert * CAP + div(inner, pieces)) & (inner < CAP * pieces)
    hit = jnp.where(hit, mod(inner, pieces), -1)
    wide = jnp.concatenate([back_ref[g * total : (g + 1) * total, :] for g in range(groups)], axis=1)
    for l in range(pieces):
        pick = (hit == l).astype(BF16)
        grad = dot(pick, wide, 0, 0).astype(BF16)
        for g in range(groups):
            input_grad_ref[:, g * share + l * LANES : g * share + (l + 1) * LANES] = grad[
                :, g * LANES : (g + 1) * LANES
            ]
    hit_dot = slot == expert * CAP + inner - CAP * pieces
    hit_dot = hit_dot & (inner >= CAP * pieces) & (inner < CAP * (pieces + 1))
    routed = dot(back_ref[:total, :], hit_dot.astype(BF16), 0, 0)
    routed = routed[:1] + routed[LANES // 2 : LANES // 2 + 1]
    routed = routed / jnp.where(weight > 0.0, weight, 1.0)
    route_grad_ref[...] = jnp.where(live, routed, 0.0).astype(BF16)


def shards(
    query_rows,
    key_rows,
    value_rows,
    gate_logits,
    gated_grad,
    moe_input,
    out_grad,
    routes,
    route_weights,
    gate_proj,
    up_proj,
    down_proj,
):
    devices = lax.axis_size("expert")
    groups = lax.axis_size("dp")
    sources = devices * groups
    chips = devices // 2
    seqs, length, _ = key_rows.shape
    tokens, width = moe_input.shape
    share = width // groups
    pieces = share // LANES
    hid = gate_proj.shape[2]
    rows = -(-2 * CAP * pieces // 16) * 16
    axes = ("dp", "expert")
    swap = [(i, i ^ 1) for i in range(devices)]
    same_core = [list(range(c, devices, 2)) for c in range(2)]

    packed = pl.pallas_call(
        pack_kernel,
        in_specs=[IN_HBM] * 2,
        out_shape=jax.ShapeDtypeStruct((seqs, length, 2 * HEAD), BF16),
        scratch_shapes=[pltpu.VMEM(key_rows.shape, BF16)] * 2 + [pltpu.SemaphoreType.DMA((2,))],
        compiler_params=params(16),
        cost_estimate=cost(MIB, MIB),
        name="pack",
    )(key_rows, value_rows)
    mine = [packed]
    for d in range(1, chips):
        up = [(i, i + 2 * d) for i in range(devices - 2 * d)]
        mine.append(lax.ppermute(packed, "expert", up))
    other = [lax.ppermute(block, "expert", swap) for block in mine]

    routes_t, weights_t = routes.T, route_weights.T
    send = pl.pallas_call(
        functools.partial(dispatch_kernel, devices, groups, rows),
        in_specs=[IN_HBM] * 4,
        out_shape=jax.ShapeDtypeStruct((sources * rows, LANES), BF16),
        scratch_shapes=[
            pltpu.VMEM(moe_input.shape, BF16),
            pltpu.VMEM(out_grad.shape, BF16),
            pltpu.VMEM(routes_t.shape, routes.dtype),
            pltpu.VMEM(weights_t.shape, BF16),
            pltpu.SemaphoreType.DMA((4,)),
        ],
        compiler_params=params(60),
        cost_estimate=cost(2e9, 2 * MIB),
        name="dispatch",
    )(moe_input, out_grad, routes_t, weights_t)
    recv = lax.all_to_all(
        send.reshape(sources, rows, LANES), axes, split_axis=0, concat_axis=0, tiled=True
    ).reshape(sources * rows, LANES)

    slot_rows = jax.ShapeDtypeStruct((sources * CAP, share), BF16)
    hid_rows = jax.ShapeDtypeStruct((sources * CAP, hid), BF16)
    inputs, grads, sent = pl.pallas_call(
        functools.partial(enter_kernel, sources, rows),
        in_specs=[IN_VMEM] * 4 + [ANYWHERE],
        out_shape=[slot_rows, slot_rows, jax.ShapeDtypeStruct((sources * CAP, 3 * hid), BF16)],
        compiler_params=params(16),
        cost_estimate=cost(2e9, 2 * MIB),
        name="enter",
    )(recv, gate_proj, up_proj, down_proj, mine[min(1, chips - 1)])
    parts = [sent] + [
        lax.ppermute(sent, "dp", [(g, g ^ k) for g in range(groups)]) for k in range(1, groups)
    ]

    back, hidden, gate_rows, up_rows = pl.pallas_call(
        functools.partial(middle_kernel, sources, rows),
        in_specs=[IN_VMEM] * (len(parts) + 2),
        out_shape=[jax.ShapeDtypeStruct((sources * rows, LANES), BF16)] + [hid_rows] * 3,
        compiler_params=params(16 if groups <= 4 else 60),
        cost_estimate=cost(1e9, MIB),
        name="middle",
    )(*parts, gate_proj, up_proj)
    query_grad, gate_grad, other_part, mine_part = attention(
        query_rows, gate_logits, gated_grad, mine + other, hidden
    )
    arrived = lax.ppermute(other_part, "expert", swap)
    merged = pl.pallas_call(
        functools.partial(merge_kernel, chips),
        out_shape=[jax.ShapeDtypeStruct(packed.shape, BF16)] * chips,
        compiler_params=params(16),
        cost_estimate=cost(MIB, 2 * MIB),
        name="merge",
    )(*mine_part, arrived)
    terms = [merged[0]]
    for d in range(1, chips):
        down = [(i, i - 2 * d) for i in range(2 * d, devices)]
        terms.append(lax.ppermute(merged[d], "expert", down))
    returned = lax.all_to_all(
        back.reshape(sources, rows, LANES), axes, split_axis=0, concat_axis=0, tiled=True
    ).reshape(sources * rows, LANES)
    gate_proj_grad, up_proj_grad, down_proj_grad = pl.pallas_call(
        weight_kernel,
        out_shape=[
            jax.ShapeDtypeStruct(gate_proj.shape, F32),
            jax.ShapeDtypeStruct(up_proj.shape, F32),
            jax.ShapeDtypeStruct(down_proj.shape, F32),
        ],
        compiler_params=params(16),
        cost_estimate=cost(2e9, 2 * MIB),
        name="weight_grads",
    )(inputs, grads, hidden, gate_rows, up_rows)
    key_grad, value_grad = pl.pallas_call(
        close_kernel,
        in_specs=[IN_VMEM] * chips,
        out_shape=[jax.ShapeDtypeStruct((seqs, length, HEAD), BF16)] * 2,
        compiler_params=params(16),
        cost_estimate=cost(6e10, MIB),
        name="close",
    )(*terms)
    input_grad, route_grad = pl.pallas_call(
        functools.partial(combine_kernel, devices, groups, rows),
        in_specs=[IN_VMEM] * 3 + [ANYWHERE],
        out_shape=[
            jax.ShapeDtypeStruct(moe_input.shape, BF16),
            jax.ShapeDtypeStruct(routes_t.shape, BF16),
        ],
        compiler_params=params(16),
        cost_estimate=cost(2e9, 2 * MIB),
        name="combine",
    )(returned, routes_t, weights_t, key_grad)

    return (
        query_grad,
        key_grad,
        value_grad,
        gate_grad,
        input_grad,
        route_grad.T,
        gate_proj_grad,
        up_proj_grad,
        down_proj_grad,
    )


def solution(mesh):
    rows3 = P("dp", "expert", None)
    tokens2 = P(("dp", "expert"), None)
    weights = P("expert", "dp", None)
    weights_down = P("expert", None, "dp")
    return jax.shard_map(
        shards,
        mesh=mesh,
        in_specs=(rows3,) * 5 + (tokens2,) * 4 + (weights, weights, weights_down),
        out_specs=(rows3,) * 4 + (tokens2,) * 2 + (weights, weights, weights_down),
        check_vma=False,
    )
```

```python
import functools

import jax
import jax.numpy as jnp
from jax import lax
from jax.experimental import pallas as pl
from jax.experimental.pallas import tpu as pltpu
from jax.sharding import PartitionSpec as P

HEADS = 8
HEAD = 256
CAP = 2
LANES = 128
BF16 = jnp.bfloat16
F32 = jnp.float32
MIB = 1 << 20
ATTENTION_MIB = 32
IN_HBM = pl.BlockSpec(memory_space=pltpu.HBM)
IN_VMEM = pl.BlockSpec(memory_space=pltpu.VMEM)
ANYWHERE = pl.BlockSpec(memory_space=pl.ANY)


def dot(a, b, ca=1, cb=0):
    return lax.dot_general(a, b, (((ca,), (cb,)), ((), ())), preferred_element_type=F32)


def div(x, size):
    assert size & (size - 1) == 0
    return x >> (size.bit_length() - 1)


def mod(x, size):
    assert size & (size - 1) == 0
    return x & (size - 1)


def iota(shape, dim):
    return lax.broadcasted_iota(jnp.int32, shape, dim)


def params(mib):
    return pltpu.CompilerParams(vmem_limit_bytes=mib * MIB)


def cost(flops, bytes_accessed):
    return pl.CostEstimate(flops=int(flops), bytes_accessed=int(bytes_accessed), transcendentals=0)


def pack_kernel(key_hbm, value_hbm, out_ref, key_ref, value_ref, sems):
    copies = [
        pltpu.make_async_copy(src, dst, sems.at[i])
        for i, (src, dst) in enumerate(((key_hbm, key_ref), (value_hbm, value_ref)))
    ]
    for copy in copies:
        copy.start()
    copies[0].wait()
    out_ref[:, :, :HEAD] = key_ref[...]
    copies[1].wait()
    out_ref[:, :, HEAD:] = value_ref[...]


def held_from(chip, chips):
    if chips == 4:
        odd = chip & 1
        return (chip, chip - 2, jnp.where(odd == 1, chip - 1, -1), chip - 2 + 1 - 2 * odd)
    return [chip - d for d in range(chips)]


def attention_kernel(chips, *refs):
    q_ref, logit_ref, grad_ref = refs[:3]
    kv_refs = refs[3 : 3 + 2 * chips]
    query_grad_hbm, gate_grad_hbm, other_ref = refs[4 + 2 * chips : 7 + 2 * chips]
    mine_refs = refs[7 + 2 * chips : 7 + 3 * chips]
    query_grad_ref, gate_grad_ref, out_sems = refs[7 + 3 * chips :]
    seqs, length, _ = q_ref.shape
    side = chips * length
    scale = HEAD ** (-0.5)
    position = lax.axis_index("expert")
    chip, core = position >> 1, position & 1

    shape = (1, 2 * side)
    col = iota(shape, 1)
    half, back, inner = div(col, side), div(mod(col, side), length), mod(col, length)
    owner = chip - back
    for d, source in enumerate(held_from(chip, chips)):
        owner = jnp.where(back == d, source, owner)
    block = 2 * owner + jnp.where(half == 0, core, 1 - core)
    key_pos = jnp.where(owner >= 0, block * length + inner, 2 * side)
    query_pos = position * length + mod(iota((HEADS * length, 1), 0), length)

    def stacked(ref, s):
        return jnp.concatenate(
            [ref[s, :, h * HEAD : (h + 1) * HEAD] for h in range(HEADS)], axis=0
        )

    stores = []
    for s in range(seqs):
        both = jnp.concatenate([ref[s] for ref in kv_refs], axis=0)
        keys, values = both[:, :HEAD], both[:, HEAD:]
        queries = stacked(q_ref, s)
        scores = jnp.where(key_pos <= query_pos, dot(queries, keys, 1, 1), -jnp.inf)
        row_max = jnp.max(scores, axis=1, keepdims=True)
        unnormed = jnp.exp((scores - row_max) * scale)
        probs = unnormed * (1.0 / jnp.sum(unnormed, axis=1, keepdims=True))
        probs_low = probs.astype(BF16)
        context = dot(probs_low, values)
        gate = jax.nn.sigmoid(stacked(logit_ref, s).astype(F32))
        upstream = stacked(grad_ref, s).astype(F32)
        context_grad = (upstream * gate).astype(BF16)
        gate_grad = (upstream * context * gate * (1.0 - gate)).astype(BF16)
        for h in range(HEADS):
            gate_grad_ref[s, :, h * HEAD : (h + 1) * HEAD] = gate_grad[h * length : (h + 1) * length]
        stores.append(pltpu.make_async_copy(gate_grad_ref.at[s], gate_grad_hbm.at[s], out_sems.at[s, 0]))
        stores[-1].start()
        grad_dot = jnp.sum(context_grad.astype(F32) * context, axis=1, keepdims=True)
        prob_grad = dot(context_grad, values, 1, 1)
        score_grad = (probs * (prob_grad - grad_dot)).astype(BF16)
        query_grad = (dot(score_grad, keys) * scale).astype(BF16)
        for h in range(HEADS):
            query_grad_ref[s, :, h * HEAD : (h + 1) * HEAD] = query_grad[h * length : (h + 1) * length]
        stores.append(pltpu.make_async_copy(query_grad_ref.at[s], query_grad_hbm.at[s], out_sems.at[s, 1]))
        stores[-1].start()
        key_part = (dot(score_grad, queries, 0, 0) * scale).astype(BF16)
        value_part = dot(probs_low, context_grad, 0, 0).astype(BF16)
        for d in range(chips):
            start = d * length
            mine_refs[d][s, :, :HEAD] = key_part[start : start + length]
            mine_refs[d][s, :, HEAD:] = value_part[start : start + length]
            start = side + d * length
            other_ref[d, s, :, :HEAD] = key_part[start : start + length]
            other_ref[d, s, :, HEAD:] = value_part[start : start + length]
    for store in stores:
        store.wait()


def attention(query_rows, gate_logits, gated_grad, pieces, after):
    seqs, length, width = query_rows.shape
    chips = len(pieces) // 2
    full = jax.ShapeDtypeStruct((seqs, length, width), BF16)
    part = jax.ShapeDtypeStruct(pieces[0].shape, BF16)
    out = pl.pallas_call(
        functools.partial(attention_kernel, chips),
        in_specs=[IN_VMEM] * (3 + 2 * chips) + [ANYWHERE],
        out_specs=[IN_HBM] * 2 + [IN_VMEM] * (1 + chips),
        out_shape=[full] * 2 + [jax.ShapeDtypeStruct((chips,) + part.shape, BF16)] + [part] * chips,
        scratch_shapes=[pltpu.VMEM(query_rows.shape, BF16)] * 2
        + [pltpu.SemaphoreType.DMA((seqs, 2))],
        compiler_params=params(ATTENTION_MIB if chips <= 4 else 56),
        cost_estimate=cost(MIB, 8),
        name="attention",
    )(query_rows, gate_logits, gated_grad, *pieces, after)
    return out[0], out[1], out[2], out[3:]


def gate_kernel(held_ref, after_ref, out_ref):
    pass


def gate(array, after):
    return pl.pallas_call(
        gate_kernel,
        in_specs=[ANYWHERE] * 2,
        out_specs=ANYWHERE,
        out_shape=jax.ShapeDtypeStruct(array.shape, array.dtype),
        input_output_aliases={0: 0},
        compiler_params=params(16),
        cost_estimate=cost(8, 8),
        name="gate",
    )(array, after)


def merge_kernel(chips, *refs):
    mine, arrived, outs = refs[:chips], refs[chips], refs[chips + 1 :]
    for d in range(chips):
        outs[d][...] = (mine[d][...].astype(F32) + arrived[d].astype(F32)).astype(BF16)


def close_kernel(*refs):
    parts, (key_ref, value_ref) = refs[:-2], refs[-2:]
    total = parts[0][...].astype(F32)
    for part in parts[1:]:
        total = total + part[...].astype(F32)
    key_ref[...] = total[:, :, :HEAD].astype(BF16)
    value_ref[...] = total[:, :, HEAD:].astype(BF16)


def slots(routes_ref, weights_ref, experts):
    routes = routes_ref[...]
    tokens = routes.shape[1]
    live = routes < experts
    expert = jnp.sum(jnp.where(live, routes, 0), axis=0, keepdims=True)
    has_live = jnp.sum(live.astype(jnp.int32), axis=0, keepdims=True) > 0
    weight = jnp.sum(
        jnp.where(live, weights_ref[...].astype(F32), 0.0), axis=0, keepdims=True
    )
    tall = max(experts, 16)
    member = (iota((tall, tokens), 0) == expert) & has_live
    earlier = (iota((tokens, tokens), 0) < iota((tokens, tokens), 1)).astype(BF16)
    before = dot(member.astype(BF16), earlier)
    rank = jnp.sum(jnp.where(member, before, 0.0), axis=0, keepdims=True).astype(jnp.int32)
    return jnp.where(has_live, expert * CAP + rank, -1), weight, live


def dispatch_kernel(
    experts, groups, rows, input_ref, grad_ref, routes_ref, weights_ref, after_ref, out_ref
):
    tokens, width = input_ref.shape
    slot, weight, _ = slots(routes_ref, weights_ref, experts)
    share = width // groups
    pieces = share // LANES
    total = experts * rows
    shape = (total, tokens)
    row = iota(shape, 0)
    inner = mod(row, rows)
    hit = slot == div(row, rows) * CAP + mod(div(inner, pieces), CAP)
    hit = jnp.where(hit, mod(inner, pieces) + pieces * div(inner, CAP * pieces), -1)
    acc = None
    for a, (ref, value) in enumerate(((input_ref, 1.0), (grad_ref, weight))):
        for l in range(pieces):
            pick = hit == a * pieces + l
            source = jnp.concatenate(
                [
                    ref[:, g * share + l * LANES : g * share + (l + 1) * LANES]
                    for g in range(groups)
                ],
                axis=1,
            )
            term = dot(jnp.where(pick, value, 0.0).astype(BF16), source)
            acc = term if acc is None else acc + term
    acc = acc.astype(BF16)
    for g in range(groups):
        out_ref[g * total : (g + 1) * total, :] = acc[:, g * LANES : (g + 1) * LANES]


def enter_kernel(
    sources, rows, recv_ref, gate_ref, up_ref, down_ref, after_ref, input_ref, grad_ref, send_ref
):
    pieces = input_ref.shape[1] // LANES
    block = min(sources, 32)
    shape = (block * CAP, block * rows)
    out_row, in_row = iota(shape, 0), iota(shape, 1)
    offset = in_row - div(out_row, CAP) * rows - mod(out_row, CAP) * pieces
    picks = [
        [(offset == a * CAP * pieces + l).astype(BF16) for l in range(pieces)]
        for a in range(2)
    ]
    for b in range(sources // block):
        arrived = recv_ref[b * block * rows : (b + 1) * block * rows, :]
        here = slice(b * block * CAP, (b + 1) * block * CAP)
        inputs, grads = (
            jnp.concatenate([dot(pick, arrived) for pick in picks[a]], axis=1).astype(BF16)
            for a in range(2)
        )
        input_ref[here, :] = inputs
        grad_ref[here, :] = grads
        partial = jnp.concatenate(
            [dot(inputs, gate_ref[0]), dot(inputs, up_ref[0]), dot(grads, down_ref[0], 1, 1)],
            axis=1,
        )
        send_ref[here, :] = partial.astype(BF16)


def middle_kernel(sources, rows, *refs):
    parts = refs[:-7]
    gate_ref, up_ref, _, back_ref, hidden_ref, gate_rows_ref, up_rows_ref = refs[-7:]
    share = gate_ref.shape[1]
    pieces = share // LANES
    hid = gate_ref.shape[2]
    block = min(sources, 32)
    shape = (block * rows, block * CAP)
    out_row, in_row = iota(shape, 0), iota(shape, 1)
    same = div(out_row, rows) == div(in_row, CAP)
    inner, which = mod(out_row, rows), mod(in_row, CAP)
    offset = jnp.where(same, inner - which * pieces, -1)
    picks = [(offset == l).astype(BF16) for l in range(pieces)]
    pick_dot = (same & (inner == CAP * pieces + which)).astype(BF16)
    for b in range(sources // block):
        here = slice(b * block * CAP, (b + 1) * block * CAP)
        terms = [part[here, :].astype(F32) for part in parts]
        total = functools.reduce(jnp.add, terms)
        gate_pre, up_pre, hidden_grad = total[:, :hid], total[:, hid : 2 * hid], total[:, 2 * hid :]
        sig = jax.nn.sigmoid(gate_pre)
        silu = gate_pre * sig
        hidden = (silu * up_pre).astype(BF16)
        slope = sig * (1.0 + gate_pre * (1.0 - sig))
        gate_rows = (hidden_grad * up_pre * slope).astype(BF16)
        up_rows = (hidden_grad * silu).astype(BF16)
        hidden_ref[here, :] = hidden
        gate_rows_ref[here, :] = gate_rows
        up_rows_ref[here, :] = up_rows
        routed = jnp.sum(hidden.astype(F32) * hidden_grad, axis=1, keepdims=True)
        high = routed.astype(BF16)
        low = (routed - high.astype(F32)).astype(BF16)
        lane = iota((block * CAP, LANES), 1)
        routed_wide = jnp.where(lane < LANES // 2, high.astype(F32), low.astype(F32)).astype(BF16)
        input_rows = (
            dot(gate_rows, gate_ref[0], 1, 1) + dot(up_rows, up_ref[0], 1, 1)
        ).astype(BF16)
        back = dot(pick_dot, routed_wide)
        for l in range(pieces):
            back = back + dot(picks[l], input_rows[:, l * LANES : (l + 1) * LANES])
        back_ref[b * block * rows : (b + 1) * block * rows, :] = back.astype(BF16)


def weight_kernel(
    input_ref, grad_ref, hidden_ref, gate_rows_ref, up_rows_ref, gate_out, up_out, down_out
):
    gate_out[0] = dot(input_ref[...], gate_rows_ref[...], 0, 0)
    up_out[0] = dot(input_ref[...], up_rows_ref[...], 0, 0)
    down_out[0] = dot(hidden_ref[...], grad_ref[...], 0, 0)


def combine_kernel(
    experts,
    groups,
    rows,
    back_ref,
    routes_ref,
    weights_ref,
    after_ref,
    input_grad_ref,
    route_grad_ref,
):
    slot, weight, live = slots(routes_ref, weights_ref, experts)
    tokens, width = input_grad_ref.shape
    share = width // groups
    pieces = share // LANES
    total = experts * rows
    shape = (total, tokens)
    row = iota(shape, 0)
    inner = mod(row, rows)
    expert = div(row, rows)
    hit = (slot == expert * CAP + div(inner, pieces)) & (inner < CAP * pieces)
    hit = jnp.where(hit, mod(inner, pieces), -1)
    wide = jnp.concatenate([back_ref[g * total : (g + 1) * total, :] for g in range(groups)], axis=1)
    for l in range(pieces):
        pick = (hit == l).astype(BF16)
        grad = dot(pick, wide, 0, 0).astype(BF16)
        for g in range(groups):
            input_grad_ref[:, g * share + l * LANES : g * share + (l + 1) * LANES] = grad[
                :, g * LANES : (g + 1) * LANES
            ]
    hit_dot = slot == expert * CAP + inner - CAP * pieces
    hit_dot = hit_dot & (inner >= CAP * pieces) & (inner < CAP * (pieces + 1))
    routed = dot(back_ref[:total, :], hit_dot.astype(BF16), 0, 0)
    routed = routed[:1] + routed[LANES // 2 : LANES // 2 + 1]
    routed = routed / jnp.where(weight > 0.0, weight, 1.0)
    route_grad_ref[...] = jnp.where(live, routed, 0.0).astype(BF16)


def shards(
    query_rows,
    key_rows,
    value_rows,
    gate_logits,
    gated_grad,
    moe_input,
    out_grad,
    routes,
    route_weights,
    gate_proj,
    up_proj,
    down_proj,
):
    devices = lax.axis_size("expert")
    groups = lax.axis_size("dp")
    sources = devices * groups
    chips = devices // 2
    seqs, length, _ = key_rows.shape
    tokens, width = moe_input.shape
    share = width // groups
    pieces = share // LANES
    hid = gate_proj.shape[2]
    rows = -(-2 * CAP * pieces // 16) * 16
    axes = ("dp", "expert")
    swap = [(i, i ^ 1) for i in range(devices)]
    same_core = [list(range(c, devices, 2)) for c in range(2)]

    packed = pl.pallas_call(
        pack_kernel,
        in_specs=[IN_HBM] * 2,
        out_shape=jax.ShapeDtypeStruct((seqs, length, 2 * HEAD), BF16),
        scratch_shapes=[pltpu.VMEM(key_rows.shape, BF16)] * 2 + [pltpu.SemaphoreType.DMA((2,))],
        compiler_params=params(16),
        cost_estimate=cost(6e10, MIB),
        name="pack",
    )(key_rows, value_rows)
    def chip_permute(array, pairs):
        return lax.ppermute(
            array, "expert", [(2 * a + c, 2 * b + c) for a, b in pairs for c in range(2)]
        )

    mine = [packed]
    if chips == 4:
        two = chip_permute(packed, [(0, 2), (1, 3)])
        one = chip_permute(packed, [(0, 1), (2, 3)])
        two = gate(two, one)
        mine += [two, one, chip_permute(two, [(2, 3), (3, 2)])]
    else:
        for d in range(1, chips):
            mine.append(chip_permute(packed, [(i, i + d) for i in range(chips - d)]))
    other = [lax.ppermute(block, "expert", swap) for block in mine]

    routes_t, weights_t = routes.T, route_weights.T
    send = pl.pallas_call(
        functools.partial(dispatch_kernel, devices, groups, rows),
        in_specs=[IN_VMEM] * 4 + [ANYWHERE],
        out_shape=jax.ShapeDtypeStruct((sources * rows, LANES), BF16),
        compiler_params=params(16),
        cost_estimate=cost(2e9, 2 * MIB),
        name="dispatch",
    )(moe_input, out_grad, routes_t, weights_t, packed)
    recv = lax.all_to_all(
        send.reshape(sources, rows, LANES), axes, split_axis=0, concat_axis=0, tiled=True
    ).reshape(sources * rows, LANES)

    slot_rows = jax.ShapeDtypeStruct((sources * CAP, share), BF16)
    hid_rows = jax.ShapeDtypeStruct((sources * CAP, hid), BF16)
    inputs, grads, sent = pl.pallas_call(
        functools.partial(enter_kernel, sources, rows),
        in_specs=[IN_VMEM] * 4 + [ANYWHERE],
        out_shape=[slot_rows, slot_rows, jax.ShapeDtypeStruct((sources * CAP, 3 * hid), BF16)],
        compiler_params=params(16),
        cost_estimate=cost(2e9, 2 * MIB),
        name="enter",
    )(recv, gate_proj, up_proj, down_proj, packed)
    parts = [sent] + [
        lax.ppermute(sent, "dp", [(g, g ^ k) for g in range(groups)]) for k in range(1, groups)
    ]

    query_grad, gate_grad, other_part, mine_part = attention(
        query_rows, gate_logits, gated_grad, mine + other, sent
    )
    arrived = lax.ppermute(other_part, "expert", swap)
    merged = pl.pallas_call(
        functools.partial(merge_kernel, chips),
        out_shape=[jax.ShapeDtypeStruct(packed.shape, BF16)] * chips,
        compiler_params=params(16),
        cost_estimate=cost(MIB, 2 * MIB),
        name="merge",
    )(*mine_part, arrived)
    if chips == 4:
        returns = [[(2, 0), (3, 1)], [(1, 0), (3, 2)], [(2, 1), (3, 0)]]
    else:
        returns = [[(i, i - d) for i in range(d, chips)] for d in range(1, chips)]
    terms = [merged[0]] + [chip_permute(m, pairs) for m, pairs in zip(merged[1:], returns)]
    back, hidden, gate_rows, up_rows = pl.pallas_call(
        functools.partial(middle_kernel, sources, rows),
        in_specs=[IN_VMEM] * (len(parts) + 2) + [ANYWHERE],
        out_shape=[jax.ShapeDtypeStruct((sources * rows, LANES), BF16)] + [hid_rows] * 3,
        compiler_params=params(16 if groups <= 4 else 60),
        cost_estimate=cost(2e9, 2 * MIB),
        name="middle",
    )(*parts, gate_proj, up_proj, terms[min(1, chips - 1)])
    returned = lax.all_to_all(
        back.reshape(sources, rows, LANES), axes, split_axis=0, concat_axis=0, tiled=True
    ).reshape(sources * rows, LANES)
    gate_proj_grad, up_proj_grad, down_proj_grad = pl.pallas_call(
        weight_kernel,
        out_shape=[
            jax.ShapeDtypeStruct(gate_proj.shape, F32),
            jax.ShapeDtypeStruct(up_proj.shape, F32),
            jax.ShapeDtypeStruct(down_proj.shape, F32),
        ],
        compiler_params=params(16),
        cost_estimate=cost(2e9, 2 * MIB),
        name="weight_grads",
    )(inputs, grads, hidden, gate_rows, up_rows)
    key_grad, value_grad = pl.pallas_call(
        close_kernel,
        in_specs=[IN_VMEM] * chips,
        out_shape=[jax.ShapeDtypeStruct((seqs, length, HEAD), BF16)] * 2,
        compiler_params=params(16),
        cost_estimate=cost(6e10, MIB),
        name="close",
    )(*terms)
    input_grad, route_grad = pl.pallas_call(
        functools.partial(combine_kernel, devices, groups, rows),
        in_specs=[IN_VMEM] * 3 + [ANYWHERE],
        out_shape=[
            jax.ShapeDtypeStruct(moe_input.shape, BF16),
            jax.ShapeDtypeStruct(routes_t.shape, BF16),
        ],
        compiler_params=params(16),
        cost_estimate=cost(2e9, 2 * MIB),
        name="combine",
    )(returned, routes_t, weights_t, key_grad)

    return (
        query_grad,
        key_grad,
        value_grad,
        gate_grad,
        input_grad,
        route_grad.T,
        gate_proj_grad,
        up_proj_grad,
        down_proj_grad,
    )


def solution(mesh):
    rows3 = P("dp", "expert", None)
    tokens2 = P(("dp", "expert"), None)
    weights = P("expert", "dp", None)
    weights_down = P("expert", None, "dp")
    return jax.shard_map(
        shards,
        mesh=mesh,
        in_specs=(rows3,) * 5 + (tokens2,) * 4 + (weights, weights, weights_down),
        out_specs=(rows3,) * 4 + (tokens2,) * 2 + (weights, weights, weights_down),
        check_vma=False,
    )
```

```python
import functools

import jax
import jax.numpy as jnp
from jax import lax
from jax.experimental import pallas as pl
from jax.experimental.pallas import tpu as pltpu
from jax.sharding import PartitionSpec as P

HEADS = 8
HEAD = 256
CAP = 2
LANES = 128
BF16 = jnp.bfloat16
F32 = jnp.float32
MIB = 1 << 20
ATTENTION_MIB = 32
IN_HBM = pl.BlockSpec(memory_space=pltpu.HBM)
IN_VMEM = pl.BlockSpec(memory_space=pltpu.VMEM)
ANYWHERE = pl.BlockSpec(memory_space=pl.ANY)


def dot(a, b, ca=1, cb=0):
    return lax.dot_general(a, b, (((ca,), (cb,)), ((), ())), preferred_element_type=F32)


def div(x, size):
    assert size & (size - 1) == 0
    return x >> (size.bit_length() - 1)


def mod(x, size):
    assert size & (size - 1) == 0
    return x & (size - 1)


def iota(shape, dim):
    return lax.broadcasted_iota(jnp.int32, shape, dim)


def params(mib):
    return pltpu.CompilerParams(vmem_limit_bytes=mib * MIB)


def cost(flops, bytes_accessed):
    return pl.CostEstimate(flops=int(flops), bytes_accessed=int(bytes_accessed), transcendentals=0)


def pack_kernel(key_hbm, value_hbm, out_ref, key_ref, value_ref, sems):
    copies = [
        pltpu.make_async_copy(src, dst, sems.at[i])
        for i, (src, dst) in enumerate(((key_hbm, key_ref), (value_hbm, value_ref)))
    ]
    for copy in copies:
        copy.start()
    copies[0].wait()
    out_ref[:, :, :HEAD] = key_ref[...]
    copies[1].wait()
    out_ref[:, :, HEAD:] = value_ref[...]


def attention_kernel(chips, *refs):
    q_ref, logit_ref, grad_ref = refs[:3]
    kv_refs = refs[3 : 3 + 2 * chips]
    query_grad_hbm, gate_grad_hbm, other_ref = refs[3 + 2 * chips : 6 + 2 * chips]
    mine_refs = refs[6 + 2 * chips : 6 + 3 * chips]
    query_grad_ref, gate_grad_ref, out_sems = refs[6 + 3 * chips :]
    seqs, length, _ = q_ref.shape
    side = chips * length
    scale = HEAD ** (-0.5)
    position = lax.axis_index("expert")
    chip, core = position >> 1, position & 1

    shape = (1, 2 * side)
    col = iota(shape, 1)
    half, back, inner = div(col, side), div(mod(col, side), length), mod(col, length)
    block = 2 * (chip - back) + jnp.where(half == 0, core, 1 - core)
    key_pos = jnp.where(back <= chip, block * length + inner, 2 * side)
    query_pos = position * length + mod(iota((HEADS * length, 1), 0), length)

    def stacked(ref, s):
        return jnp.concatenate(
            [ref[s, :, h * HEAD : (h + 1) * HEAD] for h in range(HEADS)], axis=0
        )

    stores = []
    for s in range(seqs):
        both = jnp.concatenate([ref[s] for ref in kv_refs], axis=0)
        keys, values = both[:, :HEAD], both[:, HEAD:]
        queries = stacked(q_ref, s)
        scores = jnp.where(key_pos <= query_pos, dot(queries, keys, 1, 1), -jnp.inf)
        row_max = jnp.max(scores, axis=1, keepdims=True)
        unnormed = jnp.exp((scores - row_max) * scale)
        probs = unnormed * (1.0 / jnp.sum(unnormed, axis=1, keepdims=True))
        probs_low = probs.astype(BF16)
        context = dot(probs_low, values)
        gate = jax.nn.sigmoid(stacked(logit_ref, s).astype(F32))
        upstream = stacked(grad_ref, s).astype(F32)
        context_grad = (upstream * gate).astype(BF16)
        gate_grad = (upstream * context * gate * (1.0 - gate)).astype(BF16)
        for h in range(HEADS):
            gate_grad_ref[s, :, h * HEAD : (h + 1) * HEAD] = gate_grad[h * length : (h + 1) * length]
        stores.append(pltpu.make_async_copy(gate_grad_ref.at[s], gate_grad_hbm.at[s], out_sems.at[s, 0]))
        stores[-1].start()
        grad_dot = jnp.sum(context_grad.astype(F32) * context, axis=1, keepdims=True)
        prob_grad = dot(context_grad, values, 1, 1)
        score_grad = (probs * (prob_grad - grad_dot)).astype(BF16)
        query_grad = (dot(score_grad, keys) * scale).astype(BF16)
        for h in range(HEADS):
            query_grad_ref[s, :, h * HEAD : (h + 1) * HEAD] = query_grad[h * length : (h + 1) * length]
        stores.append(pltpu.make_async_copy(query_grad_ref.at[s], query_grad_hbm.at[s], out_sems.at[s, 1]))
        stores[-1].start()
        key_part = (dot(score_grad, queries, 0, 0) * scale).astype(BF16)
        value_part = dot(probs_low, context_grad, 0, 0).astype(BF16)
        for d in range(chips):
            start = d * length
            mine_refs[d][s, :, :HEAD] = key_part[start : start + length]
            mine_refs[d][s, :, HEAD:] = value_part[start : start + length]
            start = side + d * length
            other_ref[d, s, :, :HEAD] = key_part[start : start + length]
            other_ref[d, s, :, HEAD:] = value_part[start : start + length]
    for store in stores:
        store.wait()


def attention(query_rows, gate_logits, gated_grad, pieces):
    seqs, length, width = query_rows.shape
    chips = len(pieces) // 2
    full = jax.ShapeDtypeStruct((seqs, length, width), BF16)
    part = jax.ShapeDtypeStruct(pieces[0].shape, BF16)
    out = pl.pallas_call(
        functools.partial(attention_kernel, chips),
        in_specs=[IN_VMEM] * (3 + 2 * chips),
        out_specs=[IN_HBM] * 2 + [IN_VMEM] * (1 + chips),
        out_shape=[full] * 2 + [jax.ShapeDtypeStruct((chips,) + part.shape, BF16)] + [part] * chips,
        scratch_shapes=[pltpu.VMEM(query_rows.shape, BF16)] * 2
        + [pltpu.SemaphoreType.DMA((seqs, 2))],
        compiler_params=params(ATTENTION_MIB if chips <= 4 else 56),
        cost_estimate=cost(MIB, 8),
        name="attention",
    )(query_rows, gate_logits, gated_grad, *pieces)
    return out[0], out[1], out[2], out[3:]


def gate_kernel(held_ref, after_ref, out_ref):
    pass


def gate(array, after):
    return pl.pallas_call(
        gate_kernel,
        in_specs=[ANYWHERE] * 2,
        out_specs=ANYWHERE,
        out_shape=jax.ShapeDtypeStruct(array.shape, array.dtype),
        input_output_aliases={0: 0},
        compiler_params=params(16),
        cost_estimate=cost(4e9, 8),
        name="gate",
    )(array, after)


def merge_kernel(chips, *refs):
    mine, arrived, outs = refs[:chips], refs[chips], refs[chips + 1 :]
    for d in range(chips):
        outs[d][...] = (mine[d][...].astype(F32) + arrived[d].astype(F32)).astype(BF16)


def close_kernel(*refs):
    parts, (key_ref, value_ref) = refs[:-2], refs[-2:]
    total = parts[0][...].astype(F32)
    for part in parts[1:]:
        total = total + part[...].astype(F32)
    key_ref[...] = total[:, :, :HEAD].astype(BF16)
    value_ref[...] = total[:, :, HEAD:].astype(BF16)


def slots(routes_ref, weights_ref, experts):
    routes = routes_ref[...]
    tokens = routes.shape[1]
    live = routes < experts
    expert = jnp.sum(jnp.where(live, routes, 0), axis=0, keepdims=True)
    has_live = jnp.sum(live.astype(jnp.int32), axis=0, keepdims=True) > 0
    weight = jnp.sum(
        jnp.where(live, weights_ref[...].astype(F32), 0.0), axis=0, keepdims=True
    )
    tall = max(experts, 16)
    member = (iota((tall, tokens), 0) == expert) & has_live
    earlier = (iota((tokens, tokens), 0) < iota((tokens, tokens), 1)).astype(BF16)
    before = dot(member.astype(BF16), earlier)
    rank = jnp.sum(jnp.where(member, before, 0.0), axis=0, keepdims=True).astype(jnp.int32)
    return jnp.where(has_live, expert * CAP + rank, -1), weight, live


def dispatch_kernel(
    experts, groups, rows, input_ref, grad_ref, routes_ref, weights_ref, after_ref, out_ref
):
    tokens, width = input_ref.shape
    slot, weight, _ = slots(routes_ref, weights_ref, experts)
    share = width // groups
    pieces = share // LANES
    total = experts * rows
    shape = (total, tokens)
    row = iota(shape, 0)
    inner = mod(row, rows)
    hit = slot == div(row, rows) * CAP + mod(div(inner, pieces), CAP)
    hit = jnp.where(hit, mod(inner, pieces) + pieces * div(inner, CAP * pieces), -1)
    acc = None
    for a, (ref, value) in enumerate(((input_ref, 1.0), (grad_ref, weight))):
        for l in range(pieces):
            pick = hit == a * pieces + l
            source = jnp.concatenate(
                [
                    ref[:, g * share + l * LANES : g * share + (l + 1) * LANES]
                    for g in range(groups)
                ],
                axis=1,
            )
            term = dot(jnp.where(pick, value, 0.0).astype(BF16), source)
            acc = term if acc is None else acc + term
    acc = acc.astype(BF16)
    for g in range(groups):
        out_ref[g * total : (g + 1) * total, :] = acc[:, g * LANES : (g + 1) * LANES]


def enter_kernel(
    sources, rows, recv_ref, gate_ref, up_ref, down_ref, after_ref, input_ref, grad_ref, send_ref
):
    pieces = input_ref.shape[1] // LANES
    block = min(sources, 32)
    shape = (block * CAP, block * rows)
    out_row, in_row = iota(shape, 0), iota(shape, 1)
    offset = in_row - div(out_row, CAP) * rows - mod(out_row, CAP) * pieces
    picks = [
        [(offset == a * CAP * pieces + l).astype(BF16) for l in range(pieces)]
        for a in range(2)
    ]
    for b in range(sources // block):
        arrived = recv_ref[b * block * rows : (b + 1) * block * rows, :]
        here = slice(b * block * CAP, (b + 1) * block * CAP)
        inputs, grads = (
            jnp.concatenate([dot(pick, arrived) for pick in picks[a]], axis=1).astype(BF16)
            for a in range(2)
        )
        input_ref[here, :] = inputs
        grad_ref[here, :] = grads
        partial = jnp.concatenate(
            [dot(inputs, gate_ref[0]), dot(inputs, up_ref[0]), dot(grads, down_ref[0], 1, 1)],
            axis=1,
        )
        send_ref[here, :] = partial.astype(BF16)


def middle_kernel(sources, rows, *refs):
    parts = refs[:-7]
    gate_ref, up_ref, _, back_ref, hidden_ref, gate_rows_ref, up_rows_ref = refs[-7:]
    share = gate_ref.shape[1]
    pieces = share // LANES
    hid = gate_ref.shape[2]
    block = min(sources, 32)
    shape = (block * rows, block * CAP)
    out_row, in_row = iota(shape, 0), iota(shape, 1)
    same = div(out_row, rows) == div(in_row, CAP)
    inner, which = mod(out_row, rows), mod(in_row, CAP)
    offset = jnp.where(same, inner - which * pieces, -1)
    picks = [(offset == l).astype(BF16) for l in range(pieces)]
    pick_dot = (same & (inner == CAP * pieces + which)).astype(BF16)
    for b in range(sources // block):
        here = slice(b * block * CAP, (b + 1) * block * CAP)
        terms = [part[here, :].astype(F32) for part in parts]
        total = functools.reduce(jnp.add, terms)
        gate_pre, up_pre, hidden_grad = total[:, :hid], total[:, hid : 2 * hid], total[:, 2 * hid :]
        sig = jax.nn.sigmoid(gate_pre)
        silu = gate_pre * sig
        hidden = (silu * up_pre).astype(BF16)
        slope = sig * (1.0 + gate_pre * (1.0 - sig))
        gate_rows = (hidden_grad * up_pre * slope).astype(BF16)
        up_rows = (hidden_grad * silu).astype(BF16)
        hidden_ref[here, :] = hidden
        gate_rows_ref[here, :] = gate_rows
        up_rows_ref[here, :] = up_rows
        routed = jnp.sum(hidden.astype(F32) * hidden_grad, axis=1, keepdims=True)
        high = routed.astype(BF16)
        low = (routed - high.astype(F32)).astype(BF16)
        lane = iota((block * CAP, LANES), 1)
        routed_wide = jnp.where(lane < LANES // 2, high.astype(F32), low.astype(F32)).astype(BF16)
        input_rows = (
            dot(gate_rows, gate_ref[0], 1, 1) + dot(up_rows, up_ref[0], 1, 1)
        ).astype(BF16)
        back = dot(pick_dot, routed_wide)
        for l in range(pieces):
            back = back + dot(picks[l], input_rows[:, l * LANES : (l + 1) * LANES])
        back_ref[b * block * rows : (b + 1) * block * rows, :] = back.astype(BF16)


def weight_kernel(
    input_ref, grad_ref, hidden_ref, gate_rows_ref, up_rows_ref, gate_out, up_out, down_out
):
    gate_out[0] = dot(input_ref[...], gate_rows_ref[...], 0, 0)
    up_out[0] = dot(input_ref[...], up_rows_ref[...], 0, 0)
    down_out[0] = dot(hidden_ref[...], grad_ref[...], 0, 0)


def combine_kernel(
    experts,
    groups,
    rows,
    back_ref,
    routes_ref,
    weights_ref,
    after_ref,
    input_grad_ref,
    route_grad_ref,
):
    slot, weight, live = slots(routes_ref, weights_ref, experts)
    tokens, width = input_grad_ref.shape
    share = width // groups
    pieces = share // LANES
    total = experts * rows
    shape = (total, tokens)
    row = iota(shape, 0)
    inner = mod(row, rows)
    expert = div(row, rows)
    hit = (slot == expert * CAP + div(inner, pieces)) & (inner < CAP * pieces)
    hit = jnp.where(hit, mod(inner, pieces), -1)
    wide = jnp.concatenate([back_ref[g * total : (g + 1) * total, :] for g in range(groups)], axis=1)
    for l in range(pieces):
        pick = (hit == l).astype(BF16)
        grad = dot(pick, wide, 0, 0).astype(BF16)
        for g in range(groups):
            input_grad_ref[:, g * share + l * LANES : g * share + (l + 1) * LANES] = grad[
                :, g * LANES : (g + 1) * LANES
            ]
    hit_dot = slot == expert * CAP + inner - CAP * pieces
    hit_dot = hit_dot & (inner >= CAP * pieces) & (inner < CAP * (pieces + 1))
    routed = dot(back_ref[:total, :], hit_dot.astype(BF16), 0, 0)
    routed = routed[:1] + routed[LANES // 2 : LANES // 2 + 1]
    routed = routed / jnp.where(weight > 0.0, weight, 1.0)
    route_grad_ref[...] = jnp.where(live, routed, 0.0).astype(BF16)


def shards(
    query_rows,
    key_rows,
    value_rows,
    gate_logits,
    gated_grad,
    moe_input,
    out_grad,
    routes,
    route_weights,
    gate_proj,
    up_proj,
    down_proj,
):
    devices = lax.axis_size("expert")
    groups = lax.axis_size("dp")
    sources = devices * groups
    chips = devices // 2
    seqs, length, _ = key_rows.shape
    tokens, width = moe_input.shape
    share = width // groups
    pieces = share // LANES
    hid = gate_proj.shape[2]
    rows = -(-2 * CAP * pieces // 16) * 16
    axes = ("dp", "expert")
    swap = [(i, i ^ 1) for i in range(devices)]
    same_core = [list(range(c, devices, 2)) for c in range(2)]

    packed = pl.pallas_call(
        pack_kernel,
        in_specs=[IN_HBM] * 2,
        out_shape=jax.ShapeDtypeStruct((seqs, length, 2 * HEAD), BF16),
        scratch_shapes=[pltpu.VMEM(key_rows.shape, BF16)] * 2 + [pltpu.SemaphoreType.DMA((2,))],
        compiler_params=params(16),
        cost_estimate=cost(6e10, MIB),
        name="pack",
    )(key_rows, value_rows)
    mine = [packed]
    for d in range(1, chips):
        up = [(i, i + 2 * d) for i in range(devices - 2 * d)]
        mine.append(lax.ppermute(packed, "expert", up))
    other = [lax.ppermute(block, "expert", swap) for block in mine]

    routes_t, weights_t = routes.T, route_weights.T
    send = pl.pallas_call(
        functools.partial(dispatch_kernel, devices, groups, rows),
        in_specs=[IN_VMEM] * 4 + [ANYWHERE],
        out_shape=jax.ShapeDtypeStruct((sources * rows, LANES), BF16),
        compiler_params=params(16),
        cost_estimate=cost(2e9, 2 * MIB),
        name="dispatch",
    )(moe_input, out_grad, routes_t, weights_t, packed)
    recv = lax.all_to_all(
        send.reshape(sources, rows, LANES), axes, split_axis=0, concat_axis=0, tiled=True
    ).reshape(sources * rows, LANES)

    query_grad, gate_grad, other_part, mine_part = attention(
        query_rows, gate_logits, gated_grad, mine + other
    )
    other_part = gate(other_part, recv)
    slot_rows = jax.ShapeDtypeStruct((sources * CAP, share), BF16)
    hid_rows = jax.ShapeDtypeStruct((sources * CAP, hid), BF16)
    inputs, grads, sent = pl.pallas_call(
        functools.partial(enter_kernel, sources, rows),
        in_specs=[IN_VMEM] * 4 + [ANYWHERE],
        out_shape=[slot_rows, slot_rows, jax.ShapeDtypeStruct((sources * CAP, 3 * hid), BF16)],
        compiler_params=params(16),
        cost_estimate=cost(2e9, 2 * MIB),
        name="enter",
    )(recv, gate_proj, up_proj, down_proj, other_part)
    parts = [sent] + [
        lax.ppermute(sent, "dp", [(g, g ^ k) for g in range(groups)]) for k in range(1, groups)
    ]

    arrived = lax.ppermute(other_part, "expert", swap)
    merged = pl.pallas_call(
        functools.partial(merge_kernel, chips),
        out_shape=[jax.ShapeDtypeStruct(packed.shape, BF16)] * chips,
        compiler_params=params(16),
        cost_estimate=cost(MIB, 2 * MIB),
        name="merge",
    )(*mine_part, arrived)
    terms = [merged[0]]
    for d in range(1, chips):
        down = [(i, i - 2 * d) for i in range(2 * d, devices)]
        terms.append(lax.ppermute(merged[d], "expert", down))
    back, hidden, gate_rows, up_rows = pl.pallas_call(
        functools.partial(middle_kernel, sources, rows),
        in_specs=[IN_VMEM] * (len(parts) + 2) + [ANYWHERE],
        out_shape=[jax.ShapeDtypeStruct((sources * rows, LANES), BF16)] + [hid_rows] * 3,
        compiler_params=params(16 if groups <= 4 else 60),
        cost_estimate=cost(8, 8),
        name="middle",
    )(*parts, gate_proj, up_proj, terms[min(1, chips - 1)])
    returned = lax.all_to_all(
        back.reshape(sources, rows, LANES), axes, split_axis=0, concat_axis=0, tiled=True
    ).reshape(sources * rows, LANES)
    gate_proj_grad, up_proj_grad, down_proj_grad = pl.pallas_call(
        weight_kernel,
        out_shape=[
            jax.ShapeDtypeStruct(gate_proj.shape, F32),
            jax.ShapeDtypeStruct(up_proj.shape, F32),
            jax.ShapeDtypeStruct(down_proj.shape, F32),
        ],
        compiler_params=params(16),
        cost_estimate=cost(2e9, 2 * MIB),
        name="weight_grads",
    )(inputs, grads, hidden, gate_rows, up_rows)
    key_grad, value_grad = pl.pallas_call(
        close_kernel,
        in_specs=[IN_VMEM] * chips,
        out_shape=[jax.ShapeDtypeStruct((seqs, length, HEAD), BF16)] * 2,
        compiler_params=params(16),
        cost_estimate=cost(6e10, MIB),
        name="close",
    )(*terms)
    input_grad, route_grad = pl.pallas_call(
        functools.partial(combine_kernel, devices, groups, rows),
        in_specs=[IN_VMEM] * 3 + [ANYWHERE],
        out_shape=[
            jax.ShapeDtypeStruct(moe_input.shape, BF16),
            jax.ShapeDtypeStruct(routes_t.shape, BF16),
        ],
        compiler_params=params(16),
        cost_estimate=cost(2e9, 2 * MIB),
        name="combine",
    )(returned, routes_t, weights_t, key_grad)

    return (
        query_grad,
        key_grad,
        value_grad,
        gate_grad,
        input_grad,
        route_grad.T,
        gate_proj_grad,
        up_proj_grad,
        down_proj_grad,
    )


def solution(mesh):
    rows3 = P("dp", "expert", None)
    tokens2 = P(("dp", "expert"), None)
    weights = P("expert", "dp", None)
    weights_down = P("expert", None, "dp")
    return jax.shard_map(
        shards,
        mesh=mesh,
        in_specs=(rows3,) * 5 + (tokens2,) * 4 + (weights, weights, weights_down),
        out_specs=(rows3,) * 4 + (tokens2,) * 2 + (weights, weights, weights_down),
        check_vma=False,
    )
```

```python
import functools

import jax
import jax.numpy as jnp
from jax import lax
from jax.experimental import pallas as pl
from jax.experimental.pallas import tpu as pltpu
from jax.sharding import PartitionSpec as P

HEADS = 8
HEAD = 256
CAP = 2
LANES = 128
BF16 = jnp.bfloat16
F32 = jnp.float32
MIB = 1 << 20
ATTENTION_MIB = 32
IN_HBM = pl.BlockSpec(memory_space=pltpu.HBM)
IN_VMEM = pl.BlockSpec(memory_space=pltpu.VMEM)
ANYWHERE = pl.BlockSpec(memory_space=pl.ANY)


def dot(a, b, ca=1, cb=0):
    return lax.dot_general(a, b, (((ca,), (cb,)), ((), ())), preferred_element_type=F32)


def div(x, size):
    assert size & (size - 1) == 0
    return x >> (size.bit_length() - 1)


def mod(x, size):
    assert size & (size - 1) == 0
    return x & (size - 1)


def iota(shape, dim):
    return lax.broadcasted_iota(jnp.int32, shape, dim)


def params(mib):
    return pltpu.CompilerParams(vmem_limit_bytes=mib * MIB)


def cost(flops, bytes_accessed):
    return pl.CostEstimate(flops=int(flops), bytes_accessed=int(bytes_accessed), transcendentals=0)


def pack_kernel(key_hbm, value_hbm, out_ref, key_ref, value_ref, sems):
    copies = [
        pltpu.make_async_copy(src, dst, sems.at[i])
        for i, (src, dst) in enumerate(((key_hbm, key_ref), (value_hbm, value_ref)))
    ]
    for copy in copies:
        copy.start()
    copies[0].wait()
    out_ref[:, :, :HEAD] = key_ref[...]
    copies[1].wait()
    out_ref[:, :, HEAD:] = value_ref[...]


def attention_kernel(chips, *refs):
    q_ref, logit_ref, grad_ref = refs[:3]
    kv_refs = refs[3 : 3 + 2 * chips]
    query_grad_hbm, gate_grad_hbm, other_ref = refs[3 + 2 * chips : 6 + 2 * chips]
    mine_refs = refs[6 + 2 * chips : 6 + 3 * chips]
    query_grad_ref, gate_grad_ref, out_sems = refs[6 + 3 * chips :]
    seqs, length, _ = q_ref.shape
    side = chips * length
    scale = HEAD ** (-0.5)
    position = lax.axis_index("expert")
    chip, core = position >> 1, position & 1

    shape = (1, 2 * side)
    col = iota(shape, 1)
    half, back, inner = div(col, side), div(mod(col, side), length), mod(col, length)
    block = 2 * (chip - back) + jnp.where(half == 0, core, 1 - core)
    key_pos = jnp.where(back <= chip, block * length + inner, 2 * side)
    query_pos = position * length + mod(iota((HEADS * length, 1), 0), length)

    def stacked(ref, s):
        return jnp.concatenate(
            [ref[s, :, h * HEAD : (h + 1) * HEAD] for h in range(HEADS)], axis=0
        )

    stores = []
    for s in range(seqs):
        both = jnp.concatenate([ref[s] for ref in kv_refs], axis=0)
        keys, values = both[:, :HEAD], both[:, HEAD:]
        queries = stacked(q_ref, s)
        scores = jnp.where(key_pos <= query_pos, dot(queries, keys, 1, 1), -jnp.inf)
        row_max = jnp.max(scores, axis=1, keepdims=True)
        unnormed = jnp.exp((scores - row_max) * scale)
        probs = unnormed * (1.0 / jnp.sum(unnormed, axis=1, keepdims=True))
        probs_low = probs.astype(BF16)
        context = dot(probs_low, values)
        gate = jax.nn.sigmoid(stacked(logit_ref, s).astype(F32))
        upstream = stacked(grad_ref, s).astype(F32)
        context_grad = (upstream * gate).astype(BF16)
        gate_grad = (upstream * context * gate * (1.0 - gate)).astype(BF16)
        for h in range(HEADS):
            gate_grad_ref[s, :, h * HEAD : (h + 1) * HEAD] = gate_grad[h * length : (h + 1) * length]
        stores.append(pltpu.make_async_copy(gate_grad_ref.at[s], gate_grad_hbm.at[s], out_sems.at[s, 0]))
        stores[-1].start()
        grad_dot = jnp.sum(context_grad.astype(F32) * context, axis=1, keepdims=True)
        prob_grad = dot(context_grad, values, 1, 1)
        score_grad = (probs * (prob_grad - grad_dot)).astype(BF16)
        query_grad = (dot(score_grad, keys) * scale).astype(BF16)
        for h in range(HEADS):
            query_grad_ref[s, :, h * HEAD : (h + 1) * HEAD] = query_grad[h * length : (h + 1) * length]
        stores.append(pltpu.make_async_copy(query_grad_ref.at[s], query_grad_hbm.at[s], out_sems.at[s, 1]))
        stores[-1].start()
        key_part = (dot(score_grad, queries, 0, 0) * scale).astype(BF16)
        value_part = dot(probs_low, context_grad, 0, 0).astype(BF16)
        for d in range(chips):
            start = d * length
            mine_refs[d][s, :, :HEAD] = key_part[start : start + length]
            mine_refs[d][s, :, HEAD:] = value_part[start : start + length]
            start = side + d * length
            other_ref[d, s, :, :HEAD] = key_part[start : start + length]
            other_ref[d, s, :, HEAD:] = value_part[start : start + length]
    for store in stores:
        store.wait()


def attention(query_rows, gate_logits, gated_grad, pieces):
    seqs, length, width = query_rows.shape
    chips = len(pieces) // 2
    full = jax.ShapeDtypeStruct((seqs, length, width), BF16)
    part = jax.ShapeDtypeStruct(pieces[0].shape, BF16)
    out = pl.pallas_call(
        functools.partial(attention_kernel, chips),
        in_specs=[IN_VMEM] * (3 + 2 * chips),
        out_specs=[IN_HBM] * 2 + [IN_VMEM] * (1 + chips),
        out_shape=[full] * 2 + [jax.ShapeDtypeStruct((chips,) + part.shape, BF16)] + [part] * chips,
        scratch_shapes=[pltpu.VMEM(query_rows.shape, BF16)] * 2
        + [pltpu.SemaphoreType.DMA((seqs, 2))],
        compiler_params=params(ATTENTION_MIB if chips <= 4 else 56),
        cost_estimate=cost(MIB, 8),
        name="attention",
    )(query_rows, gate_logits, gated_grad, *pieces)
    return out[0], out[1], out[2], out[3:]


def gate_kernel(held_ref, after_ref, out_ref):
    pass


def gate(array, after):
    return pl.pallas_call(
        gate_kernel,
        in_specs=[ANYWHERE] * 2,
        out_specs=ANYWHERE,
        out_shape=jax.ShapeDtypeStruct(array.shape, array.dtype),
        input_output_aliases={0: 0},
        compiler_params=params(16),
        cost_estimate=cost(4e9, 8),
        name="gate",
    )(array, after)


def merge_kernel(chips, *refs):
    mine, arrived, outs = refs[:chips], refs[chips], refs[chips + 1 :]
    for d in range(chips):
        outs[d][...] = (mine[d][...].astype(F32) + arrived[d].astype(F32)).astype(BF16)


def close_kernel(*refs):
    parts, (key_ref, value_ref) = refs[:-3], refs[-2:]
    total = parts[0][...].astype(F32)
    for part in parts[1:]:
        total = total + part[...].astype(F32)
    key_ref[...] = total[:, :, :HEAD].astype(BF16)
    value_ref[...] = total[:, :, HEAD:].astype(BF16)


def slots(routes_ref, weights_ref, experts):
    routes = routes_ref[...]
    tokens = routes.shape[1]
    live = routes < experts
    expert = jnp.sum(jnp.where(live, routes, 0), axis=0, keepdims=True)
    has_live = jnp.sum(live.astype(jnp.int32), axis=0, keepdims=True) > 0
    weight = jnp.sum(
        jnp.where(live, weights_ref[...].astype(F32), 0.0), axis=0, keepdims=True
    )
    tall = max(experts, 16)
    member = (iota((tall, tokens), 0) == expert) & has_live
    earlier = (iota((tokens, tokens), 0) < iota((tokens, tokens), 1)).astype(BF16)
    before = dot(member.astype(BF16), earlier)
    rank = jnp.sum(jnp.where(member, before, 0.0), axis=0, keepdims=True).astype(jnp.int32)
    return jnp.where(has_live, expert * CAP + rank, -1), weight, live


def dispatch_kernel(
    experts, groups, rows, input_ref, grad_ref, routes_ref, weights_ref, after_ref, out_ref
):
    tokens, width = input_ref.shape
    slot, weight, _ = slots(routes_ref, weights_ref, experts)
    share = width // groups
    pieces = share // LANES
    total = experts * rows
    shape = (total, tokens)
    row = iota(shape, 0)
    inner = mod(row, rows)
    hit = slot == div(row, rows) * CAP + mod(div(inner, pieces), CAP)
    hit = jnp.where(hit, mod(inner, pieces) + pieces * div(inner, CAP * pieces), -1)
    acc = None
    for a, (ref, value) in enumerate(((input_ref, 1.0), (grad_ref, weight))):
        for l in range(pieces):
            pick = hit == a * pieces + l
            source = jnp.concatenate(
                [
                    ref[:, g * share + l * LANES : g * share + (l + 1) * LANES]
                    for g in range(groups)
                ],
                axis=1,
            )
            term = dot(jnp.where(pick, value, 0.0).astype(BF16), source)
            acc = term if acc is None else acc + term
    acc = acc.astype(BF16)
    for g in range(groups):
        out_ref[g * total : (g + 1) * total, :] = acc[:, g * LANES : (g + 1) * LANES]


def enter_kernel(
    sources, rows, recv_ref, gate_ref, up_ref, down_ref, after_ref, input_ref, grad_ref, send_ref
):
    pieces = input_ref.shape[1] // LANES
    block = min(sources, 32)
    shape = (block * CAP, block * rows)
    out_row, in_row = iota(shape, 0), iota(shape, 1)
    offset = in_row - div(out_row, CAP) * rows - mod(out_row, CAP) * pieces
    picks = [
        [(offset == a * CAP * pieces + l).astype(BF16) for l in range(pieces)]
        for a in range(2)
    ]
    for b in range(sources // block):
        arrived = recv_ref[b * block * rows : (b + 1) * block * rows, :]
        here = slice(b * block * CAP, (b + 1) * block * CAP)
        inputs, grads = (
            jnp.concatenate([dot(pick, arrived) for pick in picks[a]], axis=1).astype(BF16)
            for a in range(2)
        )
        input_ref[here, :] = inputs
        grad_ref[here, :] = grads
        partial = jnp.concatenate(
            [dot(inputs, gate_ref[0]), dot(inputs, up_ref[0]), dot(grads, down_ref[0], 1, 1)],
            axis=1,
        )
        send_ref[here, :] = partial.astype(BF16)


def middle_kernel(sources, rows, *refs):
    parts = refs[:-8]
    gate_ref, up_ref, _, _, back_ref, hidden_ref, gate_rows_ref, up_rows_ref = refs[-8:]
    share = gate_ref.shape[1]
    pieces = share // LANES
    hid = gate_ref.shape[2]
    block = min(sources, 32)
    shape = (block * rows, block * CAP)
    out_row, in_row = iota(shape, 0), iota(shape, 1)
    same = div(out_row, rows) == div(in_row, CAP)
    inner, which = mod(out_row, rows), mod(in_row, CAP)
    offset = jnp.where(same, inner - which * pieces, -1)
    picks = [(offset == l).astype(BF16) for l in range(pieces)]
    pick_dot = (same & (inner == CAP * pieces + which)).astype(BF16)
    for b in range(sources // block):
        here = slice(b * block * CAP, (b + 1) * block * CAP)
        terms = [part[here, :].astype(F32) for part in parts]
        total = functools.reduce(jnp.add, terms)
        gate_pre, up_pre, hidden_grad = total[:, :hid], total[:, hid : 2 * hid], total[:, 2 * hid :]
        sig = jax.nn.sigmoid(gate_pre)
        silu = gate_pre * sig
        hidden = (silu * up_pre).astype(BF16)
        slope = sig * (1.0 + gate_pre * (1.0 - sig))
        gate_rows = (hidden_grad * up_pre * slope).astype(BF16)
        up_rows = (hidden_grad * silu).astype(BF16)
        hidden_ref[here, :] = hidden
        gate_rows_ref[here, :] = gate_rows
        up_rows_ref[here, :] = up_rows
        routed = jnp.sum(hidden.astype(F32) * hidden_grad, axis=1, keepdims=True)
        high = routed.astype(BF16)
        low = (routed - high.astype(F32)).astype(BF16)
        lane = iota((block * CAP, LANES), 1)
        routed_wide = jnp.where(lane < LANES // 2, high.astype(F32), low.astype(F32)).astype(BF16)
        input_rows = (
            dot(gate_rows, gate_ref[0], 1, 1) + dot(up_rows, up_ref[0], 1, 1)
        ).astype(BF16)
        back = dot(pick_dot, routed_wide)
        for l in range(pieces):
            back = back + dot(picks[l], input_rows[:, l * LANES : (l + 1) * LANES])
        back_ref[b * block * rows : (b + 1) * block * rows, :] = back.astype(BF16)


def weight_kernel(
    input_ref, grad_ref, hidden_ref, gate_rows_ref, up_rows_ref, gate_out, up_out, down_out
):
    gate_out[0] = dot(input_ref[...], gate_rows_ref[...], 0, 0)
    up_out[0] = dot(input_ref[...], up_rows_ref[...], 0, 0)
    down_out[0] = dot(hidden_ref[...], grad_ref[...], 0, 0)


def combine_kernel(
    experts,
    groups,
    rows,
    back_ref,
    routes_ref,
    weights_ref,
    input_grad_ref,
    route_grad_ref,
):
    slot, weight, live = slots(routes_ref, weights_ref, experts)
    tokens, width = input_grad_ref.shape
    share = width // groups
    pieces = share // LANES
    total = experts * rows
    shape = (total, tokens)
    row = iota(shape, 0)
    inner = mod(row, rows)
    expert = div(row, rows)
    hit = (slot == expert * CAP + div(inner, pieces)) & (inner < CAP * pieces)
    hit = jnp.where(hit, mod(inner, pieces), -1)
    wide = jnp.concatenate([back_ref[g * total : (g + 1) * total, :] for g in range(groups)], axis=1)
    for l in range(pieces):
        pick = (hit == l).astype(BF16)
        grad = dot(pick, wide, 0, 0).astype(BF16)
        for g in range(groups):
            input_grad_ref[:, g * share + l * LANES : g * share + (l + 1) * LANES] = grad[
                :, g * LANES : (g + 1) * LANES
            ]
    hit_dot = slot == expert * CAP + inner - CAP * pieces
    hit_dot = hit_dot & (inner >= CAP * pieces) & (inner < CAP * (pieces + 1))
    routed = dot(back_ref[:total, :], hit_dot.astype(BF16), 0, 0)
    routed = routed[:1] + routed[LANES // 2 : LANES // 2 + 1]
    routed = routed / jnp.where(weight > 0.0, weight, 1.0)
    route_grad_ref[...] = jnp.where(live, routed, 0.0).astype(BF16)


def shards(
    query_rows,
    key_rows,
    value_rows,
    gate_logits,
    gated_grad,
    moe_input,
    out_grad,
    routes,
    route_weights,
    gate_proj,
    up_proj,
    down_proj,
):
    devices = lax.axis_size("expert")
    groups = lax.axis_size("dp")
    sources = devices * groups
    chips = devices // 2
    seqs, length, _ = key_rows.shape
    tokens, width = moe_input.shape
    share = width // groups
    pieces = share // LANES
    hid = gate_proj.shape[2]
    rows = -(-2 * CAP * pieces // 16) * 16
    axes = ("dp", "expert")
    swap = [(i, i ^ 1) for i in range(devices)]
    same_core = [list(range(c, devices, 2)) for c in range(2)]

    packed = pl.pallas_call(
        pack_kernel,
        in_specs=[IN_HBM] * 2,
        out_shape=jax.ShapeDtypeStruct((seqs, length, 2 * HEAD), BF16),
        scratch_shapes=[pltpu.VMEM(key_rows.shape, BF16)] * 2 + [pltpu.SemaphoreType.DMA((2,))],
        compiler_params=params(16),
        cost_estimate=cost(6e10, MIB),
        name="pack",
    )(key_rows, value_rows)
    mine = [packed]
    for d in range(1, chips):
        up = [(i, i + 2 * d) for i in range(devices - 2 * d)]
        mine.append(lax.ppermute(packed, "expert", up))
    other = [lax.ppermute(block, "expert", swap) for block in mine]

    routes_t, weights_t = routes.T, route_weights.T
    send = pl.pallas_call(
        functools.partial(dispatch_kernel, devices, groups, rows),
        in_specs=[IN_VMEM] * 4 + [ANYWHERE],
        out_shape=jax.ShapeDtypeStruct((sources * rows, LANES), BF16),
        compiler_params=params(16),
        cost_estimate=cost(2e9, 2 * MIB),
        name="dispatch",
    )(moe_input, out_grad, routes_t, weights_t, packed)
    recv = lax.all_to_all(
        send.reshape(sources, rows, LANES), axes, split_axis=0, concat_axis=0, tiled=True
    ).reshape(sources * rows, LANES)

    query_grad, gate_grad, other_part, mine_part = attention(
        query_rows, gate_logits, gated_grad, mine + other
    )
    other_part = gate(other_part, recv)
    slot_rows = jax.ShapeDtypeStruct((sources * CAP, share), BF16)
    hid_rows = jax.ShapeDtypeStruct((sources * CAP, hid), BF16)
    inputs, grads, sent = pl.pallas_call(
        functools.partial(enter_kernel, sources, rows),
        in_specs=[IN_VMEM] * 4 + [ANYWHERE],
        out_shape=[slot_rows, slot_rows, jax.ShapeDtypeStruct((sources * CAP, 3 * hid), BF16)],
        compiler_params=params(16),
        cost_estimate=cost(2e9, 2 * MIB),
        name="enter",
    )(recv, gate_proj, up_proj, down_proj, other_part)
    parts = [sent] + [
        lax.ppermute(sent, "dp", [(g, g ^ k) for g in range(groups)]) for k in range(1, groups)
    ]

    arrived = lax.ppermute(other_part, "expert", swap)
    merged = pl.pallas_call(
        functools.partial(merge_kernel, chips),
        out_shape=[jax.ShapeDtypeStruct(packed.shape, BF16)] * chips,
        compiler_params=params(16),
        cost_estimate=cost(MIB, 2 * MIB),
        name="merge",
    )(*mine_part, arrived)
    terms = [merged[0]]
    for d in range(1, chips):
        down = [(i, i - 2 * d) for i in range(2 * d, devices)]
        terms.append(lax.ppermute(merged[d], "expert", down))
    back, hidden, gate_rows, up_rows = pl.pallas_call(
        functools.partial(middle_kernel, sources, rows),
        in_specs=[IN_VMEM] * (len(parts) + 2) + [ANYWHERE] * 2,
        out_shape=[jax.ShapeDtypeStruct((sources * rows, LANES), BF16)] + [hid_rows] * 3,
        compiler_params=params(16 if groups <= 4 else 60),
        cost_estimate=cost(2e9, 2 * MIB),
        name="middle",
    )(*parts, gate_proj, up_proj, terms[min(1, chips - 1)], terms[min(3, chips - 1)])
    returned = lax.all_to_all(
        back.reshape(sources, rows, LANES), axes, split_axis=0, concat_axis=0, tiled=True
    ).reshape(sources * rows, LANES)
    gate_proj_grad, up_proj_grad, down_proj_grad = pl.pallas_call(
        weight_kernel,
        out_shape=[
            jax.ShapeDtypeStruct(gate_proj.shape, F32),
            jax.ShapeDtypeStruct(up_proj.shape, F32),
            jax.ShapeDtypeStruct(down_proj.shape, F32),
        ],
        compiler_params=params(16),
        cost_estimate=cost(2e9, 2 * MIB),
        name="weight_grads",
    )(inputs, grads, hidden, gate_rows, up_rows)
    input_grad, route_grad = pl.pallas_call(
        functools.partial(combine_kernel, devices, groups, rows),
        in_specs=[IN_VMEM] * 3,
        out_shape=[
            jax.ShapeDtypeStruct(moe_input.shape, BF16),
            jax.ShapeDtypeStruct(routes_t.shape, BF16),
        ],
        compiler_params=params(16),
        cost_estimate=cost(2e9, 2 * MIB),
        name="combine",
    )(returned, routes_t, weights_t)

    key_grad, value_grad = pl.pallas_call(
        close_kernel,
        in_specs=[IN_VMEM] * chips + [ANYWHERE],
        out_shape=[jax.ShapeDtypeStruct((seqs, length, HEAD), BF16)] * 2,
        compiler_params=params(16),
        cost_estimate=cost(MIB, MIB),
        name="close",
    )(*terms, route_grad)
    return (
        query_grad,
        key_grad,
        value_grad,
        gate_grad,
        input_grad,
        route_grad.T,
        gate_proj_grad,
        up_proj_grad,
        down_proj_grad,
    )


def solution(mesh):
    rows3 = P("dp", "expert", None)
    tokens2 = P(("dp", "expert"), None)
    weights = P("expert", "dp", None)
    weights_down = P("expert", None, "dp")
    return jax.shard_map(
        shards,
        mesh=mesh,
        in_specs=(rows3,) * 5 + (tokens2,) * 4 + (weights, weights, weights_down),
        out_specs=(rows3,) * 4 + (tokens2,) * 2 + (weights, weights, weights_down),
        check_vma=False,
    )
```

```python
import functools

import jax
import jax.numpy as jnp
from jax import lax
from jax.experimental import pallas as pl
from jax.experimental.pallas import tpu as pltpu
from jax.sharding import PartitionSpec as P

HEADS = 8
HEAD = 256
CAP = 2
LANES = 128
BF16 = jnp.bfloat16
F32 = jnp.float32
MIB = 1 << 20
ATTENTION_MIB = 32
IN_HBM = pl.BlockSpec(memory_space=pltpu.HBM)
IN_VMEM = pl.BlockSpec(memory_space=pltpu.VMEM)
ANYWHERE = pl.BlockSpec(memory_space=pl.ANY)


def dot(a, b, ca=1, cb=0):
    return lax.dot_general(a, b, (((ca,), (cb,)), ((), ())), preferred_element_type=F32)


def div(x, size):
    assert size & (size - 1) == 0
    return x >> (size.bit_length() - 1)


def mod(x, size):
    assert size & (size - 1) == 0
    return x & (size - 1)


def iota(shape, dim):
    return lax.broadcasted_iota(jnp.int32, shape, dim)


def params(mib):
    return pltpu.CompilerParams(vmem_limit_bytes=mib * MIB)


def cost(flops, bytes_accessed):
    return pl.CostEstimate(flops=int(flops), bytes_accessed=int(bytes_accessed), transcendentals=0)


def pack_kernel(key_hbm, value_hbm, out_ref, key_ref, value_ref, sems):
    copies = [
        pltpu.make_async_copy(src, dst, sems.at[i])
        for i, (src, dst) in enumerate(((key_hbm, key_ref), (value_hbm, value_ref)))
    ]
    for copy in copies:
        copy.start()
    copies[0].wait()
    out_ref[:, :, :HEAD] = key_ref[...]
    copies[1].wait()
    out_ref[:, :, HEAD:] = value_ref[...]


def attention_kernel(chips, *refs):
    q_ref, logit_ref, grad_ref = refs[:3]
    kv_refs = refs[3 : 3 + 2 * chips]
    query_grad_hbm, gate_grad_hbm, other_ref = refs[3 + 2 * chips : 6 + 2 * chips]
    mine_refs = refs[6 + 2 * chips : 6 + 3 * chips]
    query_grad_ref, gate_grad_ref, out_sems = refs[6 + 3 * chips :]
    seqs, length, _ = q_ref.shape
    side = chips * length
    scale = HEAD ** (-0.5)
    position = lax.axis_index("expert")
    chip, core = position >> 1, position & 1

    shape = (1, 2 * side)
    col = iota(shape, 1)
    half, back, inner = div(col, side), div(mod(col, side), length), mod(col, length)
    block = 2 * (chip - back) + jnp.where(half == 0, core, 1 - core)
    key_pos = jnp.where(back <= chip, block * length + inner, 2 * side)
    query_pos = position * length + mod(iota((HEADS * length, 1), 0), length)

    def stacked(ref, s):
        return jnp.concatenate(
            [ref[s, :, h * HEAD : (h + 1) * HEAD] for h in range(HEADS)], axis=0
        )

    stores = []
    for s in range(seqs):
        both = jnp.concatenate([ref[s] for ref in kv_refs], axis=0)
        keys, values = both[:, :HEAD], both[:, HEAD:]
        queries = stacked(q_ref, s)
        scores = jnp.where(key_pos <= query_pos, dot(queries, keys, 1, 1), -jnp.inf)
        row_max = jnp.max(scores, axis=1, keepdims=True)
        unnormed = jnp.exp((scores - row_max) * scale)
        probs = unnormed * (1.0 / jnp.sum(unnormed, axis=1, keepdims=True))
        probs_low = probs.astype(BF16)
        context = dot(probs_low, values)
        gate = jax.nn.sigmoid(stacked(logit_ref, s).astype(F32))
        upstream = stacked(grad_ref, s).astype(F32)
        context_grad = (upstream * gate).astype(BF16)
        gate_grad = (upstream * context * gate * (1.0 - gate)).astype(BF16)
        for h in range(HEADS):
            gate_grad_ref[s, :, h * HEAD : (h + 1) * HEAD] = gate_grad[h * length : (h + 1) * length]
        stores.append(pltpu.make_async_copy(gate_grad_ref.at[s], gate_grad_hbm.at[s], out_sems.at[s, 0]))
        stores[-1].start()
        grad_dot = jnp.sum(context_grad.astype(F32) * context, axis=1, keepdims=True)
        prob_grad = dot(context_grad, values, 1, 1)
        score_grad = (probs * (prob_grad - grad_dot)).astype(BF16)
        query_grad = (dot(score_grad, keys) * scale).astype(BF16)
        for h in range(HEADS):
            query_grad_ref[s, :, h * HEAD : (h + 1) * HEAD] = query_grad[h * length : (h + 1) * length]
        stores.append(pltpu.make_async_copy(query_grad_ref.at[s], query_grad_hbm.at[s], out_sems.at[s, 1]))
        stores[-1].start()
        key_part = (dot(score_grad, queries, 0, 0) * scale).astype(BF16)
        value_part = dot(probs_low, context_grad, 0, 0).astype(BF16)
        for d in range(chips):
            start = d * length
            mine_refs[d][s, :, :HEAD] = key_part[start : start + length]
            mine_refs[d][s, :, HEAD:] = value_part[start : start + length]
            start = side + d * length
            other_ref[d, s, :, :HEAD] = key_part[start : start + length]
            other_ref[d, s, :, HEAD:] = value_part[start : start + length]
    for store in stores:
        store.wait()


def attention(query_rows, gate_logits, gated_grad, pieces):
    seqs, length, width = query_rows.shape
    chips = len(pieces) // 2
    full = jax.ShapeDtypeStruct((seqs, length, width), BF16)
    part = jax.ShapeDtypeStruct(pieces[0].shape, BF16)
    out = pl.pallas_call(
        functools.partial(attention_kernel, chips),
        in_specs=[IN_VMEM] * (3 + 2 * chips),
        out_specs=[IN_HBM] * 2 + [IN_VMEM] * (1 + chips),
        out_shape=[full] * 2 + [jax.ShapeDtypeStruct((chips,) + part.shape, BF16)] + [part] * chips,
        scratch_shapes=[pltpu.VMEM(query_rows.shape, BF16)] * 2
        + [pltpu.SemaphoreType.DMA((seqs, 2))],
        compiler_params=params(ATTENTION_MIB if chips <= 4 else 56),
        cost_estimate=cost(MIB, 8),
        name="attention",
    )(query_rows, gate_logits, gated_grad, *pieces)
    return out[0], out[1], out[2], out[3:]


def gate_kernel(held_ref, after_ref, out_ref):
    pass


def gate(array, after):
    return pl.pallas_call(
        gate_kernel,
        in_specs=[ANYWHERE] * 2,
        out_specs=ANYWHERE,
        out_shape=jax.ShapeDtypeStruct(array.shape, array.dtype),
        input_output_aliases={0: 0},
        compiler_params=params(16),
        cost_estimate=cost(4e9, 8),
        name="gate",
    )(array, after)


def merge_kernel(chips, *refs):
    mine, arrived, outs = refs[:chips], refs[chips], refs[chips + 1 :]
    for d in range(chips):
        outs[d][...] = (mine[d][...].astype(F32) + arrived[d].astype(F32)).astype(BF16)


def close_kernel(*refs):
    parts, (key_ref, value_ref) = refs[:-2], refs[-2:]
    total = parts[0][...].astype(F32)
    for part in parts[1:]:
        total = total + part[...].astype(F32)
    key_ref[...] = total[:, :, :HEAD].astype(BF16)
    value_ref[...] = total[:, :, HEAD:].astype(BF16)


def slots(routes_ref, weights_ref, experts):
    routes = routes_ref[...]
    tokens = routes.shape[1]
    live = routes < experts
    expert = jnp.sum(jnp.where(live, routes, 0), axis=0, keepdims=True)
    has_live = jnp.sum(live.astype(jnp.int32), axis=0, keepdims=True) > 0
    weight = jnp.sum(
        jnp.where(live, weights_ref[...].astype(F32), 0.0), axis=0, keepdims=True
    )
    tall = max(experts, 16)
    member = (iota((tall, tokens), 0) == expert) & has_live
    earlier = (iota((tokens, tokens), 0) < iota((tokens, tokens), 1)).astype(BF16)
    before = dot(member.astype(BF16), earlier)
    rank = jnp.sum(jnp.where(member, before, 0.0), axis=0, keepdims=True).astype(jnp.int32)
    return jnp.where(has_live, expert * CAP + rank, -1), weight, live


def dispatch_kernel(
    experts, groups, rows, input_ref, grad_ref, routes_ref, weights_ref, after_ref, out_ref
):
    tokens, width = input_ref.shape
    slot, weight, _ = slots(routes_ref, weights_ref, experts)
    share = width // groups
    pieces = share // LANES
    total = experts * rows
    shape = (total, tokens)
    row = iota(shape, 0)
    inner = mod(row, rows)
    hit = slot == div(row, rows) * CAP + mod(div(inner, pieces), CAP)
    hit = jnp.where(hit, mod(inner, pieces) + pieces * div(inner, CAP * pieces), -1)
    acc = None
    for a, (ref, value) in enumerate(((input_ref, 1.0), (grad_ref, weight))):
        for l in range(pieces):
            pick = hit == a * pieces + l
            source = jnp.concatenate(
                [
                    ref[:, g * share + l * LANES : g * share + (l + 1) * LANES]
                    for g in range(groups)
                ],
                axis=1,
            )
            term = dot(jnp.where(pick, value, 0.0).astype(BF16), source)
            acc = term if acc is None else acc + term
    acc = acc.astype(BF16)
    for g in range(groups):
        out_ref[g * total : (g + 1) * total, :] = acc[:, g * LANES : (g + 1) * LANES]


def enter_kernel(
    sources, rows, recv_ref, gate_ref, up_ref, down_ref, after_ref, input_ref, grad_ref, send_ref
):
    pieces = input_ref.shape[1] // LANES
    block = min(sources, 32)
    shape = (block * CAP, block * rows)
    out_row, in_row = iota(shape, 0), iota(shape, 1)
    offset = in_row - div(out_row, CAP) * rows - mod(out_row, CAP) * pieces
    picks = [
        [(offset == a * CAP * pieces + l).astype(BF16) for l in range(pieces)]
        for a in range(2)
    ]
    for b in range(sources // block):
        arrived = recv_ref[b * block * rows : (b + 1) * block * rows, :]
        here = slice(b * block * CAP, (b + 1) * block * CAP)
        inputs, grads = (
            jnp.concatenate([dot(pick, arrived) for pick in picks[a]], axis=1).astype(BF16)
            for a in range(2)
        )
        input_ref[here, :] = inputs
        grad_ref[here, :] = grads
        partial = jnp.concatenate(
            [dot(inputs, gate_ref[0]), dot(inputs, up_ref[0]), dot(grads, down_ref[0], 1, 1)],
            axis=1,
        )
        send_ref[here, :] = partial.astype(BF16)


def middle_kernel(sources, rows, *refs):
    parts = refs[:-7]
    gate_ref, up_ref, _, back_ref, hidden_ref, gate_rows_ref, up_rows_ref = refs[-7:]
    share = gate_ref.shape[1]
    pieces = share // LANES
    hid = gate_ref.shape[2]
    block = min(sources, 32)
    shape = (block * rows, block * CAP)
    out_row, in_row = iota(shape, 0), iota(shape, 1)
    same = div(out_row, rows) == div(in_row, CAP)
    inner, which = mod(out_row, rows), mod(in_row, CAP)
    offset = jnp.where(same, inner - which * pieces, -1)
    picks = [(offset == l).astype(BF16) for l in range(pieces)]
    pick_dot = (same & (inner == CAP * pieces + which)).astype(BF16)
    for b in range(sources // block):
        here = slice(b * block * CAP, (b + 1) * block * CAP)
        terms = [part[here, :].astype(F32) for part in parts]
        total = functools.reduce(jnp.add, terms)
        gate_pre, up_pre, hidden_grad = total[:, :hid], total[:, hid : 2 * hid], total[:, 2 * hid :]
        sig = jax.nn.sigmoid(gate_pre)
        silu = gate_pre * sig
        hidden = (silu * up_pre).astype(BF16)
        slope = sig * (1.0 + gate_pre * (1.0 - sig))
        gate_rows = (hidden_grad * up_pre * slope).astype(BF16)
        up_rows = (hidden_grad * silu).astype(BF16)
        hidden_ref[here, :] = hidden
        gate_rows_ref[here, :] = gate_rows
        up_rows_ref[here, :] = up_rows
        routed = jnp.sum(hidden.astype(F32) * hidden_grad, axis=1, keepdims=True)
        high = routed.astype(BF16)
        low = (routed - high.astype(F32)).astype(BF16)
        lane = iota((block * CAP, LANES), 1)
        routed_wide = jnp.where(lane < LANES // 2, high.astype(F32), low.astype(F32)).astype(BF16)
        input_rows = (
            dot(gate_rows, gate_ref[0], 1, 1) + dot(up_rows, up_ref[0], 1, 1)
        ).astype(BF16)
        back = dot(pick_dot, routed_wide)
        for l in range(pieces):
            back = back + dot(picks[l], input_rows[:, l * LANES : (l + 1) * LANES])
        back_ref[b * block * rows : (b + 1) * block * rows, :] = back.astype(BF16)


def weight_kernel(
    input_ref, grad_ref, hidden_ref, gate_rows_ref, up_rows_ref, gate_out, up_out, down_out
):
    gate_out[0] = dot(input_ref[...], gate_rows_ref[...], 0, 0)
    up_out[0] = dot(input_ref[...], up_rows_ref[...], 0, 0)
    down_out[0] = dot(hidden_ref[...], grad_ref[...], 0, 0)


def combine_kernel(
    experts,
    groups,
    rows,
    back_ref,
    routes_ref,
    weights_ref,
    after_ref,
    input_grad_ref,
    route_grad_ref,
):
    slot, weight, live = slots(routes_ref, weights_ref, experts)
    tokens, width = input_grad_ref.shape
    share = width // groups
    pieces = share // LANES
    total = experts * rows
    shape = (total, tokens)
    row = iota(shape, 0)
    inner = mod(row, rows)
    expert = div(row, rows)
    hit = (slot == expert * CAP + div(inner, pieces)) & (inner < CAP * pieces)
    hit = jnp.where(hit, mod(inner, pieces), -1)
    wide = jnp.concatenate([back_ref[g * total : (g + 1) * total, :] for g in range(groups)], axis=1)
    for l in range(pieces):
        pick = (hit == l).astype(BF16)
        grad = dot(pick, wide, 0, 0).astype(BF16)
        for g in range(groups):
            input_grad_ref[:, g * share + l * LANES : g * share + (l + 1) * LANES] = grad[
                :, g * LANES : (g + 1) * LANES
            ]
    hit_dot = slot == expert * CAP + inner - CAP * pieces
    hit_dot = hit_dot & (inner >= CAP * pieces) & (inner < CAP * (pieces + 1))
    routed = dot(back_ref[:total, :], hit_dot.astype(BF16), 0, 0)
    routed = routed[:1] + routed[LANES // 2 : LANES // 2 + 1]
    routed = routed / jnp.where(weight > 0.0, weight, 1.0)
    route_grad_ref[...] = jnp.where(live, routed, 0.0).astype(BF16)


def shards(
    query_rows,
    key_rows,
    value_rows,
    gate_logits,
    gated_grad,
    moe_input,
    out_grad,
    routes,
    route_weights,
    gate_proj,
    up_proj,
    down_proj,
):
    devices = lax.axis_size("expert")
    groups = lax.axis_size("dp")
    sources = devices * groups
    chips = devices // 2
    seqs, length, _ = key_rows.shape
    tokens, width = moe_input.shape
    share = width // groups
    pieces = share // LANES
    hid = gate_proj.shape[2]
    rows = -(-2 * CAP * pieces // 16) * 16
    axes = ("dp", "expert")
    swap = [(i, i ^ 1) for i in range(devices)]
    same_core = [list(range(c, devices, 2)) for c in range(2)]

    packed = pl.pallas_call(
        pack_kernel,
        in_specs=[IN_HBM] * 2,
        out_shape=jax.ShapeDtypeStruct((seqs, length, 2 * HEAD), BF16),
        scratch_shapes=[pltpu.VMEM(key_rows.shape, BF16)] * 2 + [pltpu.SemaphoreType.DMA((2,))],
        compiler_params=params(16),
        cost_estimate=cost(6e10, MIB),
        name="pack",
    )(key_rows, value_rows)
    mine = [packed]
    for d in range(1, chips):
        up = [(i, i + 2 * d) for i in range(devices - 2 * d)]
        mine.append(lax.ppermute(packed, "expert", up))
    other = [lax.ppermute(block, "expert", swap) for block in mine]

    routes_t, weights_t = routes.T, route_weights.T
    send = pl.pallas_call(
        functools.partial(dispatch_kernel, devices, groups, rows),
        in_specs=[IN_VMEM] * 4 + [ANYWHERE],
        out_shape=jax.ShapeDtypeStruct((sources * rows, LANES), BF16),
        compiler_params=params(16),
        cost_estimate=cost(2e9, 2 * MIB),
        name="dispatch",
    )(moe_input, out_grad, routes_t, weights_t, packed)
    recv = lax.all_to_all(
        send.reshape(sources, rows, LANES), axes, split_axis=0, concat_axis=0, tiled=True
    ).reshape(sources * rows, LANES)

    query_grad, gate_grad, other_part, mine_part = attention(
        query_rows, gate_logits, gated_grad, mine + other
    )
    other_part = gate(other_part, recv)
    slot_rows = jax.ShapeDtypeStruct((sources * CAP, share), BF16)
    hid_rows = jax.ShapeDtypeStruct((sources * CAP, hid), BF16)
    inputs, grads, sent = pl.pallas_call(
        functools.partial(enter_kernel, sources, rows),
        in_specs=[IN_VMEM] * 4 + [ANYWHERE],
        out_shape=[slot_rows, slot_rows, jax.ShapeDtypeStruct((sources * CAP, 3 * hid), BF16)],
        compiler_params=params(16),
        cost_estimate=cost(2e9, 2 * MIB),
        name="enter",
    )(recv, gate_proj, up_proj, down_proj, other_part)
    parts = [sent] + [
        lax.ppermute(sent, "dp", [(g, g ^ k) for g in range(groups)]) for k in range(1, groups)
    ]

    arrived = lax.ppermute(other_part, "expert", swap)
    merged = pl.pallas_call(
        functools.partial(merge_kernel, chips),
        out_shape=[jax.ShapeDtypeStruct(packed.shape, BF16)] * chips,
        compiler_params=params(16),
        cost_estimate=cost(MIB, 2 * MIB),
        name="merge",
    )(*mine_part, arrived)
    terms = [merged[0]]
    for d in range(1, chips):
        down = [(i, i - 2 * d) for i in range(2 * d, devices)]
        terms.append(lax.ppermute(merged[d], "expert", down))
    back, hidden, gate_rows, up_rows = pl.pallas_call(
        functools.partial(middle_kernel, sources, rows),
        in_specs=[IN_VMEM] * (len(parts) + 2) + [ANYWHERE],
        out_shape=[jax.ShapeDtypeStruct((sources * rows, LANES), BF16)] + [hid_rows] * 3,
        compiler_params=params(16 if groups <= 4 else 60),
        cost_estimate=cost(8e8, MIB),
        name="middle",
    )(*parts, gate_proj, up_proj, terms[min(1, chips - 1)])
    returned = lax.all_to_all(
        back.reshape(sources, rows, LANES), axes, split_axis=0, concat_axis=0, tiled=True
    ).reshape(sources * rows, LANES)
    gate_proj_grad, up_proj_grad, down_proj_grad = pl.pallas_call(
        weight_kernel,
        out_shape=[
            jax.ShapeDtypeStruct(gate_proj.shape, F32),
            jax.ShapeDtypeStruct(up_proj.shape, F32),
            jax.ShapeDtypeStruct(down_proj.shape, F32),
        ],
        compiler_params=params(16),
        cost_estimate=cost(2e9, 2 * MIB),
        name="weight_grads",
    )(inputs, grads, hidden, gate_rows, up_rows)
    key_grad, value_grad = pl.pallas_call(
        close_kernel,
        in_specs=[IN_VMEM] * chips,
        out_shape=[jax.ShapeDtypeStruct((seqs, length, HEAD), BF16)] * 2,
        compiler_params=params(16),
        cost_estimate=cost(6e10, MIB),
        name="close",
    )(*terms)
    input_grad, route_grad = pl.pallas_call(
        functools.partial(combine_kernel, devices, groups, rows),
        in_specs=[IN_VMEM] * 3 + [ANYWHERE],
        out_shape=[
            jax.ShapeDtypeStruct(moe_input.shape, BF16),
            jax.ShapeDtypeStruct(routes_t.shape, BF16),
        ],
        compiler_params=params(16),
        cost_estimate=cost(2e9, 2 * MIB),
        name="combine",
    )(returned, routes_t, weights_t, key_grad)

    return (
        query_grad,
        key_grad,
        value_grad,
        gate_grad,
        input_grad,
        route_grad.T,
        gate_proj_grad,
        up_proj_grad,
        down_proj_grad,
    )


def solution(mesh):
    rows3 = P("dp", "expert", None)
    tokens2 = P(("dp", "expert"), None)
    weights = P("expert", "dp", None)
    weights_down = P("expert", None, "dp")
    return jax.shard_map(
        shards,
        mesh=mesh,
        in_specs=(rows3,) * 5 + (tokens2,) * 4 + (weights, weights, weights_down),
        out_specs=(rows3,) * 4 + (tokens2,) * 2 + (weights, weights, weights_down),
        check_vma=False,
    )
```
